256 devices in a mesh: depth: 32 (over y, z), dp: 8 (over x, core).
Axes of the slice: x: 4, y: 4, z: 8, core: 2. Of those that a mesh axis runs over, the one named last changes fastest.
Arguments:
- checkpoints: bfloat16 [32, 8, 8, 32, 128], P('depth', 'dp'), may hold values from -6 to 6
- conv_weight: bfloat16 [3, 3, 128, 128], replicated, may hold values from -0.1875 to 0.1875
- conv_bias: float32 [128], replicated, may hold values from -3 to 3
- point_guess: float32 [32, 8, 8, 32, 128], P('depth', 'dp'), may hold values from -6 to 6
- terminal: float32 [8, 8, 32, 128], P('dp'), may hold values from -6 to 6
Outputs:
- points: float32 [32, 8, 8, 32, 128], P('depth', 'dp')
- grad_w: float32 [3, 3, 128, 128], replicated
The draws below stay inside these ranges and needn't reach their ends.
All inputs are finite; a program needn't handle non-finite values.
Results may differ from the reference program's by a relative error of at most 0.0022.
Values sent between devices are 32-bit elements; how exact they have to be, the bound alone decides.
No kernel may reach another device: no remote copies, remote signals or barrier semaphores. Data moves between devices by JAX's collectives and lax.ppermute only.
A program may use at most 64 MiB of HBM per device.

```python
import jax
import jax.numpy as jnp
from jax import lax

C = 128
HH = 8
WW = 32
STEPS_DEV = 4
SLICES = 32
STEPS = 128
BATCH = 8


def block_levels(key, extent, cuts, smallest, top_value):
    def one(axis_at, shards_of):
        draws = jax.random.uniform(jax.random.fold_in(jax.random.fold_in(key, 6), axis_at), (shards_of,), jnp.float32, smallest / len(cuts), top_value / len(cuts))
        return jnp.repeat(jnp.exp(draws), extent[axis_at] // shards_of).reshape((-1,) + (1,) * (len(extent) - axis_at - 1))

    gain = one(*cuts[0])
    for cut in cuts[1:]:
        gain = gain * one(*cut)
    return gain


def noise(key, shape, spread, bound, pieces=(), kind=jnp.bfloat16):
    drawn = jax.random.normal(key, shape, jnp.float32) * spread
    if len(pieces) > 0:
        drawn = block_levels(key, shape, pieces, -0.22, 0.18) * drawn
    return jnp.clip(drawn, min=-bound, max=bound).astype(kind)


def setup_inputs(seed: int = 0) -> dict:
    key_list = jax.random.split(jax.random.key(seed), 6)
    return {
        "checkpoints": noise(key_list[0], (SLICES, BATCH, HH, WW, C), 1.0, 6.0, ((0, 32), (1, 8))),
        "conv_weight": noise(key_list[1], (3, 3, C, C), (9 * C) ** -0.5, 0.1875),
        "conv_bias": noise(key_list[2], (C,), 0.5, 3.0, (), jnp.float32),
        "point_guess": noise(key_list[3], (SLICES, BATCH, HH, WW, C), 1.0, 6.0, ((0, 32), (1, 8)), jnp.float32),
        "terminal": noise(key_list[4], (BATCH, HH, WW, C), 1.0, 6.0, ((0, 8),), jnp.float32),
    }


def conv_apply(field, kernel):
    return lax.conv_general_dilated(field, kernel, (1, 1), "SAME", dimension_numbers=("NHWC", "HWIO", "NHWC"), preferred_element_type=jnp.float32)


def forward_states(start, kernel, conv_bias, step_size, steps_here):
    current = start
    lowered = []
    slopes = []
    for section in range(steps_here):
        low_state = current.astype(jnp.bfloat16)
        tanh_out = jnp.tanh(conv_apply(low_state, kernel) + conv_bias)
        lowered.append(low_state)
        slopes.append(1.0 - tanh_out * tanh_out)
        current = current + step_size * tanh_out
    return lowered, slopes


def correlate(low_state, low_grad):
    rows_map = low_state.shape[1]
    cols_map = low_state.shape[2]
    channels = low_state.shape[3]
    padded = jnp.pad(low_state, ((0, 0), (1, 1), (1, 1), (0, 0)))
    flat_grad = low_grad.reshape(-1, channels)
    taps = []
    for row_tap in range(3):
        for col_tap in range(3):
            patch = padded[:, row_tap:row_tap + rows_map, col_tap:col_tap + cols_map, :].reshape(-1, channels)
            taps.append(lax.dot_general(patch, flat_grad, (((0,), (0,)), ((), ())), preferred_element_type=jnp.float32))
    return jnp.stack(taps).reshape(3, 3, channels, channels)


def coarse_operator(first_slope, center, coarse_step):
    channels = center.shape[0]
    slope_mean = jnp.mean(first_slope, axis=(1, 2))
    identity = jnp.eye(channels, dtype=jnp.float32)
    return identity[None] + coarse_step * slope_mean[:, :, None] * center.T[None]


def apply_map(field, coarse_map):
    return jnp.einsum("bhwc,bcd->bhwd", field, coarse_map, precision=lax.Precision.HIGHEST)


def reference(checkpoints, conv_weight, conv_bias, point_guess, terminal):
    step_size = 2.0 / STEPS
    coarse_step = STEPS_DEV * step_size
    flipped = conv_weight[::-1, ::-1].transpose(0, 1, 3, 2)
    center = conv_weight[1, 1].astype(jnp.float32)
    maps = []
    residues = []
    for slab in range(SLICES):
        upper = terminal if slab == SLICES - 1 else point_guess[slab + 1]
        lowered, slopes = forward_states(checkpoints[slab].astype(jnp.float32), conv_weight, conv_bias, step_size, STEPS_DEV)
        adjoint = upper
        for section in range(STEPS_DEV - 1, -1, -1):
            low_grad = (slopes[section] * adjoint).astype(jnp.bfloat16)
            adjoint = adjoint + step_size * conv_apply(low_grad, flipped)
        residues.append(adjoint - point_guess[slab])
        maps.append(coarse_operator(slopes[0], center, coarse_step))
    errors = [None] * SLICES
    carry = jnp.zeros(terminal.shape, jnp.float32)
    for slab in range(SLICES - 1, -1, -1):
        carry = residues[slab] + apply_map(carry, maps[slab])
        errors[slab] = carry
    points = point_guess + jnp.stack(errors)
    channels = conv_weight.shape[3]
    grad_w = jnp.zeros((3, 3, channels, channels), jnp.float32)
    for slab in range(SLICES):
        upper = terminal if slab == SLICES - 1 else points[slab + 1]
        lowered, slopes = forward_states(checkpoints[slab].astype(jnp.float32), conv_weight, conv_bias, step_size, STEPS_DEV)
        adjoint = upper
        for section in range(STEPS_DEV - 1, -1, -1):
            low_grad = (slopes[section] * adjoint).astype(jnp.bfloat16)
            grad_w = grad_w + step_size * correlate(lowered[section], low_grad)
            if section > 0:
                adjoint = adjoint + step_size * conv_apply(low_grad, flipped)
    return points, grad_w
```

```python
import jax
import jax.numpy as jnp
from jax import lax
from jax.experimental import pallas as pl
from jax.experimental.pallas import tpu as pltpu
from jax.sharding import Mesh, PartitionSpec as P

STEPS_DEV = 4
ROWS = 8
COLS = 32
CH = 128
PIX = ROWS * COLS
PADDED = PIX + 2 * COLS
WIDE = 3 * CH
TAPS = 9 * CH
SIZE_Y = 4
SIZE_Z = 8
SIZE_X = 4
CHUNK = 40
HALF = SIZE_X * SIZE_Y * CHUNK
SLOT = COLS + 8


def call(kernel, outs, scratch=()):
    return pl.pallas_call(
        kernel,
        out_shape=outs,
        scratch_shapes=scratch,
        compiler_params=pltpu.CompilerParams(vmem_limit_bytes=40 << 20),
    )


def f32(*shape):
    return jax.ShapeDtypeStruct(shape, jnp.float32)


def bf16(*shape):
    return jax.ShapeDtypeStruct(shape, jnp.bfloat16)


def columns():
    return lax.broadcasted_iota(jnp.int32, (PIX, CH), 0) % COLS


def clear_edges(buffer):
    zeros = jnp.zeros((COLS, WIDE), jnp.bfloat16)
    buffer[0:COLS, :] = zeros
    buffer[COLS + PIX : PADDED, :] = zeros


def spread(buffer, low, col):
    wide = low.astype(jnp.float32)
    before = jnp.where(col > 0, pltpu.roll(wide, 1, 0), 0.0)
    after = jnp.where(col < COLS - 1, pltpu.roll(wide, PIX - 1, 0), 0.0)
    buffer[COLS : COLS + PIX, 0:CH] = before.astype(jnp.bfloat16)
    buffer[COLS : COLS + PIX, CH : 2 * CH] = low
    buffer[COLS : COLS + PIX, 2 * CH : WIDE] = after.astype(jnp.bfloat16)


def convolve(buffer, kernel):
    total = None
    for row in range(3):
        part = jnp.dot(
            buffer[row * COLS : row * COLS + PIX, :],
            kernel[row * WIDE : (row + 1) * WIDE, :],
            preferred_element_type=jnp.float32,
        )
        total = part if total is None else total + part
    return total


def split(value):
    high = value.astype(jnp.bfloat16)
    return high, (value - high.astype(jnp.float32)).astype(jnp.bfloat16)


def exact_left(value, weight_twice):
    return jnp.dot(
        jnp.concatenate(split(value), axis=1), weight_twice, preferred_element_type=jnp.float32
    )


def full_dot(left, right):
    return jnp.dot(
        left, right, preferred_element_type=jnp.float32, precision=lax.Precision.HIGHEST
    )


def forward_kernel(step, start_ref, kernel_ref, bias_ref, slope_ref, lowered_ref, flipped_ref, center_ref, mean_ref):
    col = columns()
    bias = bias_ref[...]
    current = start_ref[...].astype(jnp.float32)
    for section in range(STEPS_DEV):
        buffer = lowered_ref.at[section]
        clear_edges(buffer)
        spread(buffer, current.astype(jnp.bfloat16), col)
        tanh_out = jnp.tanh(convolve(buffer, kernel_ref) + bias)
        slope = 1.0 - tanh_out * tanh_out
        slope_ref[section] = slope
        if section == 0:
            mean = jnp.sum(slope, axis=0, keepdims=True) * (STEPS_DEV * step / PIX)
            mean_ref[...] = jnp.broadcast_to(mean, (8, CH))
        current = current + step * tanh_out
    for tap in range(9):
        block = kernel_ref[(8 - tap) * CH : (9 - tap) * CH, :].astype(jnp.float32)
        turned = block.T.astype(jnp.bfloat16)
        flipped_ref[tap * CH : (tap + 1) * CH, :] = turned
        if tap == 4:
            center_ref[0:CH, :] = turned
            center_ref[CH : 2 * CH, :] = turned


def adjoint_step(buffer, flipped, slope, value, step, col):
    low = (slope * value).astype(jnp.bfloat16)
    spread(buffer, low, col)
    return low, value + step * convolve(buffer, flipped)


def relax_kernel(step, final_ref, upper_ref, terminal_ref, own_ref, slope_ref, flipped_ref, mean_ref, packed_ref, buffer):
    col = columns()
    clear_edges(buffer)
    value = jnp.where(final_ref[0] == 1, terminal_ref[...], upper_ref[...])
    for section in range(STEPS_DEV - 1, -1, -1):
        low, value = adjoint_step(buffer, flipped_ref, slope_ref[section], value, step, col)
    residue = value - own_ref[...]
    for part in range(ROWS):
        packed_ref[part, 0:COLS, :] = residue[part * COLS : (part + 1) * COLS]
        packed_ref[part, COLS:SLOT, :] = mean_ref[...]


def group_kernel(packed_ref, center_ref, local_ref, maps_ref, total_ref):
    center = center_ref[...]
    row = lax.broadcasted_iota(jnp.int32, (CH, CH), 0)
    lane = lax.broadcasted_iota(jnp.int32, (CH, CH), 1)
    identity = jnp.where(row == lane, 1.0, 0.0)
    error = jnp.zeros((COLS, CH), jnp.float32)
    change = jnp.zeros((CH, CH), jnp.float32)
    for place in range(SIZE_Z - 1, -1, -1):
        local_ref[place] = error
        maps_ref[place] = change
        mean = packed_ref[place, COLS : COLS + 1, :]
        both = jnp.concatenate([error, change + identity], axis=0) * mean
        moved = exact_left(both, center)
        error = packed_ref[place, 0:COLS, :] + error + moved[0:COLS]
        change = change + moved[COLS:]
    total_ref[0:COLS, :] = error
    total_ref[COLS:, :] = change


def carry_kernel(first_ref, second_ref, third_ref, local_ref, maps_ref, upper_ref):
    third = third_ref[...]
    carry = second_ref[0:COLS, :] + third + full_dot(third, second_ref[COLS:, :])
    carry = first_ref[0:COLS, :] + carry + full_dot(carry, first_ref[COLS:, :])
    for place in range(SIZE_Z):
        upper_ref[place] = local_ref[place] + carry + full_dot(carry, maps_ref[place])


def second_kernel(
    step, final_ref, core_ref, upper_ref, terminal_ref, own_ref, packed_ref, error_ref, slope_ref, lowered_ref,
    flipped_ref, center_ref, mean_ref, points_ref, kept_ref, sent_ref, buffer, total,
):
    col = columns()
    clear_edges(buffer)
    error = error_ref[...]
    moved = exact_left(error * mean_ref[0:1, :], center_ref[...])
    for part in range(ROWS):
        span = slice(part * COLS, (part + 1) * COLS)
        points_ref[span, :] = own_ref[span, :] + (packed_ref[part, 0:COLS, :] + error[span] + moved[span])
    value = jnp.where(final_ref[0] == 1, terminal_ref[...], upper_ref[...] + error)
    for section in range(STEPS_DEV - 1, -1, -1):
        if section > 0:
            low, value = adjoint_step(buffer, flipped_ref, slope_ref[section], value, step, col)
        else:
            low = (slope_ref[section] * value).astype(jnp.bfloat16)
        for row in range(3):
            term = lax.dot_general(
                lowered_ref[section, row * COLS : row * COLS + PIX, :],
                low,
                (((0,), (0,)), ((), ())),
                preferred_element_type=jnp.float32,
            )
            span = slice(row * WIDE, (row + 1) * WIDE)
            if section == STEPS_DEV - 1:
                total[span, :] = step * term
            else:
                total[span, :] += step * term
    total[TAPS : 2 * HALF, :] = jnp.zeros((2 * HALF - TAPS, CH), jnp.float32)
    core = core_ref[0]
    kept_ref[...] = total[pl.ds(pl.multiple_of(core * HALF, 8), HALF), :]
    sent_ref[...] = total[pl.ds(pl.multiple_of((1 - core) * HALF, 8), HALF), :]


def add_kernel(left_ref, right_ref, out_ref):
    out_ref[...] = left_ref[...] + right_ref[...]


def sum_kernel(parts_ref, out_ref):
    total = parts_ref[0]
    for part in range(1, parts_ref.shape[0]):
        total = total + parts_ref[part]
    for copy in range(out_ref.shape[0]):
        out_ref[copy] = total


def passed_down(value, axes, count, distance):
    return lax.ppermute(value, axes, [(i + distance, i) for i in range(count - distance)])


def local(checkpoints, conv_weight, conv_bias, point_guess, terminal):
    slices = SIZE_Y * SIZE_Z
    step = 2.0 / (STEPS_DEV * slices)
    own = point_guess.reshape(PIX, CH)
    terminal = terminal.reshape(PIX, CH)
    kernel = conv_weight.reshape(TAPS, CH)
    final = (lax.axis_index(("y", "z")) == slices - 1).astype(jnp.int32).reshape(1)
    core = lax.axis_index("core").astype(jnp.int32).reshape(1)
    upper = passed_down(own, ("y", "z"), slices, 1)

    def bound(function):
        def kernel_of(*refs):
            function(step, *refs)

        return kernel_of

    slopes, lowered, flipped, center, mean = call(
        bound(forward_kernel),
        [f32(STEPS_DEV, PIX, CH), bf16(STEPS_DEV, PADDED, WIDE), bf16(TAPS, CH), bf16(2 * CH, CH), f32(8, CH)],
    )(checkpoints.reshape(PIX, CH), kernel, conv_bias.reshape(1, CH))

    smem = pl.BlockSpec(memory_space=pltpu.SMEM)
    vmem = pl.BlockSpec(memory_space=pltpu.VMEM)
    packed = pl.pallas_call(
        bound(relax_kernel),
        out_shape=f32(ROWS, SLOT, CH),
        in_specs=[smem] + [vmem] * 6,
        out_specs=vmem,
        scratch_shapes=[pltpu.VMEM((PADDED, WIDE), jnp.bfloat16)],
        compiler_params=pltpu.CompilerParams(vmem_limit_bytes=40 << 20),
    )(final, upper, terminal, own, slopes, flipped, mean)

    gathered = lax.all_to_all(packed, "z", 0, 0)
    in_group, maps, total = call(
        group_kernel, [f32(SIZE_Z, COLS, CH), f32(SIZE_Z, CH, CH), f32(COLS + CH, CH)]
    )(gathered, center)
    first = passed_down(total, "y", SIZE_Y, 1)
    second = passed_down(total, "y", SIZE_Y, 2)
    third = passed_down(total[0:COLS], "y", SIZE_Y, 3)
    upper_error = call(carry_kernel, f32(SIZE_Z, COLS, CH))(first, second, third, in_group, maps)
    upper_error = lax.all_to_all(upper_error, "z", 0, 0).reshape(PIX, CH)

    points, kept, sent = pl.pallas_call(
        bound(second_kernel),
        out_shape=[f32(PIX, CH), f32(HALF, CH), f32(HALF, CH)],
        in_specs=[smem] * 2 + [vmem] * 10,
        out_specs=[vmem] * 3,
        scratch_shapes=[pltpu.VMEM((PADDED, WIDE), jnp.bfloat16), pltpu.VMEM((2 * HALF, CH), jnp.float32)],
        compiler_params=pltpu.CompilerParams(vmem_limit_bytes=40 << 20),
    )(final, core, upper, terminal, own, packed, upper_error, slopes, lowered, flipped, center, mean)

    plane = SIZE_X * SIZE_Y
    received = lax.ppermute(sent, "core", [(0, 1), (1, 0)])
    half = call(add_kernel, f32(HALF, CH))(kept, received)
    parts = lax.all_to_all(half.reshape(plane, CHUNK, CH), ("y", "x"), 0, 0)
    copies = call(sum_kernel, f32(SIZE_Z, CHUNK, CH))(parts)
    parts = lax.all_to_all(copies, "z", 0, 0)
    copies = call(sum_kernel, f32(plane, CHUNK, CH))(parts)
    half = lax.all_to_all(copies, ("y", "x"), 0, 0).reshape(HALF, CH)
    grad_w = lax.all_gather(half, "core").reshape(2 * HALF, CH)[0:TAPS]
    return points.reshape(1, 1, ROWS, COLS, CH), grad_w.reshape(3, 3, CH, CH)


def solution(mesh):
    fine = Mesh(mesh.devices.reshape(SIZE_Y, SIZE_Z, SIZE_X, 2), ("y", "z", "x", "core"))
    state = P(("y", "z"), ("x", "core"), None, None, None)
    return jax.shard_map(
        local,
        mesh=fine,
        in_specs=(state, P(), P(), state, P(("x", "core"), None, None, None)),
        out_specs=(state, P()),
        check_vma=False,
    )
```

```python
import jax
import jax.numpy as jnp
from jax import lax
from jax.experimental import pallas as pl
from jax.experimental.pallas import tpu as pltpu
from jax.sharding import Mesh, PartitionSpec as P

STEPS_DEV = 4
ROWS = 8
COLS = 32
CH = 128
PIX = ROWS * COLS
PADDED = PIX + 2 * COLS
WIDE = 3 * CH
TAPS = 9 * CH
SIZE_Y = 4
SIZE_Z = 8
SIZE_X = 4
PLANE = SIZE_X * SIZE_Y
PART = 36
CHUNK = 40
HALF = PLANE * PART
SLOT = COLS + 8
LIMIT = 12 << 20


def call(kernel, outs, scratch=()):
    return pl.pallas_call(
        kernel,
        out_shape=outs,
        scratch_shapes=scratch,
        compiler_params=pltpu.CompilerParams(vmem_limit_bytes=LIMIT),
    )


def f32(*shape):
    return jax.ShapeDtypeStruct(shape, jnp.float32)


def bf16(*shape):
    return jax.ShapeDtypeStruct(shape, jnp.bfloat16)


def columns():
    return lax.broadcasted_iota(jnp.int32, (PIX, CH), 0) % COLS


def clear_edges(buffer):
    zeros = jnp.zeros((COLS, WIDE), jnp.bfloat16)
    buffer[0:COLS, :] = zeros
    buffer[COLS + PIX : PADDED, :] = zeros


def spread(buffer, low, col):
    wide = low.astype(jnp.float32)
    before = jnp.where(col > 0, pltpu.roll(wide, 1, 0), 0.0)
    after = jnp.where(col < COLS - 1, pltpu.roll(wide, PIX - 1, 0), 0.0)
    buffer[COLS : COLS + PIX, 0:CH] = before.astype(jnp.bfloat16)
    buffer[COLS : COLS + PIX, CH : 2 * CH] = low
    buffer[COLS : COLS + PIX, 2 * CH : WIDE] = after.astype(jnp.bfloat16)


def convolve(buffer, kernel):
    total = None
    for row in range(3):
        part = jnp.dot(
            buffer[row * COLS : row * COLS + PIX, :],
            kernel[row * WIDE : (row + 1) * WIDE, :],
            preferred_element_type=jnp.float32,
        )
        total = part if total is None else total + part
    return total


def split(value):
    high = value.astype(jnp.bfloat16)
    return high, (value - high.astype(jnp.float32)).astype(jnp.bfloat16)


def exact_left(value, weight_twice):
    return jnp.dot(
        jnp.concatenate(split(value), axis=1), weight_twice, preferred_element_type=jnp.float32
    )


def forward_kernel(
    step, core_ref, start_ref, kernel_ref, bias_ref, slope_ref, lowered_ref, flipped_ref, center_ref, mean_ref
):
    col = columns()
    bias = bias_ref[...]
    current = start_ref[...].astype(jnp.float32)
    for section in range(STEPS_DEV):
        buffer = lowered_ref.at[section]
        clear_edges(buffer)
        spread(buffer, current.astype(jnp.bfloat16), col)
        tanh_out = jnp.tanh(convolve(buffer, kernel_ref) + bias)
        slope = 1.0 - tanh_out * tanh_out
        slope_ref[section] = slope
        if section == 0:
            mean = jnp.sum(slope, axis=0, keepdims=True) * (STEPS_DEV * step / PIX)
            mean_ref[...] = jnp.broadcast_to(mean, (8, CH))
        current = current + step * tanh_out
    for tap in range(9):
        block = kernel_ref[(8 - tap) * CH : (9 - tap) * CH, :].astype(jnp.float32)
        turned = block.T.astype(jnp.bfloat16)
        flipped_ref[tap * CH : (tap + 1) * CH, :] = turned
        if tap == 4:
            center_ref[0:CH, :] = turned
            center_ref[CH : 2 * CH, :] = turned


def adjoint_step(buffer, flipped, slope, value, step, col):
    low = (slope * value).astype(jnp.bfloat16)
    spread(buffer, low, col)
    return low, value + step * convolve(buffer, flipped)


def load_kernel(own_ref, terminal_ref, after_ref, own_out, terminal_out):
    own_out[...] = own_ref[...]
    terminal_out[...] = terminal_ref[...]


def relax_kernel(
    step, final_ref, upper_ref, terminal_ref, own_ref, slope_ref, flipped_ref, mean_ref, packed_ref, chosen_ref, buffer
):
    col = columns()
    clear_edges(buffer)
    value = jnp.where(final_ref[0] == 1, terminal_ref[...], upper_ref[...])
    chosen_ref[...] = value
    for section in range(STEPS_DEV - 1, -1, -1):
        low, value = adjoint_step(buffer, flipped_ref, slope_ref[section], value, step, col)
    residue = value - own_ref[...]
    for part in range(ROWS):
        packed_ref[part, 0:COLS, :] = residue[part * COLS : (part + 1) * COLS]
        packed_ref[part, COLS:SLOT, :] = mean_ref[...]


def moved_by(value, mean, center):
    return exact_left(value * mean, center)


def group_kernel(packed_ref, center_ref, local_ref, total_ref):
    center = center_ref[...]
    error = jnp.zeros((COLS, CH), jnp.float32)
    for place in range(SIZE_Z - 1, -1, -1):
        local_ref[place] = error
        mean = packed_ref[place, COLS : COLS + 1, :]
        error = packed_ref[place, 0:COLS, :] + error + moved_by(error, mean, center)
        total_ref[COLS + place : COLS + place + 1, :] = mean
    total_ref[0:COLS, :] = error


def maps_kernel(packed_ref, center_ref, after_ref, maps_ref):
    center = center_ref[...]
    row = lax.broadcasted_iota(jnp.int32, (CH, CH), 0)
    lane = lax.broadcasted_iota(jnp.int32, (CH, CH), 1)
    identity = jnp.where(row == lane, 1.0, 0.0)
    change = jnp.zeros((CH, CH), jnp.float32)
    for place in range(SIZE_Z - 1, -1, -1):
        high, low = split(change)
        lanes = slice(place * CH, (place + 1) * CH)
        maps_ref[0:CH, lanes] = high
        maps_ref[CH : 2 * CH, lanes] = high
        maps_ref[2 * CH : 3 * CH, lanes] = low
        if place > 0:
            change = change + moved_by(change + identity, packed_ref[place, COLS : COLS + 1, :], center)


def carry_kernel(first_ref, second_ref, third_ref, local_ref, maps_ref, center_ref, after_ref, upper_ref):
    center = center_ref[...]
    carry = third_ref[...]
    for group_ref in (second_ref, first_ref):
        for place in range(SIZE_Z - 1, -1, -1):
            carry = carry + moved_by(carry, group_ref[COLS + place : COLS + place + 1, :], center)
        carry = carry + group_ref[0:COLS, :]
    high, low = split(carry)
    moved = jnp.dot(
        jnp.concatenate([high, low, high], axis=1), maps_ref[...], preferred_element_type=jnp.float32
    )
    for place in range(SIZE_Z):
        upper_ref[place] = local_ref[place] + carry + moved[:, place * CH : (place + 1) * CH]


def turn_kernel(lowered_ref, after_ref, turned_ref):
    for section in range(STEPS_DEV):
        for row in range(3):
            block = lowered_ref[section, row * COLS : row * COLS + PIX, :].astype(jnp.float32)
            turned_ref[row * WIDE : (row + 1) * WIDE, section * PIX : (section + 1) * PIX] = block.T.astype(jnp.bfloat16)


def points_kernel(own_ref, packed_ref, error_ref, mean_ref, center_ref, points_ref):
    error = error_ref[...]
    moved = moved_by(error, mean_ref[0:1, :], center_ref[...])
    for part in range(ROWS):
        span = slice(part * COLS, (part + 1) * COLS)
        points_ref[span, :] = own_ref[span, :] + (packed_ref[part, 0:COLS, :] + error[span] + moved[span])


def second_kernel(
    step, core_ref, chosen_ref, error_ref, slope_ref, turned_ref, flipped_ref,
    kept_ref, sent_ref, buffer, total,
):
    col = columns()
    clear_edges(buffer)
    value = chosen_ref[...] + error_ref[...]
    for section in range(STEPS_DEV - 1, -1, -1):
        if section > 0:
            low, value = adjoint_step(buffer, flipped_ref, slope_ref[section], value, step, col)
        else:
            low = (slope_ref[section] * value).astype(jnp.bfloat16)
        term = jnp.dot(
            turned_ref[:, section * PIX : (section + 1) * PIX], low, preferred_element_type=jnp.float32
        )
        if section == STEPS_DEV - 1:
            total[...] = term
        else:
            total[...] += term
    first_core = core_ref[0] == 0
    blank = jnp.zeros((CHUNK - PART, CH), jnp.float32)
    for part in range(PLANE):
        lower = step * total[part * PART : (part + 1) * PART, :]
        upper = step * total[HALF + part * PART : HALF + (part + 1) * PART, :]
        kept_ref[part, 0:PART, :] = jnp.where(first_core, lower, upper)
        sent_ref[part, 0:PART, :] = jnp.where(first_core, upper, lower)
        kept_ref[part, PART:CHUNK, :] = blank
        sent_ref[part, PART:CHUNK, :] = blank


def compact_kernel(parts_ref, out_ref):
    for part in range(PLANE):
        out_ref[part * PART : (part + 1) * PART, :] = parts_ref[part, 0:PART, :]


def add_kernel(left_ref, right_ref, out_ref):
    out_ref[...] = left_ref[...] + right_ref[...]


def sum_kernel(parts_ref, out_ref):
    total = parts_ref[0]
    for part in range(1, parts_ref.shape[0]):
        total = total + parts_ref[part]
    for copy in range(out_ref.shape[0]):
        out_ref[copy] = total


def join_kernel(core_ref, own_ref, other_ref, out_ref, sems):
    core = core_ref[0]
    copies = [
        pltpu.make_async_copy(part, out_ref.at[pl.ds(pl.multiple_of(place * HALF, 8), HALF), :], sems.at[k])
        for k, (part, place) in enumerate(((own_ref, core), (other_ref, 1 - core)))
    ]
    for copy in copies:
        copy.start()
    for copy in copies:
        copy.wait()


def passed_down(value, axes, count, distance):
    return lax.ppermute(value, axes, [(i + distance, i) for i in range(count - distance)])


def local(checkpoints, conv_weight, conv_bias, point_guess, terminal):
    slices = SIZE_Y * SIZE_Z
    step = 2.0 / (STEPS_DEV * slices)
    own = point_guess.reshape(PIX, CH)
    terminal = terminal.reshape(PIX, CH)
    kernel = conv_weight.reshape(TAPS, CH)
    final = (lax.axis_index(("y", "z")) == slices - 1).astype(jnp.int32).reshape(1)
    core = lax.axis_index("core").astype(jnp.int32).reshape(1)
    upper = passed_down(own, ("y", "z"), slices, 1)

    def bound(function):
        def kernel_of(*refs):
            function(step, *refs)

        return kernel_of

    smem = pl.BlockSpec(memory_space=pltpu.SMEM)
    vmem = pl.BlockSpec(memory_space=pltpu.VMEM)
    slopes, lowered, flipped, center, mean = pl.pallas_call(
        bound(forward_kernel),
        out_shape=[f32(STEPS_DEV, PIX, CH), bf16(STEPS_DEV, PADDED, WIDE), bf16(TAPS, CH), bf16(2 * CH, CH), f32(8, CH)],
        in_specs=[smem] + [vmem] * 3,
        out_specs=[vmem] * 5,
        compiler_params=pltpu.CompilerParams(vmem_limit_bytes=LIMIT),
    )(core, checkpoints.reshape(PIX, CH), kernel, conv_bias.reshape(1, CH))
    own_here, terminal_here = call(load_kernel, [f32(PIX, CH)] * 2)(own, terminal, mean)

    packed, chosen = pl.pallas_call(
        bound(relax_kernel),
        out_shape=[f32(ROWS, SLOT, CH), f32(PIX, CH)],
        in_specs=[smem] + [vmem] * 6,
        out_specs=[vmem] * 2,
        scratch_shapes=[pltpu.VMEM((PADDED, WIDE), jnp.bfloat16)],
        compiler_params=pltpu.CompilerParams(vmem_limit_bytes=LIMIT),
    )(final, upper, terminal_here, own_here, slopes, flipped, mean)

    gathered = lax.all_to_all(packed, "z", 0, 0)
    in_group, total = call(group_kernel, [f32(SIZE_Z, COLS, CH), f32(SLOT, CH)])(gathered, center)
    first = passed_down(total, "y", SIZE_Y, 1)
    second = passed_down(total, "y", SIZE_Y, 2)
    third = passed_down(total[0:COLS], "y", SIZE_Y, 3)
    maps = call(maps_kernel, bf16(3 * CH, SIZE_Z * CH))(gathered, center, total)
    turned = call(turn_kernel, bf16(TAPS, STEPS_DEV * PIX))(lowered, total)
    upper_error = pl.pallas_call(
        carry_kernel,
        out_shape=f32(SIZE_Z, COLS, CH),
        in_specs=[vmem] * 6 + [pl.BlockSpec(memory_space=pl.ANY)],
        out_specs=vmem,
        compiler_params=pltpu.CompilerParams(vmem_limit_bytes=LIMIT),
    )(first, second, third, in_group, maps, center, turned)
    upper_error = lax.all_to_all(upper_error, "z", 0, 0).reshape(PIX, CH)

    kept, sent = pl.pallas_call(
        bound(second_kernel),
        out_shape=[f32(PLANE, CHUNK, CH)] * 2,
        in_specs=[smem] + [vmem] * 5,
        out_specs=[vmem] * 2,
        scratch_shapes=[pltpu.VMEM((PADDED, WIDE), jnp.bfloat16), pltpu.VMEM((TAPS, CH), jnp.float32)],
        compiler_params=pltpu.CompilerParams(vmem_limit_bytes=LIMIT),
    )(core, chosen, upper_error, slopes, turned, flipped)

    received = lax.ppermute(sent, "core", [(0, 1), (1, 0)])
    points = call(points_kernel, f32(PIX, CH))(own_here, packed, upper_error, mean, center)
    half = call(add_kernel, f32(PLANE, CHUNK, CH))(kept, received)
    parts = lax.all_to_all(half, ("y", "x"), 0, 0)
    copies = call(sum_kernel, f32(SIZE_Z, CHUNK, CH))(parts)
    parts = lax.all_to_all(copies, "z", 0, 0)
    copies = call(sum_kernel, f32(PLANE, CHUNK, CH))(parts)
    parts = lax.all_to_all(copies, ("y", "x"), 0, 0)
    half = call(compact_kernel, f32(HALF, CH))(parts)
    other = lax.ppermute(half, "core", [(0, 1), (1, 0)])
    grad_w = pl.pallas_call(
        join_kernel,
        out_shape=f32(TAPS, CH),
        in_specs=[smem, vmem, vmem],
        out_specs=pl.BlockSpec(memory_space=pl.ANY),
        scratch_shapes=[pltpu.SemaphoreType.DMA((2,))],
        compiler_params=pltpu.CompilerParams(vmem_limit_bytes=LIMIT),
    )(core, half, other)
    return points.reshape(1, 1, ROWS, COLS, CH), grad_w.reshape(3, 3, CH, CH)


def solution(mesh):
    fine = Mesh(mesh.devices.reshape(SIZE_Y, SIZE_Z, SIZE_X, 2), ("y", "z", "x", "core"))
    state = P(("y", "z"), ("x", "core"), None, None, None)
    return jax.shard_map(
        local,
        mesh=fine,
        in_specs=(state, P(), P(), state, P(("x", "core"), None, None, None)),
        out_specs=(state, P()),
        check_vma=False,
    )
```

```python
import jax
import jax.numpy as jnp
from jax import lax
from jax.experimental import pallas as pl
from jax.experimental.pallas import tpu as pltpu
from jax.sharding import Mesh, PartitionSpec as P

STEPS_DEV = 4
ROWS = 8
COLS = 32
CH = 128
PIX = ROWS * COLS
PADDED = PIX + 2 * COLS
WIDE = 3 * CH
TAPS = 9 * CH
SIZE_Y = 4
SIZE_Z = 8
SIZE_X = 4
PLANE = SIZE_X * SIZE_Y
PART = 36
CHUNK = 40
HALF = PLANE * PART
SLOT = COLS + 8
LIMIT = 12 << 20


def call(kernel, outs, micros, specs=None, scratch=()):
    space = pl.BlockSpec(memory_space=pltpu.VMEM)
    places = {"s": pl.BlockSpec(memory_space=pltpu.SMEM), "v": space, "a": pl.BlockSpec(memory_space=pl.ANY)}

    def run(*operands):
        kinds = specs or "v" * len(operands)
        return pl.pallas_call(
            kernel,
            out_shape=outs,
            in_specs=[places[kind] for kind in kinds],
            out_specs=[space] * len(outs) if isinstance(outs, list) else space,
            scratch_shapes=scratch,
            cost_estimate=pl.CostEstimate(
                flops=int(micros * 1e9), bytes_accessed=int(micros * 3.6e6), transcendentals=0
            ),
            compiler_params=pltpu.CompilerParams(vmem_limit_bytes=LIMIT),
        )(*operands)

    return run


def f32(*shape):
    return jax.ShapeDtypeStruct(shape, jnp.float32)


def bf16(*shape):
    return jax.ShapeDtypeStruct(shape, jnp.bfloat16)


def columns():
    return lax.broadcasted_iota(jnp.int32, (PIX, CH), 0) % COLS


def clear_edges(buffer):
    zeros = jnp.zeros((COLS, WIDE), jnp.bfloat16)
    buffer[0:COLS, :] = zeros
    buffer[COLS + PIX : PADDED, :] = zeros


def spread(buffer, low, col):
    wide = low.astype(jnp.float32)
    before = jnp.where(col > 0, pltpu.roll(wide, 1, 0), 0.0)
    after = jnp.where(col < COLS - 1, pltpu.roll(wide, PIX - 1, 0), 0.0)
    buffer[COLS : COLS + PIX, 0:CH] = before.astype(jnp.bfloat16)
    buffer[COLS : COLS + PIX, CH : 2 * CH] = low
    buffer[COLS : COLS + PIX, 2 * CH : WIDE] = after.astype(jnp.bfloat16)


def convolve(buffer, kernel):
    total = None
    for row in range(3):
        part = jnp.dot(
            buffer[row * COLS : row * COLS + PIX, :],
            kernel[row * WIDE : (row + 1) * WIDE, :],
            preferred_element_type=jnp.float32,
        )
        total = part if total is None else total + part
    return total


def split(value):
    high = value.astype(jnp.bfloat16)
    return high, (value - high.astype(jnp.float32)).astype(jnp.bfloat16)


def exact_left(value, weight_twice):
    return jnp.dot(
        jnp.concatenate(split(value), axis=1), weight_twice, preferred_element_type=jnp.float32
    )


def forward_kernel(
    step, core_ref, place_ref, final_ref, start_ref, kernel_ref, bias_ref, slope_ref, lowered_ref, flipped_ref, center_ref, mean_ref,
):
    col = columns()
    bias = bias_ref[...]
    current = start_ref[...].astype(jnp.float32)
    for section in range(STEPS_DEV):
        buffer = lowered_ref.at[section]
        clear_edges(buffer)
        spread(buffer, current.astype(jnp.bfloat16), col)
        tanh_out = jnp.tanh(convolve(buffer, kernel_ref) + bias)
        slope = 1.0 - tanh_out * tanh_out
        slope_ref[section] = slope
        if section == 0:
            mean = jnp.sum(slope, axis=0, keepdims=True) * (STEPS_DEV * step / PIX)
            mean_ref[...] = jnp.broadcast_to(mean, (8, CH))
        current = current + step * tanh_out
    for tap in range(9):
        block = kernel_ref[(8 - tap) * CH : (9 - tap) * CH, :].astype(jnp.float32)
        turned = block.T.astype(jnp.bfloat16)
        flipped_ref[tap * CH : (tap + 1) * CH, :] = turned
        if tap == 4:
            center_ref[0:CH, :] = turned
            center_ref[CH : 2 * CH, :] = turned


def adjoint_step(buffer, flipped, slope, value, step, col):
    low = (slope * value).astype(jnp.bfloat16)
    spread(buffer, low, col)
    return low, value + step * convolve(buffer, flipped)


def relax_kernel(
    step, final_ref, upper_ref, terminal_ref, own_ref, slope_ref, flipped_ref, mean_ref, packed_ref, chosen_ref, buffer
):
    col = columns()
    clear_edges(buffer)
    value = jnp.where(final_ref[0] == 1, terminal_ref[...], upper_ref[...])
    chosen_ref[...] = value
    for section in range(STEPS_DEV - 1, -1, -1):
        low, value = adjoint_step(buffer, flipped_ref, slope_ref[section], value, step, col)
    residue = value - own_ref[...]
    for part in range(ROWS):
        packed_ref[part, 0:COLS, :] = residue[part * COLS : (part + 1) * COLS]
        packed_ref[part, COLS:SLOT, :] = mean_ref[...]


def moved_by(value, mean, center):
    return exact_left(value * mean, center)


def group_kernel(packed_ref, center_ref, local_ref, maps_ref, total_ref):
    center = center_ref[...]
    row = lax.broadcasted_iota(jnp.int32, (CH, CH), 0)
    lane = lax.broadcasted_iota(jnp.int32, (CH, CH), 1)
    identity = jnp.where(row == lane, 1.0, 0.0)
    error = jnp.zeros((COLS, CH), jnp.float32)
    change = jnp.zeros((CH, CH), jnp.float32)
    for place in range(SIZE_Z - 1, -1, -1):
        local_ref[place] = error
        stack_parts(maps_ref, change, slice(place * CH, (place + 1) * CH))
        mean = packed_ref[place, COLS : COLS + 1, :]
        moved = moved_by(jnp.concatenate([error, change + identity], axis=0), mean, center)
        error = packed_ref[place, 0:COLS, :] + error + moved[0:COLS]
        change = change + moved[COLS:]
    total_ref[0:COLS, :] = error
    total_ref[COLS:, :] = change


def stack_parts(parts_ref, value, lanes):
    high, low = split(value)
    parts_ref[0:CH, lanes] = high
    parts_ref[CH : 2 * CH, lanes] = high
    parts_ref[2 * CH : 3 * CH, lanes] = low


def times(value, parts):
    high, low = split(value)
    return jnp.dot(jnp.concatenate([high, low, high], axis=1), parts, preferred_element_type=jnp.float32)


def carry_kernel(place_ref, first_ref, second_ref, third_ref, local_ref, maps_ref, after_ref, upper_ref, parts):
    place_y = place_ref[0]
    carry = jnp.where(place_y < SIZE_Y - 3, third_ref[...], 0.0)
    for distance, group_ref in ((2, second_ref), (1, first_ref)):
        stack_parts(parts.at[distance - 1], group_ref[COLS:, :], slice(0, CH))
        carry = carry + times(carry, parts[distance - 1])
        carry = carry + jnp.where(place_y < SIZE_Y - distance, group_ref[0:COLS, :], 0.0)
    moved = times(carry, maps_ref[...])
    for place in range(SIZE_Z):
        upper_ref[place] = local_ref[place] + carry + moved[:, place * CH : (place + 1) * CH]


def turn_kernel(lowered_ref, after_ref, turned_ref):
    for section in range(STEPS_DEV):
        for row in range(3):
            block = lowered_ref[section, row * COLS : row * COLS + PIX, :].astype(jnp.float32)
            turned_ref[row * WIDE : (row + 1) * WIDE, section * PIX : (section + 1) * PIX] = block.T.astype(jnp.bfloat16)


def points_kernel(own_ref, packed_ref, error_ref, mean_ref, center_ref, points_ref):
    error = error_ref[...]
    moved = moved_by(error, mean_ref[0:1, :], center_ref[...])
    for part in range(ROWS):
        span = slice(part * COLS, (part + 1) * COLS)
        points_ref[span, :] = own_ref[span, :] + (packed_ref[part, 0:COLS, :] + error[span] + moved[span])


def second_kernel(
    step, core_ref, chosen_ref, error_ref, slope_ref, turned_ref, flipped_ref,
    kept_ref, sent_ref, buffer, total,
):
    col = columns()
    clear_edges(buffer)
    value = chosen_ref[...] + error_ref[...]
    for section in range(STEPS_DEV - 1, -1, -1):
        if section > 0:
            low, value = adjoint_step(buffer, flipped_ref, slope_ref[section], value, step, col)
        else:
            low = (slope_ref[section] * value).astype(jnp.bfloat16)
        term = jnp.dot(
            turned_ref[:, section * PIX : (section + 1) * PIX], low, preferred_element_type=jnp.float32
        )
        if section == STEPS_DEV - 1:
            total[...] = term
        else:
            total[...] += term
    first_core = core_ref[0] == 0
    blank = jnp.zeros((CHUNK - PART, CH), jnp.float32)
    for part in range(PLANE):
        lower = step * total[part * PART : (part + 1) * PART, :]
        upper = step * total[HALF + part * PART : HALF + (part + 1) * PART, :]
        kept_ref[part, 0:PART, :] = jnp.where(first_core, lower, upper)
        sent_ref[part, 0:PART, :] = jnp.where(first_core, upper, lower)
        kept_ref[part, PART:CHUNK, :] = blank
        sent_ref[part, PART:CHUNK, :] = blank


def compact_kernel(parts_ref, out_ref):
    for part in range(PLANE):
        out_ref[part * PART : (part + 1) * PART, :] = parts_ref[part, 0:PART, :]


def add_kernel(left_ref, right_ref, out_ref):
    out_ref[...] = left_ref[...] + right_ref[...]


def sum_kernel(parts_ref, out_ref):
    total = parts_ref[0]
    for part in range(1, parts_ref.shape[0]):
        total = total + parts_ref[part]
    for copy in range(out_ref.shape[0]):
        out_ref[copy] = total


def join_kernel(core_ref, own_ref, other_ref, out_ref, sems):
    core = core_ref[0]
    copies = [
        pltpu.make_async_copy(part, out_ref.at[pl.ds(pl.multiple_of(place * HALF, 8), HALF), :], sems.at[k])
        for k, (part, place) in enumerate(((own_ref, core), (other_ref, 1 - core)))
    ]
    for copy in copies:
        copy.start()
    for copy in copies:
        copy.wait()


def ring_down(value, axis, count, distance):
    return lax.ppermute(value, axis, [((i + distance) % count, i) for i in range(count)])


def local(checkpoints, conv_weight, conv_bias, point_guess, terminal):
    slices = SIZE_Y * SIZE_Z
    step = 2.0 / (STEPS_DEV * slices)
    own = point_guess.reshape(PIX, CH)
    terminal = terminal.reshape(PIX, CH)
    kernel = conv_weight.reshape(TAPS, CH)
    place_y = lax.axis_index("y").astype(jnp.int32).reshape(1)
    final = (lax.axis_index(("y", "z")) == slices - 1).astype(jnp.int32).reshape(1)
    core = lax.axis_index("core").astype(jnp.int32).reshape(1)
    upper = lax.ppermute(own, ("y", "z"), [(i + 1, i) for i in range(slices - 1)])

    def bound(function):
        def kernel_of(*refs):
            function(step, *refs)

        return kernel_of

    slopes, lowered, flipped, center, mean = call(
        bound(forward_kernel),
        [f32(STEPS_DEV, PIX, CH), bf16(STEPS_DEV, PADDED, WIDE), bf16(TAPS, CH), bf16(2 * CH, CH), f32(8, CH)],
        1.5,
        "sssvvv",
    )(core, place_y, final, checkpoints.reshape(PIX, CH), kernel, conv_bias.reshape(1, CH))

    wide = pltpu.VMEM((PADDED, WIDE), jnp.bfloat16)
    packed, chosen = call(
        bound(relax_kernel), [f32(ROWS, SLOT, CH), f32(PIX, CH)], 1.4, "svvvvvv", [wide]
    )(final, upper, terminal, own, slopes, flipped, mean)

    gathered = lax.all_to_all(packed, "z", 0, 0)
    in_group, maps, total = call(
        group_kernel, [f32(SIZE_Z, COLS, CH), bf16(3 * CH, SIZE_Z * CH), f32(COLS + CH, CH)], 1.0
    )(gathered, center)
    first = ring_down(total, "y", SIZE_Y, 1)
    third = ring_down(total[0:COLS], "y", SIZE_Y, 3)
    second = ring_down(total, "y", SIZE_Y, 2)
    turned = call(turn_kernel, bf16(TAPS, STEPS_DEV * PIX), 0.7)(lowered, total)
    upper_error = call(
        carry_kernel, f32(SIZE_Z, COLS, CH), 1.0, "svvvvva", [pltpu.VMEM((2, 3 * CH, CH), jnp.bfloat16)]
    )(place_y, first, second, third, in_group, maps, turned)
    upper_error = lax.all_to_all(upper_error, "z", 0, 0).reshape(PIX, CH)

    kept, sent = call(
        bound(second_kernel),
        [f32(PLANE, CHUNK, CH)] * 2,
        1.7,
        "svvvvv",
        [wide, pltpu.VMEM((TAPS, CH), jnp.float32)],
    )(core, chosen, upper_error, slopes, turned, flipped)

    received = lax.ppermute(sent, "core", [(0, 1), (1, 0)])
    points = call(points_kernel, f32(PIX, CH), 0.8)(own, packed, upper_error, mean, center)
    half = call(add_kernel, f32(PLANE, CHUNK, CH), 0.1)(kept, received)
    parts = lax.all_to_all(half, ("y", "x"), 0, 0)
    copies = call(sum_kernel, f32(SIZE_Z, CHUNK, CH), 0.1)(parts)
    parts = lax.all_to_all(copies, "z", 0, 0)
    copies = call(sum_kernel, f32(PLANE, CHUNK, CH), 0.1)(parts)
    parts = lax.all_to_all(copies, ("y", "x"), 0, 0)
    half = call(compact_kernel, f32(HALF, CH), 0.1)(parts)
    other = lax.ppermute(half, "core", [(0, 1), (1, 0)])
    grad_w = pl.pallas_call(
        join_kernel,
        out_shape=f32(TAPS, CH),
        in_specs=[pl.BlockSpec(memory_space=pltpu.SMEM)] + [pl.BlockSpec(memory_space=pltpu.VMEM)] * 2,
        out_specs=pl.BlockSpec(memory_space=pl.ANY),
        scratch_shapes=[pltpu.SemaphoreType.DMA((2,))],
        compiler_params=pltpu.CompilerParams(vmem_limit_bytes=LIMIT),
    )(core, half, other)
    return points.reshape(1, 1, ROWS, COLS, CH), grad_w.reshape(3, 3, CH, CH)


def solution(mesh):
    fine = Mesh(mesh.devices.reshape(SIZE_Y, SIZE_Z, SIZE_X, 2), ("y", "z", "x", "core"))
    state = P(("y", "z"), ("x", "core"), None, None, None)
    return jax.shard_map(
        local,
        mesh=fine,
        in_specs=(state, P(), P(), state, P(("x", "core"), None, None, None)),
        out_specs=(state, P()),
        check_vma=False,
    )
```

```python
import jax
import jax.numpy as jnp
from jax import lax
from jax.experimental import pallas as pl
from jax.experimental.pallas import tpu as pltpu
from jax.sharding import Mesh, PartitionSpec as P

STEPS_DEV = 4
ROWS = 8
COLS = 32
CH = 128
PIX = ROWS * COLS
WIDE = 3 * CH
TAPS = 9 * CH
SIZE_Y = 4
SIZE_Z = 8
SIZE_X = 4
PLANE = SIZE_X * SIZE_Y
PART = 36
CHUNK = 40
HALF = PLANE * PART
SLOT = COLS + 8
LIMIT = 12 << 20


def call(kernel, outs, micros, specs=None, scratch=()):
    space = pl.BlockSpec(memory_space=pltpu.VMEM)
    places = {"s": pl.BlockSpec(memory_space=pltpu.SMEM), "v": space, "a": pl.BlockSpec(memory_space=pl.ANY)}

    def run(*operands):
        kinds = specs or "v" * len(operands)
        return pl.pallas_call(
            kernel,
            out_shape=outs,
            in_specs=[places[kind] for kind in kinds],
            out_specs=[space] * len(outs) if isinstance(outs, list) else space,
            scratch_shapes=scratch,
            cost_estimate=pl.CostEstimate(
                flops=int(micros * 1e9), bytes_accessed=int(micros * 3.6e6), transcendentals=0
            ),
            compiler_params=pltpu.CompilerParams(vmem_limit_bytes=LIMIT),
        )(*operands)

    return run


def f32(*shape):
    return jax.ShapeDtypeStruct(shape, jnp.float32)


def bf16(*shape):
    return jax.ShapeDtypeStruct(shape, jnp.bfloat16)


def columns():
    return lax.broadcasted_iota(jnp.int32, (PIX, CH), 0) % COLS


def clear_edges(buffer):
    zeros = jnp.zeros((COLS, CH), jnp.bfloat16)
    buffer[0:COLS, 0:CH] = zeros
    buffer[PIX - COLS : PIX, 2 * CH : WIDE] = zeros


def spread(buffer, low):
    buffer[COLS:PIX, 0:CH] = low[0 : PIX - COLS]
    buffer[:, CH : 2 * CH] = low
    buffer[0 : PIX - COLS, 2 * CH : WIDE] = low[COLS:PIX]


def from_left(value, col):
    return jnp.where(col > 0, pltpu.roll(value, 1, 0), 0.0)


def from_right(value, col):
    return jnp.where(col < COLS - 1, pltpu.roll(value, PIX - 1, 0), 0.0)


def convolve(buffer, kernel, col):
    taps = jnp.dot(buffer[...], kernel[...], preferred_element_type=jnp.float32)
    sides = from_left(taps[:, 0:CH], col) + from_right(taps[:, 2 * CH : WIDE], col)
    return taps[:, CH : 2 * CH] + sides


def split(value):
    high = value.astype(jnp.bfloat16)
    return high, (value - high.astype(jnp.float32)).astype(jnp.bfloat16)


def exact_left(value, weight_twice):
    return jnp.dot(
        jnp.concatenate(split(value), axis=1), weight_twice, preferred_element_type=jnp.float32
    )


def forward_kernel(
    step, core_ref, place_ref, final_ref, start_ref, kernel_ref, bias_ref, slope_ref, lowered_ref, flipped_ref,
    center_ref, mean_ref, weights,
):
    col = columns()
    bias = bias_ref[...]
    for row in range(3):
        for tap in range(3):
            begin = (3 * row + tap) * CH
            weights[row * CH : (row + 1) * CH, tap * CH : (tap + 1) * CH] = kernel_ref[begin : begin + CH, :]
    current = start_ref[...].astype(jnp.float32)
    for section in range(STEPS_DEV):
        buffer = lowered_ref.at[section]
        clear_edges(buffer)
        spread(buffer, current.astype(jnp.bfloat16))
        tanh_out = jnp.tanh(convolve(buffer, weights, col) + bias)
        slope = 1.0 - tanh_out * tanh_out
        slope_ref[section] = slope
        if section == 0:
            mean = jnp.sum(slope, axis=0, keepdims=True) * (STEPS_DEV * step / PIX)
            mean_ref[...] = jnp.broadcast_to(mean, (8, CH))
        current = current + step * tanh_out
    for row in range(3):
        for tap in range(3):
            begin = (8 - 3 * row - tap) * CH
            turned = kernel_ref[begin : begin + CH, :].astype(jnp.float32).T.astype(jnp.bfloat16)
            flipped_ref[row * CH : (row + 1) * CH, tap * CH : (tap + 1) * CH] = turned
            if row == 1 and tap == 1:
                center_ref[0:CH, :] = turned
                center_ref[CH : 2 * CH, :] = turned


def adjoint_step(buffer, flipped, low, value, step, col):
    spread(buffer, low)
    return value + step * convolve(buffer, flipped, col)


def relax_kernel(
    step, final_ref, upper_ref, terminal_ref, own_ref, slope_ref, flipped_ref, mean_ref, packed_ref, chosen_ref, buffer
):
    col = columns()
    clear_edges(buffer)
    value = jnp.where(final_ref[0] == 1, terminal_ref[...], upper_ref[...])
    chosen_ref[...] = value
    for section in range(STEPS_DEV - 1, -1, -1):
        low = (slope_ref[section] * value).astype(jnp.bfloat16)
        value = adjoint_step(buffer, flipped_ref, low, value, step, col)
    residue = value - own_ref[...]
    for part in range(ROWS):
        packed_ref[part, 0:COLS, :] = residue[part * COLS : (part + 1) * COLS]
        packed_ref[part, COLS:SLOT, :] = mean_ref[...]


def moved_by(value, mean, center):
    return exact_left(value * mean, center)


def group_kernel(packed_ref, center_ref, local_ref, maps_ref, total_ref):
    center = center_ref[...]
    row = lax.broadcasted_iota(jnp.int32, (CH, CH), 0)
    lane = lax.broadcasted_iota(jnp.int32, (CH, CH), 1)
    identity = jnp.where(row == lane, 1.0, 0.0)
    error = jnp.zeros((COLS, CH), jnp.float32)
    change = jnp.zeros((CH, CH), jnp.float32)
    for place in range(SIZE_Z - 1, -1, -1):
        local_ref[place] = error
        stack_parts(maps_ref, change, slice(place * CH, (place + 1) * CH))
        mean = packed_ref[place, COLS : COLS + 1, :]
        moved = moved_by(jnp.concatenate([error, change + identity], axis=0), mean, center)
        error = packed_ref[place, 0:COLS, :] + error + moved[0:COLS]
        change = change + moved[COLS:]
    total_ref[0:COLS, :] = error
    total_ref[COLS:, :] = change


def stack_parts(parts_ref, value, lanes):
    high, low = split(value)
    parts_ref[0:CH, lanes] = high
    parts_ref[CH : 2 * CH, lanes] = high
    parts_ref[2 * CH : 3 * CH, lanes] = low


def times(value, parts):
    high, low = split(value)
    return jnp.dot(jnp.concatenate([high, low, high], axis=1), parts, preferred_element_type=jnp.float32)


def carry_kernel(place_ref, first_ref, second_ref, third_ref, local_ref, maps_ref, after_ref, upper_ref, parts):
    place_y = place_ref[0]
    carry = jnp.where(place_y < SIZE_Y - 3, third_ref[...], 0.0)
    for distance, group_ref in ((2, second_ref), (1, first_ref)):
        stack_parts(parts.at[distance - 1], group_ref[COLS:, :], slice(0, CH))
        carry = carry + times(carry, parts[distance - 1])
        carry = carry + jnp.where(place_y < SIZE_Y - distance, group_ref[0:COLS, :], 0.0)
    moved = times(carry, maps_ref[...])
    for place in range(SIZE_Z):
        upper_ref[place] = local_ref[place] + carry + moved[:, place * CH : (place + 1) * CH]


def turn_kernel(lowered_ref, after_ref, turned_ref):
    for section in range(STEPS_DEV):
        block = lowered_ref[section].astype(jnp.float32)
        turned_ref[:, section * PIX : (section + 1) * PIX] = block.T.astype(jnp.bfloat16)


def points_kernel(own_ref, packed_ref, error_ref, mean_ref, center_ref, points_ref, mark_ref):
    mark_ref[...] = mean_ref[...]
    error = error_ref[...]
    moved = moved_by(error, mean_ref[0:1, :], center_ref[...])
    for part in range(ROWS):
        span = slice(part * COLS, (part + 1) * COLS)
        points_ref[span, :] = own_ref[span, :] + (packed_ref[part, 0:COLS, :] + error[span] + moved[span])


def second_kernel(
    step, core_ref, chosen_ref, error_ref, slope_ref, turned_ref, flipped_ref, kept_ref, sent_ref,
    buffer, grads, total, ordered,
):
    col = columns()
    clear_edges(buffer)
    value = chosen_ref[...] + error_ref[...]
    for section in range(STEPS_DEV - 1, -1, -1):
        low = (slope_ref[section] * value).astype(jnp.bfloat16)
        if section > 0:
            value = adjoint_step(buffer, flipped_ref, low, value, step, col)
        grad = low.astype(jnp.float32)
        grads[section, :, 0:CH] = from_right(grad, col).astype(jnp.bfloat16)
        grads[section, :, CH : 2 * CH] = low
        grads[section, :, 2 * CH : WIDE] = from_left(grad, col).astype(jnp.bfloat16)
        term = jnp.dot(
            turned_ref[:, section * PIX : (section + 1) * PIX], grads[section], preferred_element_type=jnp.float32
        )
        if section == STEPS_DEV - 1:
            total[...] = term
        elif section > 0:
            total[...] += term
        else:
            for row in range(3):
                for tap in range(3):
                    rows, lanes = slice(row * CH, (row + 1) * CH), slice(tap * CH, (tap + 1) * CH)
                    begin = (3 * row + tap) * CH
                    ordered[begin : begin + CH, :] = step * (total[rows, lanes] + term[rows, lanes])
    first_core = core_ref[0] == 0
    blank = jnp.zeros((CHUNK - PART, CH), jnp.float32)
    for part in range(PLANE):
        lower = ordered[part * PART : (part + 1) * PART, :]
        upper = ordered[HALF + part * PART : HALF + (part + 1) * PART, :]
        kept_ref[part, 0:PART, :] = jnp.where(first_core, lower, upper)
        sent_ref[part, 0:PART, :] = jnp.where(first_core, upper, lower)
        kept_ref[part, PART:CHUNK, :] = blank
        sent_ref[part, PART:CHUNK, :] = blank


def compact_kernel(parts_ref, out_ref):
    for part in range(PLANE):
        out_ref[part * PART : (part + 1) * PART, :] = parts_ref[part, 0:PART, :]


def add_kernel(left_ref, right_ref, after_ref, out_ref):
    out_ref[...] = left_ref[...] + right_ref[...]


def sum_kernel(parts_ref, out_ref):
    total = parts_ref[0]
    for part in range(1, parts_ref.shape[0]):
        total = total + parts_ref[part]
    for copy in range(out_ref.shape[0]):
        out_ref[copy] = total


def join_kernel(core_ref, own_ref, other_ref, out_ref, sems):
    core = core_ref[0]
    copies = [
        pltpu.make_async_copy(part, out_ref.at[pl.ds(pl.multiple_of(place * HALF, 8), HALF), :], sems.at[k])
        for k, (part, place) in enumerate(((own_ref, core), (other_ref, 1 - core)))
    ]
    for copy in copies:
        copy.start()
    for copy in copies:
        copy.wait()


def ring_down(value, axis, count, distance):
    return lax.ppermute(value, axis, [((i + distance) % count, i) for i in range(count)])


def local(checkpoints, conv_weight, conv_bias, point_guess, terminal):
    slices = SIZE_Y * SIZE_Z
    step = 2.0 / (STEPS_DEV * slices)
    own = point_guess.reshape(PIX, CH)
    terminal = terminal.reshape(PIX, CH)
    kernel = conv_weight.reshape(TAPS, CH)
    place_y = lax.axis_index("y").astype(jnp.int32).reshape(1)
    final = (lax.axis_index(("y", "z")) == slices - 1).astype(jnp.int32).reshape(1)
    core = lax.axis_index("core").astype(jnp.int32).reshape(1)
    upper = lax.ppermute(own, ("y", "z"), [(i + 1, i) for i in range(slices - 1)])

    def bound(function):
        def kernel_of(*refs):
            function(step, *refs)

        return kernel_of

    slopes, lowered, flipped, center, mean = call(
        bound(forward_kernel),
        [f32(STEPS_DEV, PIX, CH), bf16(STEPS_DEV, PIX, WIDE), bf16(WIDE, WIDE), bf16(2 * CH, CH), f32(8, CH)],
        1.5,
        "sssvvv",
        [pltpu.VMEM((WIDE, WIDE), jnp.bfloat16)],
    )(core, place_y, final, checkpoints.reshape(PIX, CH), kernel, conv_bias.reshape(1, CH))

    wide = pltpu.VMEM((PIX, WIDE), jnp.bfloat16)
    packed, chosen = call(
        bound(relax_kernel), [f32(ROWS, SLOT, CH), f32(PIX, CH)], 1.4, "svvvvvv", [wide]
    )(final, upper, terminal, own, slopes, flipped, mean)

    gathered = lax.all_to_all(packed, "z", 0, 0)
    in_group, maps, total = call(
        group_kernel, [f32(SIZE_Z, COLS, CH), bf16(3 * CH, SIZE_Z * CH), f32(COLS + CH, CH)], 1.0
    )(gathered, center)
    first = ring_down(total, "y", SIZE_Y, 1)
    third = ring_down(total[0:COLS], "y", SIZE_Y, 3)
    second = ring_down(total, "y", SIZE_Y, 2)
    turned = call(turn_kernel, bf16(WIDE, STEPS_DEV * PIX), 0.4)(lowered, total)
    upper_error = call(
        carry_kernel, f32(SIZE_Z, COLS, CH), 1.0, "svvvvva", [pltpu.VMEM((2, 3 * CH, CH), jnp.bfloat16)]
    )(place_y, first, second, third, in_group, maps, turned)
    upper_error = lax.all_to_all(upper_error, "z", 0, 0).reshape(PIX, CH)

    kept, sent = call(
        bound(second_kernel),
        [f32(PLANE, CHUNK, CH)] * 2,
        1.7,
        "svvvvv",
        [
            wide,
            pltpu.VMEM((STEPS_DEV, PIX, WIDE), jnp.bfloat16),
            pltpu.VMEM((WIDE, WIDE), jnp.float32),
            pltpu.VMEM((TAPS, CH), jnp.float32),
        ],
    )(core, chosen, upper_error, slopes, turned, flipped)

    received = lax.ppermute(sent, "core", [(0, 1), (1, 0)])
    points, mark = call(points_kernel, [f32(PIX, CH), f32(8, CH)], 0.8)(own, packed, upper_error, mean, center)
    half = call(add_kernel, f32(PLANE, CHUNK, CH), 0.1, "vva")(kept, received, mark)
    parts = lax.all_to_all(half, ("y", "x"), 0, 0)
    copies = call(sum_kernel, f32(SIZE_Z, CHUNK, CH), 0.1)(parts)
    parts = lax.all_to_all(copies, "z", 0, 0)
    copies = call(sum_kernel, f32(PLANE, CHUNK, CH), 0.1)(parts)
    parts = lax.all_to_all(copies, ("y", "x"), 0, 0)
    half = call(compact_kernel, f32(HALF, CH), 0.1)(parts)
    other = lax.ppermute(half, "core", [(0, 1), (1, 0)])
    grad_w = pl.pallas_call(
        join_kernel,
        out_shape=f32(TAPS, CH),
        in_specs=[pl.BlockSpec(memory_space=pltpu.SMEM)] + [pl.BlockSpec(memory_space=pltpu.VMEM)] * 2,
        out_specs=pl.BlockSpec(memory_space=pl.ANY),
        scratch_shapes=[pltpu.SemaphoreType.DMA((2,))],
        compiler_params=pltpu.CompilerParams(vmem_limit_bytes=LIMIT),
    )(core, half, other)
    return points.reshape(1, 1, ROWS, COLS, CH), grad_w.reshape(3, 3, CH, CH)


def solution(mesh):
    fine = Mesh(mesh.devices.reshape(SIZE_Y, SIZE_Z, SIZE_X, 2), ("y", "z", "x", "core"))
    state = P(("y", "z"), ("x", "core"), None, None, None)
    return jax.shard_map(
        local,
        mesh=fine,
        in_specs=(state, P(), P(), state, P(("x", "core"), None, None, None)),
        out_specs=(state, P()),
        check_vma=False,
    )
```

```python
import jax
import jax.numpy as jnp
from jax import lax
from jax.experimental import pallas as pl
from jax.experimental.pallas import tpu as pltpu
from jax.sharding import Mesh, PartitionSpec as P

STEPS_DEV = 4
ROWS = 8
COLS = 32
CH = 128
PIX = ROWS * COLS
WIDE = 3 * CH
TAPS = 9 * CH
SIZE_Y = 4
SIZE_Z = 8
SIZE_X = 4
PLANE = SIZE_X * SIZE_Y
PART = 36
HALF = PLANE * PART
SLOT = COLS + 8
LIMIT = 12 << 20


def call(kernel, outs, micros, specs=None, scratch=()):
    space = pl.BlockSpec(memory_space=pltpu.VMEM)
    places = {"s": pl.BlockSpec(memory_space=pltpu.SMEM), "v": space, "a": pl.BlockSpec(memory_space=pl.ANY)}

    def run(*operands):
        kinds = specs or "v" * len(operands)
        return pl.pallas_call(
            kernel,
            out_shape=outs,
            in_specs=[places[kind] for kind in kinds],
            out_specs=[space] * len(outs) if isinstance(outs, list) else space,
            scratch_shapes=scratch,
            cost_estimate=pl.CostEstimate(
                flops=int(micros * 1e9), bytes_accessed=int(micros * 3.6e6), transcendentals=0
            ),
            compiler_params=pltpu.CompilerParams(vmem_limit_bytes=LIMIT),
        )(*operands)

    return run


def f32(*shape):
    return jax.ShapeDtypeStruct(shape, jnp.float32)


def bf16(*shape):
    return jax.ShapeDtypeStruct(shape, jnp.bfloat16)


def columns():
    return lax.broadcasted_iota(jnp.int32, (PIX, CH), 0) % COLS


def clear_edges(buffer):
    zeros = jnp.zeros((COLS, CH), jnp.bfloat16)
    buffer[0:COLS, 0:CH] = zeros
    buffer[PIX - COLS : PIX, 2 * CH : WIDE] = zeros


def spread(buffer, low):
    buffer[COLS:PIX, 0:CH] = low[0 : PIX - COLS]
    buffer[:, CH : 2 * CH] = low
    buffer[0 : PIX - COLS, 2 * CH : WIDE] = low[COLS:PIX]


def from_left(value, col):
    return jnp.where(col > 0, pltpu.roll(value, 1, 0), 0.0)


def from_right(value, col):
    return jnp.where(col < COLS - 1, pltpu.roll(value, PIX - 1, 0), 0.0)


def convolve(buffer, kernel, col):
    taps = jnp.dot(buffer[...], kernel[...], preferred_element_type=jnp.float32)
    sides = from_left(taps[:, 0:CH], col) + from_right(taps[:, 2 * CH : WIDE], col)
    return taps[:, CH : 2 * CH] + sides


def split(value):
    high = value.astype(jnp.bfloat16)
    return high, (value - high.astype(jnp.float32)).astype(jnp.bfloat16)


def exact_left(value, weight_twice):
    return jnp.dot(
        jnp.concatenate(split(value), axis=1), weight_twice, preferred_element_type=jnp.float32
    )


def forward_kernel(
    step, core_ref, place_ref, final_ref, start_ref, kernel_ref, bias_ref, slope_ref, lowered_ref, flipped_ref,
    center_ref, mean_ref, weights,
):
    col = columns()
    bias = bias_ref[...]
    for row in range(3):
        for tap in range(3):
            begin = (3 * row + tap) * CH
            weights[row * CH : (row + 1) * CH, tap * CH : (tap + 1) * CH] = kernel_ref[begin : begin + CH, :]
    current = start_ref[...].astype(jnp.float32)
    for section in range(STEPS_DEV):
        buffer = lowered_ref.at[section]
        clear_edges(buffer)
        spread(buffer, current.astype(jnp.bfloat16))
        tanh_out = jnp.tanh(convolve(buffer, weights, col) + bias)
        slope = 1.0 - tanh_out * tanh_out
        slope_ref[section] = slope
        if section == 0:
            mean = jnp.sum(slope, axis=0, keepdims=True) * (STEPS_DEV * step / PIX)
            mean_ref[...] = jnp.broadcast_to(mean, (8, CH))
        current = current + step * tanh_out
    for row in range(3):
        for tap in range(3):
            begin = (8 - 3 * row - tap) * CH
            turned = kernel_ref[begin : begin + CH, :].astype(jnp.float32).T.astype(jnp.bfloat16)
            flipped_ref[row * CH : (row + 1) * CH, tap * CH : (tap + 1) * CH] = turned
            if row == 1 and tap == 1:
                center_ref[0:CH, :] = turned
                center_ref[CH : 2 * CH, :] = turned


def adjoint_step(buffer, flipped, low, value, step, col):
    spread(buffer, low)
    return value + step * convolve(buffer, flipped, col)


def relax_kernel(
    step, final_ref, upper_ref, terminal_ref, own_ref, slope_ref, flipped_ref, mean_ref, packed_ref, chosen_ref, buffer
):
    col = columns()
    clear_edges(buffer)
    value = jnp.where(final_ref[0] == 1, terminal_ref[...], upper_ref[...])
    chosen_ref[...] = value
    for section in range(STEPS_DEV - 1, -1, -1):
        low = (slope_ref[section] * value).astype(jnp.bfloat16)
        value = adjoint_step(buffer, flipped_ref, low, value, step, col)
    residue = value - own_ref[...]
    for part in range(ROWS):
        packed_ref[part, 0:COLS, :] = residue[part * COLS : (part + 1) * COLS]
        packed_ref[part, COLS:SLOT, :] = mean_ref[...]


def moved_by(value, mean, center):
    return exact_left(value * mean, center)


def group_kernel(packed_ref, center_ref, local_ref, maps_ref, total_ref):
    center = center_ref[...]
    row = lax.broadcasted_iota(jnp.int32, (CH, CH), 0)
    lane = lax.broadcasted_iota(jnp.int32, (CH, CH), 1)
    identity = jnp.where(row == lane, 1.0, 0.0)
    error = jnp.zeros((COLS, CH), jnp.float32)
    change = jnp.zeros((CH, CH), jnp.float32)
    for place in range(SIZE_Z - 1, -1, -1):
        local_ref[place] = error
        stack_parts(maps_ref, change, slice(place * CH, (place + 1) * CH))
        mean = packed_ref[place, COLS : COLS + 1, :]
        moved = moved_by(jnp.concatenate([error, change + identity], axis=0), mean, center)
        error = packed_ref[place, 0:COLS, :] + error + moved[0:COLS]
        change = change + moved[COLS:]
    total_ref[0:COLS, :] = error
    total_ref[COLS:, :] = change


def stack_parts(parts_ref, value, lanes):
    high, low = split(value)
    parts_ref[0:CH, lanes] = high
    parts_ref[CH : 2 * CH, lanes] = high
    parts_ref[2 * CH : 3 * CH, lanes] = low


def times(value, parts):
    high, low = split(value)
    return jnp.dot(jnp.concatenate([high, low, high], axis=1), parts, preferred_element_type=jnp.float32)


def carry_kernel(place_ref, first_ref, second_ref, third_ref, local_ref, maps_ref, after_ref, upper_ref, parts):
    place_y = place_ref[0]
    carry = jnp.where(place_y < SIZE_Y - 3, third_ref[...], 0.0)
    for distance, group_ref in ((2, second_ref), (1, first_ref)):
        stack_parts(parts.at[distance - 1], group_ref[COLS:, :], slice(0, CH))
        carry = carry + times(carry, parts[distance - 1])
        carry = carry + jnp.where(place_y < SIZE_Y - distance, group_ref[0:COLS, :], 0.0)
    moved = times(carry, maps_ref[...])
    for place in range(SIZE_Z):
        upper_ref[place] = local_ref[place] + carry + moved[:, place * CH : (place + 1) * CH]


def turn_kernel(lowered_ref, after_ref, turned_ref):
    for section in range(STEPS_DEV):
        block = lowered_ref[section].astype(jnp.float32)
        turned_ref[:, section * PIX : (section + 1) * PIX] = block.T.astype(jnp.bfloat16)


def points_kernel(own_ref, packed_ref, error_ref, mean_ref, center_ref, points_ref, mark_ref):
    mark_ref[...] = mean_ref[...]
    error = error_ref[...]
    moved = moved_by(error, mean_ref[0:1, :], center_ref[...])
    for part in range(ROWS):
        span = slice(part * COLS, (part + 1) * COLS)
        points_ref[span, :] = own_ref[span, :] + (packed_ref[part, 0:COLS, :] + error[span] + moved[span])


def second_kernel(
    step, core_ref, chosen_ref, error_ref, slope_ref, turned_ref, flipped_ref, kept_ref, sent_ref,
    buffer, grads, total, ordered,
):
    col = columns()
    clear_edges(buffer)
    value = chosen_ref[...] + error_ref[...]
    for section in range(STEPS_DEV - 1, -1, -1):
        low = (slope_ref[section] * value).astype(jnp.bfloat16)
        if section > 0:
            value = adjoint_step(buffer, flipped_ref, low, value, step, col)
        grad = low.astype(jnp.float32)
        grads[section, :, 0:CH] = from_right(grad, col).astype(jnp.bfloat16)
        grads[section, :, CH : 2 * CH] = low
        grads[section, :, 2 * CH : WIDE] = from_left(grad, col).astype(jnp.bfloat16)
        term = jnp.dot(
            turned_ref[:, section * PIX : (section + 1) * PIX], grads[section], preferred_element_type=jnp.float32
        )
        if section == STEPS_DEV - 1:
            total[...] = term
        elif section > 0:
            total[...] += term
        else:
            for row in range(3):
                for tap in range(3):
                    rows, lanes = slice(row * CH, (row + 1) * CH), slice(tap * CH, (tap + 1) * CH)
                    begin = (3 * row + tap) * CH
                    ordered[begin : begin + CH, :] = step * (total[rows, lanes] + term[rows, lanes])
    first_core = core_ref[0] == 0
    lower, upper = ordered[0:HALF, :], ordered[HALF:TAPS, :]
    kept_ref[...] = jnp.where(first_core, lower, upper)
    sent_ref[...] = jnp.where(first_core, upper, lower)


def add_kernel(left_ref, right_ref, after_ref, out_ref):
    out_ref[...] = left_ref[...] + right_ref[...]


def sum_kernel(parts_ref, out_ref):
    total = parts_ref[0:PART, :]
    for part in range(1, parts_ref.shape[0] // PART):
        total = total + parts_ref[part * PART : (part + 1) * PART, :]
    for copy in range(out_ref.shape[0] // PART):
        out_ref[copy * PART : (copy + 1) * PART, :] = total


def join_kernel(core_ref, own_ref, other_ref, out_ref, sems):
    core = core_ref[0]
    copies = [
        pltpu.make_async_copy(part, out_ref.at[pl.ds(pl.multiple_of(place * HALF, 8), HALF), :], sems.at[k])
        for k, (part, place) in enumerate(((own_ref, core), (other_ref, 1 - core)))
    ]
    for copy in copies:
        copy.start()
    for copy in copies:
        copy.wait()


def ring_down(value, axis, count, distance):
    return lax.ppermute(value, axis, [((i + distance) % count, i) for i in range(count)])


def swapped(rows, axes, count):
    parts = rows.reshape(count, 1, rows.shape[0] // count * CH)
    return lax.all_to_all(parts, axes, 0, 0).reshape(rows.shape)


def local(checkpoints, conv_weight, conv_bias, point_guess, terminal):
    slices = SIZE_Y * SIZE_Z
    step = 2.0 / (STEPS_DEV * slices)
    own = point_guess.reshape(PIX, CH)
    terminal = terminal.reshape(PIX, CH)
    kernel = conv_weight.reshape(TAPS, CH)
    place_y = lax.axis_index("y").astype(jnp.int32).reshape(1)
    final = (lax.axis_index(("y", "z")) == slices - 1).astype(jnp.int32).reshape(1)
    core = lax.axis_index("core").astype(jnp.int32).reshape(1)
    upper = ring_down(own, ("y", "z"), slices, 1)

    def bound(function):
        def kernel_of(*refs):
            function(step, *refs)

        return kernel_of

    slopes, lowered, flipped, center, mean = call(
        bound(forward_kernel),
        [f32(STEPS_DEV, PIX, CH), bf16(STEPS_DEV, PIX, WIDE), bf16(WIDE, WIDE), bf16(2 * CH, CH), f32(8, CH)],
        1.5,
        "sssvvv",
        [pltpu.VMEM((WIDE, WIDE), jnp.bfloat16)],
    )(core, place_y, final, checkpoints.reshape(PIX, CH), kernel, conv_bias.reshape(1, CH))

    wide = pltpu.VMEM((PIX, WIDE), jnp.bfloat16)
    packed, chosen = call(
        bound(relax_kernel), [f32(ROWS, SLOT, CH), f32(PIX, CH)], 1.4, "svvvvvv", [wide]
    )(final, upper, terminal, own, slopes, flipped, mean)

    gathered = lax.all_to_all(packed, "z", 0, 0)
    in_group, maps, total = call(
        group_kernel, [f32(SIZE_Z, COLS, CH), bf16(3 * CH, SIZE_Z * CH), f32(COLS + CH, CH)], 1.0
    )(gathered, center)
    first = ring_down(total, "y", SIZE_Y, 1)
    third = ring_down(total[0:COLS], "y", SIZE_Y, 3)
    second = ring_down(total, "y", SIZE_Y, 2)
    turned = call(turn_kernel, bf16(WIDE, STEPS_DEV * PIX), 0.4)(lowered, total)
    upper_error = call(
        carry_kernel, f32(SIZE_Z, COLS, CH), 1.0, "svvvvva", [pltpu.VMEM((2, 3 * CH, CH), jnp.bfloat16)]
    )(place_y, first, second, third, in_group, maps, turned)
    upper_error = lax.all_to_all(upper_error, "z", 0, 0).reshape(PIX, CH)

    kept, sent = call(
        bound(second_kernel),
        [f32(HALF, CH)] * 2,
        1.7,
        "svvvvv",
        [
            wide,
            pltpu.VMEM((STEPS_DEV, PIX, WIDE), jnp.bfloat16),
            pltpu.VMEM((WIDE, WIDE), jnp.float32),
            pltpu.VMEM((TAPS, CH), jnp.float32),
        ],
    )(core, chosen, upper_error, slopes, turned, flipped)

    received = lax.ppermute(sent, "core", [(0, 1), (1, 0)])
    points, mark = call(points_kernel, [f32(PIX, CH), f32(8, CH)], 0.8)(own, packed, upper_error, mean, center)
    half = call(add_kernel, f32(HALF, CH), 0.1, "vva")(kept, received, mark)
    parts = swapped(half, ("y", "x"), PLANE)
    copies = call(sum_kernel, f32(SIZE_Z * PART, CH), 0.1)(parts)
    parts = swapped(copies, "z", SIZE_Z)
    copies = call(sum_kernel, f32(HALF, CH), 0.1)(parts)
    half = swapped(copies, ("y", "x"), PLANE)
    other = lax.ppermute(half, "core", [(0, 1), (1, 0)])
    grad_w = pl.pallas_call(
        join_kernel,
        out_shape=f32(TAPS, CH),
        in_specs=[pl.BlockSpec(memory_space=pltpu.SMEM)] + [pl.BlockSpec(memory_space=pltpu.VMEM)] * 2,
        out_specs=pl.BlockSpec(memory_space=pl.ANY),
        scratch_shapes=[pltpu.SemaphoreType.DMA((2,))],
        compiler_params=pltpu.CompilerParams(vmem_limit_bytes=LIMIT),
    )(core, half, other)
    return points.reshape(1, 1, ROWS, COLS, CH), grad_w.reshape(3, 3, CH, CH)


def solution(mesh):
    fine = Mesh(mesh.devices.reshape(SIZE_Y, SIZE_Z, SIZE_X, 2), ("y", "z", "x", "core"))
    state = P(("y", "z"), ("x", "core"), None, None, None)
    return jax.shard_map(
        local,
        mesh=fine,
        in_specs=(state, P(), P(), state, P(("x", "core"), None, None, None)),
        out_specs=(state, P()),
        check_vma=False,
    )
```

```python
import jax
import jax.numpy as jnp
from jax import lax
from jax.experimental import pallas as pl
from jax.experimental.pallas import tpu as pltpu
from jax.sharding import Mesh, PartitionSpec as P

STEPS_DEV = 4
ROWS = 8
COLS = 32
CH = 128
PIX = ROWS * COLS
WIDE = 3 * CH
TAPS = 9 * CH
SIZE_Y = 4
SIZE_Z = 8
SIZE_X = 4
PLANE = SIZE_X * SIZE_Y
PART = 36
HALF = PLANE * PART
SLICES = SIZE_Y * SIZE_Z
SHARE = PIX // SLICES
SLOT = SHARE + 1
LIMIT = 12 << 20


def call(kernel, outs, micros, specs=None, scratch=()):
    space = pl.BlockSpec(memory_space=pltpu.VMEM)
    places = {"s": pl.BlockSpec(memory_space=pltpu.SMEM), "v": space, "a": pl.BlockSpec(memory_space=pl.ANY)}

    def run(*operands):
        kinds = specs or "v" * len(operands)
        return pl.pallas_call(
            kernel,
            out_shape=outs,
            in_specs=[places[kind] for kind in kinds],
            out_specs=[space] * len(outs) if isinstance(outs, list) else space,
            scratch_shapes=scratch,
            cost_estimate=pl.CostEstimate(
                flops=int(micros * 1e9), bytes_accessed=int(micros * 3.6e6), transcendentals=0
            ),
            compiler_params=pltpu.CompilerParams(vmem_limit_bytes=LIMIT),
        )(*operands)

    return run


def f32(*shape):
    return jax.ShapeDtypeStruct(shape, jnp.float32)


def bf16(*shape):
    return jax.ShapeDtypeStruct(shape, jnp.bfloat16)


def columns():
    return lax.broadcasted_iota(jnp.int32, (PIX, CH), 0) % COLS


def clear_edges(buffer):
    zeros = jnp.zeros((COLS, CH), jnp.bfloat16)
    buffer[0:COLS, 0:CH] = zeros
    buffer[PIX - COLS : PIX, 2 * CH : WIDE] = zeros


def spread(buffer, low):
    buffer[COLS:PIX, 0:CH] = low[0 : PIX - COLS]
    buffer[:, CH : 2 * CH] = low
    buffer[0 : PIX - COLS, 2 * CH : WIDE] = low[COLS:PIX]


def from_left(value, col):
    return jnp.where(col > 0, pltpu.roll(value, 1, 0), 0.0)


def from_right(value, col):
    return jnp.where(col < COLS - 1, pltpu.roll(value, PIX - 1, 0), 0.0)


def convolve(buffer, kernel, col):
    taps = jnp.dot(buffer[...], kernel[...], preferred_element_type=jnp.float32)
    sides = from_left(taps[:, 0:CH], col) + from_right(taps[:, 2 * CH : WIDE], col)
    return taps[:, CH : 2 * CH] + sides


def split(value):
    high = value.astype(jnp.bfloat16)
    return high, (value - high.astype(jnp.float32)).astype(jnp.bfloat16)


def exact_left(value, weight_twice):
    return jnp.dot(
        jnp.concatenate(split(value), axis=1), weight_twice, preferred_element_type=jnp.float32
    )


def forward_kernel(
    step, core_ref, final_ref, start_ref, kernel_ref, bias_ref, slope_ref, turned_ref, flipped_ref,
    center_ref, mean_ref, weights, lowered,
):
    col = columns()
    bias = bias_ref[...]
    for row in range(3):
        for tap in range(3):
            begin = (3 * row + tap) * CH
            weights[row * CH : (row + 1) * CH, tap * CH : (tap + 1) * CH] = kernel_ref[begin : begin + CH, :]
    current = start_ref[...].astype(jnp.float32)
    for section in range(STEPS_DEV):
        buffer = lowered.at[section]
        clear_edges(buffer)
        spread(buffer, current.astype(jnp.bfloat16))
        tanh_out = jnp.tanh(convolve(buffer, weights, col) + bias)
        slope = 1.0 - tanh_out * tanh_out
        slope_ref[section] = slope
        if section == 0:
            mean = jnp.sum(slope, axis=0, keepdims=True) * (STEPS_DEV * step / PIX)
            mean_ref[...] = jnp.broadcast_to(mean, (8, CH))
        current = current + step * tanh_out
    for section in range(STEPS_DEV):
        block = lowered[section].astype(jnp.float32)
        turned_ref[:, section * PIX : (section + 1) * PIX] = block.T.astype(jnp.bfloat16)
    for row in range(3):
        for tap in range(3):
            begin = (8 - 3 * row - tap) * CH
            turned = kernel_ref[begin : begin + CH, :].astype(jnp.float32).T.astype(jnp.bfloat16)
            flipped_ref[row * CH : (row + 1) * CH, tap * CH : (tap + 1) * CH] = turned
            if row == 1 and tap == 1:
                center_ref[0:CH, :] = turned
                center_ref[CH : 2 * CH, :] = turned


def adjoint_step(buffer, flipped, low, value, step, col):
    spread(buffer, low)
    return value + step * convolve(buffer, flipped, col)


def relax_kernel(
    step, final_ref, upper_ref, terminal_ref, own_ref, slope_ref, flipped_ref, mean_ref, packed_ref, residue_ref, chosen_ref, buffer
):
    col = columns()
    clear_edges(buffer)
    value = jnp.where(final_ref[0] == 1, terminal_ref[...], upper_ref[...])
    chosen_ref[...] = value
    for section in range(STEPS_DEV - 1, -1, -1):
        low = (slope_ref[section] * value).astype(jnp.bfloat16)
        value = adjoint_step(buffer, flipped_ref, low, value, step, col)
    residue = value - own_ref[...]
    residue_ref[...] = residue
    mean = mean_ref[0:1, :]
    for part in range(SLICES):
        packed_ref[part * SLOT : part * SLOT + SHARE, :] = residue[part * SHARE : (part + 1) * SHARE]
        packed_ref[part * SLOT + SHARE : (part + 1) * SLOT, :] = mean


def moved_by(value, mean, center):
    return exact_left(value * mean, center)


def stack_parts(parts_ref, value, lanes):
    high, low = split(value)
    parts_ref[0:CH, lanes] = high
    parts_ref[CH : 2 * CH, lanes] = high
    parts_ref[2 * CH : 3 * CH, lanes] = low


def times(value, parts):
    high, low = split(value)
    return jnp.dot(jnp.concatenate([high, low, high], axis=1), parts, preferred_element_type=jnp.float32)


def scan_kernel(packed_ref, center_ref, upper_ref, parts):
    center = center_ref[...]
    row = lax.broadcasted_iota(jnp.int32, (CH, CH), 0)
    lane = lax.broadcasted_iota(jnp.int32, (CH, CH), 1)
    identity = jnp.where(row == lane, 1.0, 0.0)
    middle = range(1, SIZE_Y - 1)

    def residues(place):
        begins = [(group * SIZE_Z + place) * SLOT for group in range(SIZE_Y)]
        return jnp.concatenate([packed_ref[begin : begin + SHARE, :] for begin in begins], axis=0)

    def mean(group, place):
        begin = (group * SIZE_Z + place) * SLOT + SHARE
        return packed_ref[begin : begin + 1, :]

    def scaled(errors, place):
        return [
            errors[group * SHARE : (group + 1) * SHARE] * mean(group, place) for group in range(SIZE_Y)
        ]

    split_at = SIZE_Y * SHARE
    errors = jnp.zeros((split_at, CH), jnp.float32)
    changes = jnp.zeros((len(middle) * CH, CH), jnp.float32)
    for place in range(SIZE_Z - 1, -1, -1):
        rows = scaled(errors, place)
        for k, group in enumerate(middle):
            rows.append((changes[k * CH : (k + 1) * CH] + identity) * mean(group, place))
        moved = exact_left(jnp.concatenate(rows, axis=0), center)
        errors = residues(place) + errors + moved[0:split_at]
        changes = changes + moved[split_at:]
    carry = jnp.zeros((SHARE, CH), jnp.float32)
    carries = [carry]
    for group in range(SIZE_Y - 1, 0, -1):
        if group in middle:
            stack_parts(parts.at[group - 1], changes[(group - 1) * CH : group * CH], slice(0, CH))
            carry = carry + times(carry, parts[group - 1])
        carry = carry + errors[group * SHARE : (group + 1) * SHARE]
        carries.insert(0, carry)
    errors = jnp.concatenate(carries, axis=0)
    for place in range(SIZE_Z - 1, -1, -1):
        for group in range(SIZE_Y):
            begin = (group * SIZE_Z + place) * SHARE
            upper_ref[begin : begin + SHARE, :] = errors[group * SHARE : (group + 1) * SHARE]
        if place > 0:
            moved = exact_left(jnp.concatenate(scaled(errors, place), axis=0), center)
            errors = residues(place) + errors + moved


def points_kernel(own_ref, residue_ref, error_ref, mean_ref, center_ref, points_ref, mark_ref):
    mark_ref[...] = mean_ref[...]
    error = error_ref[...]
    moved = moved_by(error, mean_ref[0:1, :], center_ref[...])
    points_ref[...] = own_ref[...] + (residue_ref[...] + error + moved)


def second_kernel(
    step, core_ref, chosen_ref, error_ref, slope_ref, turned_ref, flipped_ref, kept_ref, sent_ref,
    buffer, grads, total, ordered,
):
    col = columns()
    clear_edges(buffer)
    value = chosen_ref[...] + error_ref[...]
    for section in range(STEPS_DEV - 1, -1, -1):
        low = (slope_ref[section] * value).astype(jnp.bfloat16)
        if section > 0:
            value = adjoint_step(buffer, flipped_ref, low, value, step, col)
        grad = low.astype(jnp.float32)
        grads[section, :, 0:CH] = from_right(grad, col).astype(jnp.bfloat16)
        grads[section, :, CH : 2 * CH] = low
        grads[section, :, 2 * CH : WIDE] = from_left(grad, col).astype(jnp.bfloat16)
        term = jnp.dot(
            turned_ref[:, section * PIX : (section + 1) * PIX], grads[section], preferred_element_type=jnp.float32
        )
        if section == STEPS_DEV - 1:
            total[...] = term
        elif section > 0:
            total[...] += term
        else:
            for row in range(3):
                for tap in range(3):
                    rows, lanes = slice(row * CH, (row + 1) * CH), slice(tap * CH, (tap + 1) * CH)
                    begin = (3 * row + tap) * CH
                    ordered[begin : begin + CH, :] = step * (total[rows, lanes] + term[rows, lanes])
    first_core = core_ref[0] == 0
    lower, upper = ordered[0:HALF, :], ordered[HALF:TAPS, :]
    kept_ref[...] = jnp.where(first_core, lower, upper)
    sent_ref[...] = jnp.where(first_core, upper, lower)


def add_kernel(left_ref, right_ref, after_ref, out_ref):
    out_ref[...] = left_ref[...] + right_ref[...]


def sum_kernel(parts_ref, out_ref):
    total = parts_ref[0:PART, :]
    for part in range(1, parts_ref.shape[0] // PART):
        total = total + parts_ref[part * PART : (part + 1) * PART, :]
    for copy in range(out_ref.shape[0] // PART):
        out_ref[copy * PART : (copy + 1) * PART, :] = total


def join_kernel(core_ref, own_ref, other_ref, out_ref, sems):
    core = core_ref[0]
    copies = [
        pltpu.make_async_copy(part, out_ref.at[pl.ds(pl.multiple_of(place * HALF, 8), HALF), :], sems.at[k])
        for k, (part, place) in enumerate(((own_ref, core), (other_ref, 1 - core)))
    ]
    for copy in copies:
        copy.start()
    for copy in copies:
        copy.wait()


def ring_down(value, axis, count, distance):
    return lax.ppermute(value, axis, [((i + distance) % count, i) for i in range(count)])


def swapped(rows, axes, count):
    parts = rows.reshape(count, 1, rows.shape[0] // count * CH)
    return lax.all_to_all(parts, axes, 0, 0).reshape(rows.shape)


def local(checkpoints, conv_weight, conv_bias, point_guess, terminal):
    step = 2.0 / (STEPS_DEV * SLICES)
    own = point_guess.reshape(PIX, CH)
    terminal = terminal.reshape(PIX, CH)
    kernel = conv_weight.reshape(TAPS, CH)
    final = (lax.axis_index(("y", "z")) == SLICES - 1).astype(jnp.int32).reshape(1)
    core = lax.axis_index("core").astype(jnp.int32).reshape(1)
    upper = ring_down(own, ("y", "z"), SLICES, 1)

    def bound(function):
        def kernel_of(*refs):
            function(step, *refs)

        return kernel_of

    slopes, turned, flipped, center, mean = call(
        bound(forward_kernel),
        [f32(STEPS_DEV, PIX, CH), bf16(WIDE, STEPS_DEV * PIX), bf16(WIDE, WIDE), bf16(2 * CH, CH), f32(8, CH)],
        1.5,
        "ssvvv",
        [pltpu.VMEM((WIDE, WIDE), jnp.bfloat16), pltpu.VMEM((STEPS_DEV, PIX, WIDE), jnp.bfloat16)],
    )(core, final, checkpoints.reshape(PIX, CH), kernel, conv_bias.reshape(1, CH))

    wide = pltpu.VMEM((PIX, WIDE), jnp.bfloat16)
    packed, residue, chosen = call(
        bound(relax_kernel),
        [f32(SLICES * SLOT, CH), f32(PIX, CH), f32(PIX, CH)],
        1.2,
        "svvvvvv",
        [wide],
    )(final, upper, terminal, own, slopes, flipped, mean)

    gathered = swapped(packed, ("y", "z"), SLICES)
    errors = call(
        scan_kernel, f32(PIX, CH), 2.5, scratch=[pltpu.VMEM((SIZE_Y - 2, 3 * CH, CH), jnp.bfloat16)]
    )(gathered, center)
    upper_error = swapped(errors, ("y", "z"), SLICES)

    kept, sent = call(
        bound(second_kernel),
        [f32(HALF, CH)] * 2,
        1.7,
        "svvvvv",
        [
            wide,
            pltpu.VMEM((STEPS_DEV, PIX, WIDE), jnp.bfloat16),
            pltpu.VMEM((WIDE, WIDE), jnp.float32),
            pltpu.VMEM((TAPS, CH), jnp.float32),
        ],
    )(core, chosen, upper_error, slopes, turned, flipped)

    received = lax.ppermute(sent, "core", [(0, 1), (1, 0)])
    points, mark = call(points_kernel, [f32(PIX, CH), f32(8, CH)], 0.8)(own, residue, upper_error, mean, center)
    half = call(add_kernel, f32(HALF, CH), 0.1, "vva")(kept, received, mark)
    parts = swapped(half, ("y", "x"), PLANE)
    copies = call(sum_kernel, f32(SIZE_Z * PART, CH), 0.1)(parts)
    parts = swapped(copies, "z", SIZE_Z)
    copies = call(sum_kernel, f32(HALF, CH), 0.1)(parts)
    half = swapped(copies, ("y", "x"), PLANE)
    other = lax.ppermute(half, "core", [(0, 1), (1, 0)])
    grad_w = pl.pallas_call(
        join_kernel,
        out_shape=f32(TAPS, CH),
        in_specs=[pl.BlockSpec(memory_space=pltpu.SMEM)] + [pl.BlockSpec(memory_space=pltpu.VMEM)] * 2,
        out_specs=pl.BlockSpec(memory_space=pl.ANY),
        scratch_shapes=[pltpu.SemaphoreType.DMA((2,))],
        compiler_params=pltpu.CompilerParams(vmem_limit_bytes=LIMIT),
    )(core, half, other)
    return points.reshape(1, 1, ROWS, COLS, CH), grad_w.reshape(3, 3, CH, CH)


def solution(mesh):
    fine = Mesh(mesh.devices.reshape(SIZE_Y, SIZE_Z, SIZE_X, 2), ("y", "z", "x", "core"))
    state = P(("y", "z"), ("x", "core"), None, None, None)
    return jax.shard_map(
        local,
        mesh=fine,
        in_specs=(state, P(), P(), state, P(("x", "core"), None, None, None)),
        out_specs=(state, P()),
        check_vma=False,
    )
```

```python
import jax
import jax.numpy as jnp
from jax import lax
from jax.experimental import pallas as pl
from jax.experimental.pallas import tpu as pltpu
from jax.sharding import Mesh, PartitionSpec as P

STEPS_DEV = 4
ROWS = 8
COLS = 32
CH = 128
PIX = ROWS * COLS
WIDE = 3 * CH
TAPS = 9 * CH
SIZE_Y = 4
SIZE_Z = 8
SIZE_X = 4
PLANE = SIZE_X * SIZE_Y
PART = 36
HALF = PLANE * PART
SLICES = SIZE_Y * SIZE_Z
SHARE = PIX // SLICES
SLOT = SHARE + 1
LIMIT = 12 << 20


def call(kernel, outs, micros, specs=None, scratch=()):
    space = pl.BlockSpec(memory_space=pltpu.VMEM)
    places = {"s": pl.BlockSpec(memory_space=pltpu.SMEM), "v": space, "a": pl.BlockSpec(memory_space=pl.ANY)}

    def run(*operands):
        kinds = specs or "v" * len(operands)
        return pl.pallas_call(
            kernel,
            out_shape=outs,
            in_specs=[places[kind] for kind in kinds],
            out_specs=[space] * len(outs) if isinstance(outs, list) else space,
            scratch_shapes=scratch,
            cost_estimate=pl.CostEstimate(
                flops=int(micros * 1e9), bytes_accessed=int(micros * 3.6e6), transcendentals=0
            ),
            compiler_params=pltpu.CompilerParams(vmem_limit_bytes=LIMIT),
        )(*operands)

    return run


def f32(*shape):
    return jax.ShapeDtypeStruct(shape, jnp.float32)


def bf16(*shape):
    return jax.ShapeDtypeStruct(shape, jnp.bfloat16)


def columns():
    return lax.broadcasted_iota(jnp.int32, (PIX, CH), 0) % COLS


def clear_edges(buffer):
    zeros = jnp.zeros((COLS, CH), jnp.bfloat16)
    buffer[0:COLS, 0:CH] = zeros
    buffer[PIX - COLS : PIX, 2 * CH : WIDE] = zeros


def spread(buffer, low):
    buffer[COLS:PIX, 0:CH] = low[0 : PIX - COLS]
    buffer[:, CH : 2 * CH] = low
    buffer[0 : PIX - COLS, 2 * CH : WIDE] = low[COLS:PIX]


def from_left(value, col):
    return jnp.where(col > 0, pltpu.roll(value, 1, 0), 0.0)


def from_right(value, col):
    return jnp.where(col < COLS - 1, pltpu.roll(value, PIX - 1, 0), 0.0)


def convolve(buffer, kernel, col):
    taps = jnp.dot(buffer[...], kernel[...], preferred_element_type=jnp.float32)
    sides = from_left(taps[:, 0:CH], col) + from_right(taps[:, 2 * CH : WIDE], col)
    return taps[:, CH : 2 * CH] + sides


def split(value):
    high = value.astype(jnp.bfloat16)
    return high, (value - high.astype(jnp.float32)).astype(jnp.bfloat16)


def exact_left(value, weight_twice):
    return jnp.dot(
        jnp.concatenate(split(value), axis=1), weight_twice, preferred_element_type=jnp.float32
    )


def first_kernel(core_ref, final_ref, mark_ref):
    mark_ref[...] = jnp.zeros_like(mark_ref)


def forward_kernel(
    step, mark_ref, start_ref, kernel_ref, bias_ref, slope_ref, turned_ref, flipped_ref,
    center_ref, mean_ref, weights, lowered,
):
    col = columns()
    bias = bias_ref[...]
    for row in range(3):
        for tap in range(3):
            begin = (3 * row + tap) * CH
            weights[row * CH : (row + 1) * CH, tap * CH : (tap + 1) * CH] = kernel_ref[begin : begin + CH, :]
    current = start_ref[...].astype(jnp.float32)
    for section in range(STEPS_DEV):
        buffer = lowered.at[section]
        clear_edges(buffer)
        spread(buffer, current.astype(jnp.bfloat16))
        tanh_out = jnp.tanh(convolve(buffer, weights, col) + bias)
        slope = 1.0 - tanh_out * tanh_out
        slope_ref[section] = slope
        if section == 0:
            mean = jnp.sum(slope, axis=0, keepdims=True) * (STEPS_DEV * step / PIX)
            mean_ref[...] = jnp.broadcast_to(mean, (8, CH))
        current = current + step * tanh_out
    for section in range(STEPS_DEV):
        block = lowered[section].astype(jnp.float32)
        turned_ref[:, section * PIX : (section + 1) * PIX] = block.T.astype(jnp.bfloat16)
    for row in range(3):
        for tap in range(3):
            begin = (8 - 3 * row - tap) * CH
            turned = kernel_ref[begin : begin + CH, :].astype(jnp.float32).T.astype(jnp.bfloat16)
            flipped_ref[row * CH : (row + 1) * CH, tap * CH : (tap + 1) * CH] = turned
            if row == 1 and tap == 1:
                center_ref[0:CH, :] = turned
                center_ref[CH : 2 * CH, :] = turned


def adjoint_step(buffer, flipped, low, value, step, col):
    spread(buffer, low)
    return value + step * convolve(buffer, flipped, col)


def relax_kernel(
    step, final_ref, upper_ref, terminal_ref, own_ref, slope_ref, flipped_ref, mean_ref, packed_ref, residue_ref, chosen_ref, buffer
):
    col = columns()
    clear_edges(buffer)
    value = jnp.where(final_ref[0] == 1, terminal_ref[...], upper_ref[...])
    chosen_ref[...] = value
    for section in range(STEPS_DEV - 1, -1, -1):
        low = (slope_ref[section] * value).astype(jnp.bfloat16)
        value = adjoint_step(buffer, flipped_ref, low, value, step, col)
    residue = value - own_ref[...]
    residue_ref[...] = residue
    mean = mean_ref[0:1, :]
    for part in range(SLICES):
        packed_ref[part * SLOT : part * SLOT + SHARE, :] = residue[part * SHARE : (part + 1) * SHARE]
        packed_ref[part * SLOT + SHARE : (part + 1) * SLOT, :] = mean


def moved_by(value, mean, center):
    return exact_left(value * mean, center)


def stack_parts(parts_ref, value, lanes):
    high, low = split(value)
    parts_ref[0:CH, lanes] = high
    parts_ref[CH : 2 * CH, lanes] = high
    parts_ref[2 * CH : 3 * CH, lanes] = low


def times(value, parts):
    high, low = split(value)
    return jnp.dot(jnp.concatenate([high, low, high], axis=1), parts, preferred_element_type=jnp.float32)


def scan_kernel(packed_ref, center_ref, upper_ref, parts):
    center = center_ref[...]
    row = lax.broadcasted_iota(jnp.int32, (CH, CH), 0)
    lane = lax.broadcasted_iota(jnp.int32, (CH, CH), 1)
    identity = jnp.where(row == lane, 1.0, 0.0)
    middle = range(1, SIZE_Y - 1)

    def residues(place):
        begins = [(group * SIZE_Z + place) * SLOT for group in range(SIZE_Y)]
        return jnp.concatenate([packed_ref[begin : begin + SHARE, :] for begin in begins], axis=0)

    def mean(group, place):
        begin = (group * SIZE_Z + place) * SLOT + SHARE
        return packed_ref[begin : begin + 1, :]

    def scaled(errors, place):
        return [
            errors[group * SHARE : (group + 1) * SHARE] * mean(group, place) for group in range(SIZE_Y)
        ]

    split_at = SIZE_Y * SHARE
    errors = jnp.zeros((split_at, CH), jnp.float32)
    changes = jnp.zeros((len(middle) * CH, CH), jnp.float32)
    for place in range(SIZE_Z - 1, -1, -1):
        rows = scaled(errors, place)
        for k, group in enumerate(middle):
            rows.append((changes[k * CH : (k + 1) * CH] + identity) * mean(group, place))
        moved = exact_left(jnp.concatenate(rows, axis=0), center)
        errors = residues(place) + errors + moved[0:split_at]
        changes = changes + moved[split_at:]
    carry = jnp.zeros((SHARE, CH), jnp.float32)
    carries = [carry]
    for group in range(SIZE_Y - 1, 0, -1):
        if group in middle:
            stack_parts(parts.at[group - 1], changes[(group - 1) * CH : group * CH], slice(0, CH))
            carry = carry + times(carry, parts[group - 1])
        carry = carry + errors[group * SHARE : (group + 1) * SHARE]
        carries.insert(0, carry)
    errors = jnp.concatenate(carries, axis=0)
    for place in range(SIZE_Z - 1, -1, -1):
        for group in range(SIZE_Y):
            begin = (group * SIZE_Z + place) * SHARE
            upper_ref[begin : begin + SHARE, :] = errors[group * SHARE : (group + 1) * SHARE]
        if place > 0:
            moved = exact_left(jnp.concatenate(scaled(errors, place), axis=0), center)
            errors = residues(place) + errors + moved


def points_kernel(own_ref, residue_ref, error_ref, mean_ref, center_ref, points_ref, mark_ref):
    mark_ref[...] = mean_ref[...]
    error = error_ref[...]
    moved = moved_by(error, mean_ref[0:1, :], center_ref[...])
    points_ref[...] = own_ref[...] + (residue_ref[...] + error + moved)


def second_kernel(
    step, core_ref, chosen_ref, error_ref, slope_ref, turned_ref, flipped_ref, kept_ref, sent_ref,
    buffer, grads, total, ordered,
):
    col = columns()
    clear_edges(buffer)
    value = chosen_ref[...] + error_ref[...]
    for section in range(STEPS_DEV - 1, -1, -1):
        low = (slope_ref[section] * value).astype(jnp.bfloat16)
        if section > 0:
            value = adjoint_step(buffer, flipped_ref, low, value, step, col)
        grad = low.astype(jnp.float32)
        grads[section, :, 0:CH] = from_right(grad, col).astype(jnp.bfloat16)
        grads[section, :, CH : 2 * CH] = low
        grads[section, :, 2 * CH : WIDE] = from_left(grad, col).astype(jnp.bfloat16)
        term = jnp.dot(
            turned_ref[:, section * PIX : (section + 1) * PIX], grads[section], preferred_element_type=jnp.float32
        )
        if section == STEPS_DEV - 1:
            total[...] = term
        elif section > 0:
            total[...] += term
        else:
            for row in range(3):
                for tap in range(3):
                    rows, lanes = slice(row * CH, (row + 1) * CH), slice(tap * CH, (tap + 1) * CH)
                    begin = (3 * row + tap) * CH
                    ordered[begin : begin + CH, :] = step * (total[rows, lanes] + term[rows, lanes])
    first_core = core_ref[0] == 0
    lower, upper = ordered[0:HALF, :], ordered[HALF:TAPS, :]
    kept_ref[...] = jnp.where(first_core, lower, upper)
    sent_ref[...] = jnp.where(first_core, upper, lower)


def add_kernel(left_ref, right_ref, after_ref, out_ref):
    out_ref[...] = left_ref[...] + right_ref[...]


def sum_kernel(parts_ref, out_ref):
    total = parts_ref[0:PART, :]
    for part in range(1, parts_ref.shape[0] // PART):
        total = total + parts_ref[part * PART : (part + 1) * PART, :]
    for copy in range(out_ref.shape[0] // PART):
        out_ref[copy * PART : (copy + 1) * PART, :] = total


def place_kernel(other, core_ref, half_ref, *refs):
    out_ref, sem = refs[-2:]
    place = 1 - core_ref[0] if other else core_ref[0]
    copy = pltpu.make_async_copy(half_ref, out_ref.at[pl.ds(pl.multiple_of(place * HALF, 8), HALF), :], sem)
    copy.start()
    copy.wait()


def placed(other, core, half, so_far=()):
    anywhere = pl.BlockSpec(memory_space=pl.ANY)

    def kernel_of(*refs):
        place_kernel(other, *refs)

    return pl.pallas_call(
        kernel_of,
        out_shape=f32(TAPS, CH),
        in_specs=[pl.BlockSpec(memory_space=pltpu.SMEM), pl.BlockSpec(memory_space=pltpu.VMEM)]
        + [anywhere] * len(so_far),
        out_specs=anywhere,
        scratch_shapes=[pltpu.SemaphoreType.DMA],
        input_output_aliases={2: 0} if so_far else {},
        cost_estimate=pl.CostEstimate(flops=0, bytes_accessed=8 * HALF * CH, transcendentals=0),
        compiler_params=pltpu.CompilerParams(vmem_limit_bytes=LIMIT),
    )(core, half, *so_far)


def ring_down(value, axis, count, distance):
    return lax.ppermute(value, axis, [((i + distance) % count, i) for i in range(count)])


def swapped(rows, axes, count):
    parts = rows.reshape(count, 1, rows.shape[0] // count * CH)
    return lax.all_to_all(parts, axes, 0, 0).reshape(rows.shape)


def local(checkpoints, conv_weight, conv_bias, point_guess, terminal):
    step = 2.0 / (STEPS_DEV * SLICES)
    own = point_guess.reshape(PIX, CH)
    terminal = terminal.reshape(PIX, CH)
    kernel = conv_weight.reshape(TAPS, CH)
    final = (lax.axis_index(("y", "z")) == SLICES - 1).astype(jnp.int32).reshape(1)
    core = lax.axis_index("core").astype(jnp.int32).reshape(1)
    upper = ring_down(own, ("y", "z"), SLICES, 1)

    def bound(function):
        def kernel_of(*refs):
            function(step, *refs)

        return kernel_of

    mark = call(first_kernel, f32(8, CH), 3.0, "ss")(core, final)
    slopes, turned, flipped, center, mean = call(
        bound(forward_kernel),
        [f32(STEPS_DEV, PIX, CH), bf16(WIDE, STEPS_DEV * PIX), bf16(WIDE, WIDE), bf16(2 * CH, CH), f32(8, CH)],
        1.5,
        "vvvv",
        [pltpu.VMEM((WIDE, WIDE), jnp.bfloat16), pltpu.VMEM((STEPS_DEV, PIX, WIDE), jnp.bfloat16)],
    )(mark, checkpoints.reshape(PIX, CH), kernel, conv_bias.reshape(1, CH))

    wide = pltpu.VMEM((PIX, WIDE), jnp.bfloat16)
    packed, residue, chosen = call(
        bound(relax_kernel),
        [f32(SLICES * SLOT, CH), f32(PIX, CH), f32(PIX, CH)],
        1.2,
        "svvvvvv",
        [wide],
    )(final, upper, terminal, own, slopes, flipped, mean)

    gathered = swapped(packed, ("y", "z"), SLICES)
    errors = call(
        scan_kernel, f32(PIX, CH), 2.5, scratch=[pltpu.VMEM((SIZE_Y - 2, 3 * CH, CH), jnp.bfloat16)]
    )(gathered, center)
    upper_error = swapped(errors, ("y", "z"), SLICES)

    kept, sent = call(
        bound(second_kernel),
        [f32(HALF, CH)] * 2,
        1.7,
        "svvvvv",
        [
            wide,
            pltpu.VMEM((STEPS_DEV, PIX, WIDE), jnp.bfloat16),
            pltpu.VMEM((WIDE, WIDE), jnp.float32),
            pltpu.VMEM((TAPS, CH), jnp.float32),
        ],
    )(core, chosen, upper_error, slopes, turned, flipped)

    received = lax.ppermute(sent, "core", [(0, 1), (1, 0)])
    points, points_mark = call(points_kernel, [f32(PIX, CH), f32(8, CH)], 0.8)(own, residue, upper_error, mean, center)
    half = call(add_kernel, f32(HALF, CH), 0.1, "vva")(kept, received, points_mark)
    parts = swapped(half, ("y", "x"), PLANE)
    copies = call(sum_kernel, f32(SIZE_Z * PART, CH), 0.1)(parts)
    parts = swapped(copies, "z", SIZE_Z)
    copies = call(sum_kernel, f32(HALF, CH), 0.1)(parts)
    half = swapped(copies, ("y", "x"), PLANE)
    other = lax.ppermute(half, "core", [(0, 1), (1, 0)])
    grad_w = placed(True, core, other, [placed(False, core, half)])
    return points.reshape(1, 1, ROWS, COLS, CH), grad_w.reshape(3, 3, CH, CH)


def solution(mesh):
    fine = Mesh(mesh.devices.reshape(SIZE_Y, SIZE_Z, SIZE_X, 2), ("y", "z", "x", "core"))
    state = P(("y", "z"), ("x", "core"), None, None, None)
    return jax.shard_map(
        local,
        mesh=fine,
        in_specs=(state, P(), P(), state, P(("x", "core"), None, None, None)),
        out_specs=(state, P()),
        check_vma=False,
    )
```

```python
import jax
import jax.numpy as jnp
from jax import lax
from jax.experimental import pallas as pl
from jax.experimental.pallas import tpu as pltpu
from jax.sharding import Mesh, PartitionSpec as P

STEPS_DEV = 4
ROWS = 8
COLS = 32
CH = 128
PIX = ROWS * COLS
WIDE = 3 * CH
PIECE = 64
LENGTH = 4
TAPS = 9 * CH
SIZE_Y = 4
SIZE_Z = 8
SIZE_X = 4
PLANE = SIZE_X * SIZE_Y
PART = 36
HALF = PLANE * PART
SLICES = SIZE_Y * SIZE_Z
SHARE = PIX // SLICES
SLOT = SHARE + 1
LIMIT = 12 << 20


def call(kernel, outs, micros, specs=None, scratch=()):
    space = pl.BlockSpec(memory_space=pltpu.VMEM)
    places = {"s": pl.BlockSpec(memory_space=pltpu.SMEM), "v": space, "a": pl.BlockSpec(memory_space=pl.ANY)}

    def run(*operands):
        kinds = specs or "v" * len(operands)
        return pl.pallas_call(
            kernel,
            out_shape=outs,
            in_specs=[places[kind] for kind in kinds],
            out_specs=[space] * len(outs) if isinstance(outs, list) else space,
            scratch_shapes=scratch,
            cost_estimate=pl.CostEstimate(
                flops=int(micros * 1e9), bytes_accessed=int(micros * 3.6e6), transcendentals=0
            ),
            compiler_params=pltpu.CompilerParams(vmem_limit_bytes=LIMIT),
        )(*operands)

    return run


def f32(*shape):
    return jax.ShapeDtypeStruct(shape, jnp.float32)


def bf16(*shape):
    return jax.ShapeDtypeStruct(shape, jnp.bfloat16)


def columns(count):
    return lax.broadcasted_iota(jnp.int32, (count, CH), 0) % COLS


def clear_edges(buffer):
    zeros = jnp.zeros((COLS, CH), jnp.bfloat16)
    buffer[0:COLS, 0:CH] = zeros
    buffer[PIX - COLS : PIX, 2 * CH : WIDE] = zeros


def spread(buffer, low):
    buffer[COLS:PIX, 0:CH] = low[0 : PIX - COLS]
    buffer[:, CH : 2 * CH] = low
    buffer[0 : PIX - COLS, 2 * CH : WIDE] = low[COLS:PIX]


def from_left(value, col):
    return jnp.where(col > 0, pltpu.roll(value, 1, 0), 0.0)


def from_right(value, col):
    return jnp.where(col < COLS - 1, pltpu.roll(value, value.shape[0] - 1, 0), 0.0)


def convolve(buffer, kernel, col):
    taps = jnp.dot(buffer, kernel[...], preferred_element_type=jnp.float32)
    sides = from_left(taps[:, 0:CH], col) + from_right(taps[:, 2 * CH : WIDE], col)
    return taps[:, CH : 2 * CH] + sides


def spread_piece(buffer, low, begin):
    end = begin + PIECE
    below, above = min(PIX, end + COLS), max(0, begin - COLS)
    buffer[begin + COLS : below, 0:CH] = low[0 : below - begin - COLS]
    buffer[begin:end, CH : 2 * CH] = low
    buffer[above : end - COLS, 2 * CH : WIDE] = low[above + COLS - begin : PIECE]


def pieces(ref, *lead):
    return [ref[(*lead, slice(begin, begin + PIECE))] for begin in range(0, PIX, PIECE)]


def split(value):
    high = value.astype(jnp.bfloat16)
    return high, (value - high.astype(jnp.float32)).astype(jnp.bfloat16)


def exact_left(value, weight_twice):
    return jnp.dot(
        jnp.concatenate(split(value), axis=1), weight_twice, preferred_element_type=jnp.float32
    )


def first_kernel(core_ref, final_ref, mark_ref):
    mark_ref[...] = jnp.zeros_like(mark_ref)


def forward_kernel(
    step, mark_ref, start_ref, kernel_ref, bias_ref, slope_ref, turned_ref, flipped_ref,
    center_ref, mean_ref, weights, lowered,
):
    col = columns(PIX)
    bias = bias_ref[...]
    for row in range(3):
        for tap in range(3):
            begin = (3 * row + tap) * CH
            weights[row * CH : (row + 1) * CH, tap * CH : (tap + 1) * CH] = kernel_ref[begin : begin + CH, :]
    current = start_ref[...].astype(jnp.float32)
    for section in range(STEPS_DEV):
        buffer = lowered.at[section]
        clear_edges(buffer)
        spread(buffer, current.astype(jnp.bfloat16))
        tanh_out = jnp.tanh(convolve(buffer[...], weights, col) + bias)
        slope = 1.0 - tanh_out * tanh_out
        slope_ref[section] = slope
        if section == 0:
            mean = jnp.sum(slope, axis=0, keepdims=True) * (STEPS_DEV * step / PIX)
            mean_ref[...] = jnp.broadcast_to(mean, (8, CH))
        current = current + step * tanh_out
    for section in range(STEPS_DEV):
        block = lowered[section].astype(jnp.float32)
        turned_ref[:, section * PIX : (section + 1) * PIX] = block.T.astype(jnp.bfloat16)
    for row in range(3):
        for tap in range(3):
            begin = (8 - 3 * row - tap) * CH
            turned = kernel_ref[begin : begin + CH, :].astype(jnp.float32).T.astype(jnp.bfloat16)
            flipped_ref[row * CH : (row + 1) * CH, tap * CH : (tap + 1) * CH] = turned
            if row == 1 and tap == 1:
                center_ref[0:CH, :] = turned
                center_ref[CH : 2 * CH, :] = turned


def adjoint_step(buffer, flipped, lows, values, step, col):
    for k, low in enumerate(lows):
        spread_piece(buffer, low, k * PIECE)
    return [
        value + step * convolve(buffer[k * PIECE : (k + 1) * PIECE, :], flipped, col)
        for k, value in enumerate(values)
    ]


def lowered_grads(slope_ref, section, values):
    return [(slope * value).astype(jnp.bfloat16) for slope, value in zip(pieces(slope_ref, section), values)]


def relax_kernel(
    step, final_ref, upper_ref, terminal_ref, own_ref, slope_ref, flipped_ref, mean_ref,
    packed_ref, residue_ref, chosen_ref, buffer,
):
    col = columns(PIECE)
    clear_edges(buffer)
    final = final_ref[0] == 1
    values = [jnp.where(final, last, upper) for last, upper in zip(pieces(terminal_ref), pieces(upper_ref))]
    for k, value in enumerate(values):
        chosen_ref[k * PIECE : (k + 1) * PIECE, :] = value
    for section in range(STEPS_DEV - 1, -1, -1):
        lows = lowered_grads(slope_ref, section, values)
        values = adjoint_step(buffer, flipped_ref, lows, values, step, col)
    mean = mean_ref[0:1, :]
    for k, (value, own) in enumerate(zip(values, pieces(own_ref))):
        residue = value - own
        residue_ref[k * PIECE : (k + 1) * PIECE, :] = residue
        for share in range(PIECE // SHARE):
            begin = (k * (PIECE // SHARE) + share) * SLOT
            packed_ref[begin : begin + SHARE, :] = residue[share * SHARE : (share + 1) * SHARE]
            packed_ref[begin + SHARE : begin + SLOT, :] = mean


def moved_by(value, mean, center):
    return exact_left(value * mean, center)


def stack_parts(parts_ref, value, lanes):
    high, low = split(value)
    parts_ref[0:CH, lanes] = high
    parts_ref[CH : 2 * CH, lanes] = high
    parts_ref[2 * CH : 3 * CH, lanes] = low


def times(value, parts):
    high, low = split(value)
    return jnp.dot(jnp.concatenate([high, low, high], axis=1), parts, preferred_element_type=jnp.float32)


def scan_kernel(packed_ref, center_ref, upper_ref, parts):
    center = center_ref[...]
    row = lax.broadcasted_iota(jnp.int32, (CH, CH), 0)
    lane = lax.broadcasted_iota(jnp.int32, (CH, CH), 1)
    identity = jnp.where(row == lane, 1.0, 0.0)
    groups = SLICES // LENGTH
    pairs = groups // 2
    middle = range(1, groups - 1)

    def residues(place):
        begins = [(group * LENGTH + place) * SLOT for group in range(groups)]
        return jnp.concatenate([packed_ref[begin : begin + SHARE, :] for begin in begins], axis=0)

    def mean(group, place):
        begin = (group * LENGTH + place) * SLOT + SHARE
        return packed_ref[begin : begin + 1, :]

    def scaled(errors, place):
        return [errors[group * SHARE : (group + 1) * SHARE] * mean(group, place) for group in range(groups)]

    def change(group):
        return changes[(group - 1) * CH : group * CH]

    def prepared(place, value):
        stack_parts(parts.at[place], value, slice(0, CH))
        return parts[place]

    split_at = groups * SHARE
    errors = residues(LENGTH - 1)
    starts = [identity * mean(group, LENGTH - 1) for group in middle]
    changes = exact_left(jnp.concatenate(starts, axis=0), center)
    for place in range(LENGTH - 2, -1, -1):
        rows = scaled(errors, place)
        for group in middle:
            rows.append((change(group) + identity) * mean(group, place))
        moved = exact_left(jnp.concatenate(rows, axis=0), center)
        errors = residues(place) + errors + moved[0:split_at]
        changes = changes + moved[split_at:]

    totals = [errors[group * SHARE : (group + 1) * SHARE] for group in range(groups)]
    maps = {group: prepared(group, change(group)) for group in middle}
    pair_totals, pair_maps = {}, {}
    for pair in range(1, pairs):
        low, high = 2 * pair, 2 * pair + 1
        pair_totals[pair] = totals[low] + totals[high] + times(totals[high], maps[low])
        if pair < pairs - 1:
            both = change(low) + change(high) + times(change(high), maps[low])
            pair_maps[pair] = prepared(groups - 1 + pair, both)
    carries = [None] * groups
    carry = jnp.zeros((SHARE, CH), jnp.float32)
    for pair in range(pairs - 1, -1, -1):
        low, high = 2 * pair, 2 * pair + 1
        carries[high] = carry
        carries[low] = totals[high] if pair == pairs - 1 else totals[high] + carry + times(carry, maps[high])
        if pair > 0:
            if pair < pairs - 1:
                carry = carry + times(carry, pair_maps[pair])
            carry = carry + pair_totals[pair]

    errors = jnp.concatenate(carries, axis=0)
    for place in range(LENGTH - 1, -1, -1):
        for group in range(groups):
            begin = (group * LENGTH + place) * SHARE
            upper_ref[begin : begin + SHARE, :] = errors[group * SHARE : (group + 1) * SHARE]
        if place > 0:
            moved = exact_left(jnp.concatenate(scaled(errors, place), axis=0), center)
            errors = residues(place) + errors + moved


def points_kernel(own_ref, residue_ref, error_ref, mean_ref, center_ref, points_ref, mark_ref):
    mark_ref[...] = mean_ref[...]
    error = error_ref[...]
    moved = moved_by(error, mean_ref[0:1, :], center_ref[...])
    points_ref[...] = own_ref[...] + (residue_ref[...] + error + moved)


def second_kernel(
    step, core_ref, chosen_ref, error_ref, slope_ref, turned_ref, flipped_ref, kept_ref, sent_ref,
    buffer, grads, total, ordered,
):
    col = columns(PIECE)
    clear_edges(buffer)
    values = [chosen + error for chosen, error in zip(pieces(chosen_ref), pieces(error_ref))]
    for section in range(STEPS_DEV - 1, -1, -1):
        lows = lowered_grads(slope_ref, section, values)
        if section > 0:
            values = adjoint_step(buffer, flipped_ref, lows, values, step, col)
        for k, low in enumerate(lows):
            grad, span = low.astype(jnp.float32), slice(k * PIECE, (k + 1) * PIECE)
            grads[section, span, 0:CH] = from_right(grad, col).astype(jnp.bfloat16)
            grads[section, span, CH : 2 * CH] = low
            grads[section, span, 2 * CH : WIDE] = from_left(grad, col).astype(jnp.bfloat16)
        term = jnp.dot(
            turned_ref[:, section * PIX : (section + 1) * PIX], grads[section], preferred_element_type=jnp.float32
        )
        if section == STEPS_DEV - 1:
            total[...] = term
        elif section > 0:
            total[...] += term
        else:
            for row in range(3):
                for tap in range(3):
                    rows, lanes = slice(row * CH, (row + 1) * CH), slice(tap * CH, (tap + 1) * CH)
                    begin = (3 * row + tap) * CH
                    ordered[begin : begin + CH, :] = step * (total[rows, lanes] + term[rows, lanes])
    first_core = core_ref[0] == 0
    lower, upper = ordered[0:HALF, :], ordered[HALF:TAPS, :]
    kept_ref[...] = jnp.where(first_core, lower, upper)
    sent_ref[...] = jnp.where(first_core, upper, lower)


def add_kernel(left_ref, right_ref, after_ref, out_ref):
    out_ref[...] = left_ref[...] + right_ref[...]


def sum_kernel(parts_ref, out_ref):
    total = parts_ref[0:PART, :]
    for part in range(1, parts_ref.shape[0] // PART):
        total = total + parts_ref[part * PART : (part + 1) * PART, :]
    for copy in range(out_ref.shape[0] // PART):
        out_ref[copy * PART : (copy + 1) * PART, :] = total


def place_kernel(other, core_ref, half_ref, *refs):
    out_ref, sem = refs[-2:]
    place = 1 - core_ref[0] if other else core_ref[0]
    copy = pltpu.make_async_copy(half_ref, out_ref.at[pl.ds(pl.multiple_of(place * HALF, 8), HALF), :], sem)
    copy.start()
    copy.wait()


def placed(other, core, half, so_far=()):
    anywhere = pl.BlockSpec(memory_space=pl.ANY)

    def kernel_of(*refs):
        place_kernel(other, *refs)

    return pl.pallas_call(
        kernel_of,
        out_shape=f32(TAPS, CH),
        in_specs=[pl.BlockSpec(memory_space=pltpu.SMEM), pl.BlockSpec(memory_space=pltpu.VMEM)]
        + [anywhere] * len(so_far),
        out_specs=anywhere,
        scratch_shapes=[pltpu.SemaphoreType.DMA],
        input_output_aliases={2: 0} if so_far else {},
        cost_estimate=pl.CostEstimate(flops=0, bytes_accessed=8 * HALF * CH, transcendentals=0),
        compiler_params=pltpu.CompilerParams(vmem_limit_bytes=LIMIT),
    )(core, half, *so_far)


def ring_down(value, axis, count, distance):
    return lax.ppermute(value, axis, [((i + distance) % count, i) for i in range(count)])


def swapped(rows, axes, count):
    parts = rows.reshape(count, 1, rows.shape[0] // count * CH)
    return lax.all_to_all(parts, axes, 0, 0).reshape(rows.shape)


def local(checkpoints, conv_weight, conv_bias, point_guess, terminal):
    step = 2.0 / (STEPS_DEV * SLICES)
    own = point_guess.reshape(PIX, CH)
    terminal = terminal.reshape(PIX, CH)
    kernel = conv_weight.reshape(TAPS, CH)
    final = (lax.axis_index(("y", "z")) == SLICES - 1).astype(jnp.int32).reshape(1)
    core = lax.axis_index("core").astype(jnp.int32).reshape(1)
    upper = ring_down(own, ("y", "z"), SLICES, 1)

    def bound(function):
        def kernel_of(*refs):
            function(step, *refs)

        return kernel_of

    mark = call(first_kernel, f32(8, CH), 3.0, "ss")(core, final)
    slopes, turned, flipped, center, mean = call(
        bound(forward_kernel),
        [f32(STEPS_DEV, PIX, CH), bf16(WIDE, STEPS_DEV * PIX), bf16(WIDE, WIDE), bf16(2 * CH, CH), f32(8, CH)],
        1.5,
        "vvvv",
        [pltpu.VMEM((WIDE, WIDE), jnp.bfloat16), pltpu.VMEM((STEPS_DEV, PIX, WIDE), jnp.bfloat16)],
    )(mark, checkpoints.reshape(PIX, CH), kernel, conv_bias.reshape(1, CH))

    wide = pltpu.VMEM((PIX, WIDE), jnp.bfloat16)
    packed, residue, chosen = call(
        bound(relax_kernel),
        [f32(SLICES * SLOT, CH), f32(PIX, CH), f32(PIX, CH)],
        1.2,
        "svvvvvv",
        [wide],
    )(final, upper, terminal, own, slopes, flipped, mean)

    gathered = swapped(packed, ("y", "z"), SLICES)
    errors = call(
        scan_kernel, f32(PIX, CH), 2.5, scratch=[pltpu.VMEM((SLICES // LENGTH * 3 // 2, 3 * CH, CH), jnp.bfloat16)]
    )(gathered, center)
    upper_error = swapped(errors, ("y", "z"), SLICES)

    kept, sent = call(
        bound(second_kernel),
        [f32(HALF, CH)] * 2,
        1.7,
        "svvvvv",
        [
            wide,
            pltpu.VMEM((STEPS_DEV, PIX, WIDE), jnp.bfloat16),
            pltpu.VMEM((WIDE, WIDE), jnp.float32),
            pltpu.VMEM((TAPS, CH), jnp.float32),
        ],
    )(core, chosen, upper_error, slopes, turned, flipped)

    received = lax.ppermute(sent, "core", [(0, 1), (1, 0)])
    points, points_mark = call(points_kernel, [f32(PIX, CH), f32(8, CH)], 0.8)(own, residue, upper_error, mean, center)
    half = call(add_kernel, f32(HALF, CH), 0.1, "vva")(kept, received, points_mark)
    parts = swapped(half, ("y", "x"), PLANE)
    copies = call(sum_kernel, f32(SIZE_Z * PART, CH), 0.1)(parts)
    parts = swapped(copies, "z", SIZE_Z)
    copies = call(sum_kernel, f32(HALF, CH), 0.1)(parts)
    half = swapped(copies, ("y", "x"), PLANE)
    other = lax.ppermute(half, "core", [(0, 1), (1, 0)])
    grad_w = placed(True, core, other, [placed(False, core, half)])
    return points.reshape(1, 1, ROWS, COLS, CH), grad_w.reshape(3, 3, CH, CH)


def solution(mesh):
    fine = Mesh(mesh.devices.reshape(SIZE_Y, SIZE_Z, SIZE_X, 2), ("y", "z", "x", "core"))
    state = P(("y", "z"), ("x", "core"), None, None, None)
    return jax.shard_map(
        local,
        mesh=fine,
        in_specs=(state, P(), P(), state, P(("x", "core"), None, None, None)),
        out_specs=(state, P()),
        check_vma=False,
    )
```

```python
import jax
import jax.numpy as jnp
from jax import lax
from jax.experimental import pallas as pl
from jax.experimental.pallas import tpu as pltpu
from jax.sharding import Mesh, PartitionSpec as P

STEPS_DEV = 4
ROWS = 8
COLS = 32
CH = 128
PIX = ROWS * COLS
WIDE = 3 * CH
PIECE = 64
LENGTH = 4
TAPS = 9 * CH
SIZE_Y = 4
SIZE_Z = 8
SIZE_X = 4
PLANE = SIZE_X * SIZE_Y
PART = 36
HALF = PLANE * PART
SLICES = SIZE_Y * SIZE_Z
SHARE = PIX // SLICES
SLOT = SHARE + 1
LIMIT = 12 << 20


def call(kernel, outs, micros, specs=None, scratch=()):
    space = pl.BlockSpec(memory_space=pltpu.VMEM)
    places = {"s": pl.BlockSpec(memory_space=pltpu.SMEM), "v": space, "a": pl.BlockSpec(memory_space=pl.ANY)}

    def run(*operands):
        kinds = specs or "v" * len(operands)
        return pl.pallas_call(
            kernel,
            out_shape=outs,
            in_specs=[places[kind] for kind in kinds],
            out_specs=[space] * len(outs) if isinstance(outs, list) else space,
            scratch_shapes=scratch,
            cost_estimate=pl.CostEstimate(
                flops=int(micros * 1e9), bytes_accessed=int(micros * 3.6e6), transcendentals=0
            ),
            compiler_params=pltpu.CompilerParams(vmem_limit_bytes=LIMIT),
        )(*operands)

    return run


def f32(*shape):
    return jax.ShapeDtypeStruct(shape, jnp.float32)


def bf16(*shape):
    return jax.ShapeDtypeStruct(shape, jnp.bfloat16)


def columns(count):
    return lax.broadcasted_iota(jnp.int32, (count, CH), 0) % COLS


def clear_edges(buffer):
    zeros = jnp.zeros((COLS, CH), jnp.bfloat16)
    buffer[0:COLS, 0:CH] = zeros
    buffer[PIX - COLS : PIX, 2 * CH : WIDE] = zeros


def spread(buffer, low):
    buffer[COLS:PIX, 0:CH] = low[0 : PIX - COLS]
    buffer[:, CH : 2 * CH] = low
    buffer[0 : PIX - COLS, 2 * CH : WIDE] = low[COLS:PIX]


def from_left(value, col):
    return jnp.where(col > 0, pltpu.roll(value, 1, 0), 0.0)


def from_right(value, col):
    return jnp.where(col < COLS - 1, pltpu.roll(value, value.shape[0] - 1, 0), 0.0)


def convolve(buffer, kernel, col):
    taps = jnp.dot(buffer, kernel[...], preferred_element_type=jnp.float32)
    sides = from_left(taps[:, 0:CH], col) + from_right(taps[:, 2 * CH : WIDE], col)
    return taps[:, CH : 2 * CH] + sides


def spread_piece(buffer, low, begin):
    end = begin + PIECE
    below, above = min(PIX, end + COLS), max(0, begin - COLS)
    buffer[begin + COLS : below, 0:CH] = low[0 : below - begin - COLS]
    buffer[begin:end, CH : 2 * CH] = low
    buffer[above : end - COLS, 2 * CH : WIDE] = low[above + COLS - begin : PIECE]


def pieces(ref, *lead):
    return [ref[(*lead, slice(begin, begin + PIECE))] for begin in range(0, PIX, PIECE)]


def split(value):
    high = value.astype(jnp.bfloat16)
    return high, (value - high.astype(jnp.float32)).astype(jnp.bfloat16)


def exact_left(value, weight_twice):
    return jnp.dot(
        jnp.concatenate(split(value), axis=1), weight_twice, preferred_element_type=jnp.float32
    )


def first_kernel(core_ref, final_ref, mark_ref):
    mark_ref[...] = jnp.zeros_like(mark_ref)


def forward_kernel(
    step, mark_ref, start_ref, kernel_ref, bias_ref, slope_ref, turned_ref, flipped_ref,
    center_ref, mean_ref, weights, lowered,
):
    col = columns(PIX)
    bias = bias_ref[...]
    for row in range(3):
        for tap in range(3):
            begin = (3 * row + tap) * CH
            weights[row * CH : (row + 1) * CH, tap * CH : (tap + 1) * CH] = kernel_ref[begin : begin + CH, :]
    current = start_ref[...].astype(jnp.float32)
    for section in range(STEPS_DEV):
        buffer = lowered.at[section]
        clear_edges(buffer)
        spread(buffer, current.astype(jnp.bfloat16))
        tanh_out = jnp.tanh(convolve(buffer[...], weights, col) + bias)
        slope = 1.0 - tanh_out * tanh_out
        slope_ref[section] = slope
        if section == 0:
            mean = jnp.sum(slope, axis=0, keepdims=True) * (STEPS_DEV * step / PIX)
            mean_ref[...] = jnp.broadcast_to(mean, (8, CH))
        current = current + step * tanh_out
    for section in range(STEPS_DEV):
        block = lowered[section].astype(jnp.float32)
        turned_ref[:, section * PIX : (section + 1) * PIX] = block.T.astype(jnp.bfloat16)
    for row in range(3):
        for tap in range(3):
            begin = (8 - 3 * row - tap) * CH
            turned = kernel_ref[begin : begin + CH, :].astype(jnp.float32).T.astype(jnp.bfloat16)
            flipped_ref[row * CH : (row + 1) * CH, tap * CH : (tap + 1) * CH] = turned
            if row == 1 and tap == 1:
                center_ref[0:CH, :] = turned
                center_ref[CH : 2 * CH, :] = turned


def adjoint_step(buffer, flipped, lows, values, step, col):
    for k, low in enumerate(lows):
        spread_piece(buffer, low, k * PIECE)
    return [
        value + step * convolve(buffer[k * PIECE : (k + 1) * PIECE, :], flipped, col)
        for k, value in enumerate(values)
    ]


def lowered_grads(slope_ref, section, values):
    return [(slope * value).astype(jnp.bfloat16) for slope, value in zip(pieces(slope_ref, section), values)]


def relax_kernel(
    step, final_ref, upper_ref, terminal_ref, own_ref, slope_ref, flipped_ref, mean_ref,
    packed_ref, residue_ref, chosen_ref, buffer,
):
    col = columns(PIECE)
    clear_edges(buffer)
    final = final_ref[0] == 1
    values = [jnp.where(final, last, upper) for last, upper in zip(pieces(terminal_ref), pieces(upper_ref))]
    for k, value in enumerate(values):
        chosen_ref[k * PIECE : (k + 1) * PIECE, :] = value
    for section in range(STEPS_DEV - 1, -1, -1):
        lows = lowered_grads(slope_ref, section, values)
        values = adjoint_step(buffer, flipped_ref, lows, values, step, col)
    mean = mean_ref[0:1, :]
    for k, (value, own) in enumerate(zip(values, pieces(own_ref))):
        residue = value - own
        residue_ref[k * PIECE : (k + 1) * PIECE, :] = residue
        for share in range(PIECE // SHARE):
            begin = (k * (PIECE // SHARE) + share) * SLOT
            packed_ref[begin : begin + SHARE, :] = residue[share * SHARE : (share + 1) * SHARE]
            packed_ref[begin + SHARE : begin + SLOT, :] = mean


def moved_by(value, mean, center):
    return exact_left(value * mean, center)


def stack_parts(parts_ref, value, lanes):
    high, low = split(value)
    parts_ref[0:CH, lanes] = high
    parts_ref[CH : 2 * CH, lanes] = high
    parts_ref[2 * CH : 3 * CH, lanes] = low


def times(value, parts):
    high, low = split(value)
    return jnp.dot(jnp.concatenate([high, low, high], axis=1), parts, preferred_element_type=jnp.float32)


def scan_kernel(packed_ref, center_ref, upper_ref, parts):
    center = center_ref[...]
    row = lax.broadcasted_iota(jnp.int32, (CH, CH), 0)
    lane = lax.broadcasted_iota(jnp.int32, (CH, CH), 1)
    identity = jnp.where(row == lane, 1.0, 0.0)
    groups = SLICES // LENGTH
    pairs = groups // 2
    middle = range(1, groups - 1)

    def residues(place):
        begins = [(group * LENGTH + place) * SLOT for group in range(groups)]
        return jnp.concatenate([packed_ref[begin : begin + SHARE, :] for begin in begins], axis=0)

    def mean(group, place):
        begin = (group * LENGTH + place) * SLOT + SHARE
        return packed_ref[begin : begin + 1, :]

    def scaled(errors, place):
        return [errors[group * SHARE : (group + 1) * SHARE] * mean(group, place) for group in range(groups)]

    def change(group):
        return changes[(group - 1) * CH : group * CH]

    def prepared(place, value):
        stack_parts(parts.at[place], value, slice(0, CH))
        return parts[place]

    split_at = groups * SHARE
    errors = residues(LENGTH - 1)
    starts = [identity * mean(group, LENGTH - 1) for group in middle]
    changes = exact_left(jnp.concatenate(starts, axis=0), center)
    for place in range(LENGTH - 2, -1, -1):
        rows = scaled(errors, place)
        for group in middle:
            rows.append((change(group) + identity) * mean(group, place))
        moved = exact_left(jnp.concatenate(rows, axis=0), center)
        errors = residues(place) + errors + moved[0:split_at]
        changes = changes + moved[split_at:]

    totals = [errors[group * SHARE : (group + 1) * SHARE] for group in range(groups)]
    maps = {group: prepared(group, change(group)) for group in middle}
    pair_totals, pair_maps = {}, {}
    for pair in range(1, pairs):
        low, high = 2 * pair, 2 * pair + 1
        pair_totals[pair] = totals[low] + totals[high] + times(totals[high], maps[low])
        if pair < pairs - 1:
            both = change(low) + change(high) + times(change(high), maps[low])
            pair_maps[pair] = prepared(groups - 1 + pair, both)
    carries = [None] * groups
    carry = jnp.zeros((SHARE, CH), jnp.float32)
    for pair in range(pairs - 1, -1, -1):
        low, high = 2 * pair, 2 * pair + 1
        carries[high] = carry
        carries[low] = totals[high] if pair == pairs - 1 else totals[high] + carry + times(carry, maps[high])
        if pair > 0:
            if pair < pairs - 1:
                carry = carry + times(carry, pair_maps[pair])
            carry = carry + pair_totals[pair]

    errors = jnp.concatenate(carries, axis=0)
    for place in range(LENGTH - 1, -1, -1):
        for group in range(groups):
            begin = (group * LENGTH + place) * SHARE
            upper_ref[begin : begin + SHARE, :] = errors[group * SHARE : (group + 1) * SHARE]
        if place > 0:
            moved = exact_left(jnp.concatenate(scaled(errors, place), axis=0), center)
            errors = residues(place) + errors + moved


def points_kernel(own_ref, residue_ref, error_ref, mean_ref, center_ref, points_ref, mark_ref):
    mark_ref[...] = mean_ref[...]
    error = error_ref[...]
    moved = moved_by(error, mean_ref[0:1, :], center_ref[...])
    points_ref[...] = own_ref[...] + (residue_ref[...] + error + moved)


def half_rows(turned_ref, half, lanes):
    begins = [pl.multiple_of(row * CH + half * (CH // 2), CH // 2) for row in range(3)]
    return jnp.concatenate([turned_ref[pl.ds(begin, CH // 2), lanes] for begin in begins], axis=0)


def store_half(out_ref, taps):
    height = CH // 2
    for row in range(3):
        for tap in range(3):
            begin = (3 * row + tap) * height
            out_ref[begin : begin + height, :] = taps[row * height : (row + 1) * height, tap * CH : (tap + 1) * CH]


def second_kernel(
    step, core_ref, chosen_ref, error_ref, slope_ref, turned_ref, flipped_ref, sent_ref, grads_ref, buffer, total
):
    col = columns(PIECE)
    clear_edges(buffer)
    values = [chosen + error for chosen, error in zip(pieces(chosen_ref), pieces(error_ref))]
    for section in range(STEPS_DEV - 1, -1, -1):
        lows = lowered_grads(slope_ref, section, values)
        if section > 0:
            values = adjoint_step(buffer, flipped_ref, lows, values, step, col)
        for k, low in enumerate(lows):
            begin = section * PIX + k * PIECE
            grad, span = low.astype(jnp.float32), slice(begin, begin + PIECE)
            grads_ref[span, 0:CH] = from_right(grad, col).astype(jnp.bfloat16)
            grads_ref[span, CH : 2 * CH] = low
            grads_ref[span, 2 * CH : WIDE] = from_left(grad, col).astype(jnp.bfloat16)
        part = slice(section * PIX, (section + 1) * PIX)
        term = jnp.dot(
            half_rows(turned_ref, 1 - core_ref[0], part), grads_ref[part, :], preferred_element_type=jnp.float32
        )
        if section == STEPS_DEV - 1:
            total[...] = term
        elif section > 0:
            total[...] += term
        else:
            store_half(sent_ref, step * (total[...] + term))


def kept_kernel(step, core_ref, turned_ref, grads_ref, kept_ref):
    rows = half_rows(turned_ref, core_ref[0], slice(0, STEPS_DEV * PIX))
    store_half(kept_ref, step * jnp.dot(rows, grads_ref[...], preferred_element_type=jnp.float32))


def add_kernel(left_ref, right_ref, after_ref, out_ref):
    out_ref[...] = left_ref[...] + right_ref[...]


def sum_kernel(parts_ref, out_ref):
    total = parts_ref[0:PART, :]
    for part in range(1, parts_ref.shape[0] // PART):
        total = total + parts_ref[part * PART : (part + 1) * PART, :]
    for copy in range(out_ref.shape[0] // PART):
        out_ref[copy * PART : (copy + 1) * PART, :] = total


def place_kernel(other, core_ref, half_ref, *refs):
    out_ref, sems = refs[-2:]
    place = 1 - core_ref[0] if other else core_ref[0]
    copies = []
    for row in range(3):
        taps = slice(3 * row, 3 * row + 3)
        copies.append(pltpu.make_async_copy(half_ref.at[taps], out_ref.at[taps, place], sems.at[row]))
    for copy in copies:
        copy.start()
    for copy in copies:
        copy.wait()


def placed(other, core, half, so_far=()):
    anywhere = pl.BlockSpec(memory_space=pl.ANY)

    def kernel_of(*refs):
        place_kernel(other, *refs)

    return pl.pallas_call(
        kernel_of,
        out_shape=f32(9, 2, CH // 2, CH),
        in_specs=[pl.BlockSpec(memory_space=pltpu.SMEM), pl.BlockSpec(memory_space=pltpu.VMEM)]
        + [anywhere] * len(so_far),
        out_specs=anywhere,
        scratch_shapes=[pltpu.SemaphoreType.DMA((3,))],
        input_output_aliases={2: 0} if so_far else {},
        cost_estimate=pl.CostEstimate(flops=0, bytes_accessed=8 * HALF * CH, transcendentals=0),
        compiler_params=pltpu.CompilerParams(vmem_limit_bytes=LIMIT),
    )(core, half.reshape(9, CH // 2, CH), *so_far)


def ring_down(value, axis, count, distance):
    return lax.ppermute(value, axis, [((i + distance) % count, i) for i in range(count)])


def swapped(rows, axes, count):
    parts = rows.reshape(count, 1, rows.shape[0] // count * CH)
    return lax.all_to_all(parts, axes, 0, 0).reshape(rows.shape)


def local(checkpoints, conv_weight, conv_bias, point_guess, terminal):
    step = 2.0 / (STEPS_DEV * SLICES)
    own = point_guess.reshape(PIX, CH)
    terminal = terminal.reshape(PIX, CH)
    kernel = conv_weight.reshape(TAPS, CH)
    final = (lax.axis_index(("y", "z")) == SLICES - 1).astype(jnp.int32).reshape(1)
    core = lax.axis_index("core").astype(jnp.int32).reshape(1)
    upper = ring_down(own, ("y", "z"), SLICES, 1)

    def bound(function):
        def kernel_of(*refs):
            function(step, *refs)

        return kernel_of

    mark = call(first_kernel, f32(8, CH), 3.0, "ss")(core, final)
    slopes, turned, flipped, center, mean = call(
        bound(forward_kernel),
        [f32(STEPS_DEV, PIX, CH), bf16(WIDE, STEPS_DEV * PIX), bf16(WIDE, WIDE), bf16(2 * CH, CH), f32(8, CH)],
        1.5,
        "vvvv",
        [pltpu.VMEM((WIDE, WIDE), jnp.bfloat16), pltpu.VMEM((STEPS_DEV, PIX, WIDE), jnp.bfloat16)],
    )(mark, checkpoints.reshape(PIX, CH), kernel, conv_bias.reshape(1, CH))

    wide = pltpu.VMEM((PIX, WIDE), jnp.bfloat16)
    packed, residue, chosen = call(
        bound(relax_kernel),
        [f32(SLICES * SLOT, CH), f32(PIX, CH), f32(PIX, CH)],
        1.2,
        "svvvvvv",
        [wide],
    )(final, upper, terminal, own, slopes, flipped, mean)

    gathered = swapped(packed, ("y", "z"), SLICES)
    errors = call(
        scan_kernel, f32(PIX, CH), 2.5, scratch=[pltpu.VMEM((SLICES // LENGTH * 3 // 2, 3 * CH, CH), jnp.bfloat16)]
    )(gathered, center)
    upper_error = swapped(errors, ("y", "z"), SLICES)

    sent, grads = call(
        bound(second_kernel),
        [f32(HALF, CH), bf16(STEPS_DEV * PIX, WIDE)],
        1.1,
        "svvvvv",
        [wide, pltpu.VMEM((WIDE // 2, WIDE), jnp.float32)],
    )(core, chosen, upper_error, slopes, turned, flipped)

    received = lax.ppermute(sent, "core", [(0, 1), (1, 0)])
    kept = call(bound(kept_kernel), f32(HALF, CH), 0.4, "svv")(core, turned, grads)
    points, points_mark = call(points_kernel, [f32(PIX, CH), f32(8, CH)], 0.8)(own, residue, upper_error, mean, center)
    half = call(add_kernel, f32(HALF, CH), 0.1, "vva")(kept, received, points_mark)
    parts = swapped(half, ("y", "x"), PLANE)
    copies = call(sum_kernel, f32(SIZE_Z * PART, CH), 0.1)(parts)
    parts = swapped(copies, "z", SIZE_Z)
    copies = call(sum_kernel, f32(HALF, CH), 0.1)(parts)
    half = swapped(copies, ("y", "x"), PLANE)
    other = lax.ppermute(half, "core", [(0, 1), (1, 0)])
    grad_w = placed(True, core, other, [placed(False, core, half)])
    return points.reshape(1, 1, ROWS, COLS, CH), grad_w.reshape(3, 3, CH, CH)


def solution(mesh):
    fine = Mesh(mesh.devices.reshape(SIZE_Y, SIZE_Z, SIZE_X, 2), ("y", "z", "x", "core"))
    state = P(("y", "z"), ("x", "core"), None, None, None)
    return jax.shard_map(
        local,
        mesh=fine,
        in_specs=(state, P(), P(), state, P(("x", "core"), None, None, None)),
        out_specs=(state, P()),
        check_vma=False,
    )
```

```python
import jax
import jax.numpy as jnp
from jax import lax
from jax.experimental import pallas as pl
from jax.experimental.pallas import tpu as pltpu
from jax.sharding import Mesh, PartitionSpec as P

STEPS_DEV = 4
ROWS = 8
COLS = 32
CH = 128
PIX = ROWS * COLS
WIDE = 3 * CH
PIECE = 64
LENGTH = 4
TAPS = 9 * CH
SIZE_Y = 4
SIZE_Z = 8
SIZE_X = 4
PLANE = SIZE_X * SIZE_Y
PART = 36
HALF = PLANE * PART
SLICES = SIZE_Y * SIZE_Z
SHARE = PIX // SLICES
SLOT = SHARE + 1
LIMIT = 12 << 20


def call(kernel, outs, micros, specs=None, scratch=()):
    space = pl.BlockSpec(memory_space=pltpu.VMEM)
    places = {"s": pl.BlockSpec(memory_space=pltpu.SMEM), "v": space, "a": pl.BlockSpec(memory_space=pl.ANY)}

    def run(*operands):
        kinds = specs or "v" * len(operands)
        return pl.pallas_call(
            kernel,
            out_shape=outs,
            in_specs=[places[kind] for kind in kinds],
            out_specs=[space] * len(outs) if isinstance(outs, list) else space,
            scratch_shapes=scratch,
            cost_estimate=pl.CostEstimate(
                flops=int(micros * 1e9), bytes_accessed=int(micros * 3.6e6), transcendentals=0
            ),
            compiler_params=pltpu.CompilerParams(vmem_limit_bytes=LIMIT),
        )(*operands)

    return run


def f32(*shape):
    return jax.ShapeDtypeStruct(shape, jnp.float32)


def bf16(*shape):
    return jax.ShapeDtypeStruct(shape, jnp.bfloat16)


def columns(count):
    return lax.broadcasted_iota(jnp.int32, (count, CH), 0) % COLS


def clear_edges(buffer):
    zeros = jnp.zeros((COLS, CH), jnp.bfloat16)
    buffer[0:COLS, 0:CH] = zeros
    buffer[PIX - COLS : PIX, 2 * CH : WIDE] = zeros


def spread(buffer, low):
    buffer[COLS:PIX, 0:CH] = low[0 : PIX - COLS]
    buffer[:, CH : 2 * CH] = low
    buffer[0 : PIX - COLS, 2 * CH : WIDE] = low[COLS:PIX]


def from_left(value, col):
    return jnp.where(col > 0, pltpu.roll(value, 1, 0), 0.0)


def from_right(value, col):
    return jnp.where(col < COLS - 1, pltpu.roll(value, value.shape[0] - 1, 0), 0.0)


def convolve(buffer, kernel, col):
    taps = jnp.dot(buffer, kernel[...], preferred_element_type=jnp.float32)
    sides = from_left(taps[:, 0:CH], col) + from_right(taps[:, 2 * CH : WIDE], col)
    return taps[:, CH : 2 * CH] + sides


def spread_piece(buffer, low, begin):
    end = begin + PIECE
    below, above = min(PIX, end + COLS), max(0, begin - COLS)
    buffer[begin + COLS : below, 0:CH] = low[0 : below - begin - COLS]
    buffer[begin:end, CH : 2 * CH] = low
    buffer[above : end - COLS, 2 * CH : WIDE] = low[above + COLS - begin : PIECE]


def pieces(ref, *lead):
    return [ref[(*lead, slice(begin, begin + PIECE))] for begin in range(0, PIX, PIECE)]


def split(value):
    high = value.astype(jnp.bfloat16)
    return high, (value - high.astype(jnp.float32)).astype(jnp.bfloat16)


def exact_left(value, weight_twice):
    return jnp.dot(
        jnp.concatenate(split(value), axis=1), weight_twice, preferred_element_type=jnp.float32
    )


def first_kernel(mark_ref):
    mark_ref[...] = jnp.zeros_like(mark_ref)


def forward_kernel(
    step, mark_ref, start_ref, kernel_ref, bias_ref, slope_ref, turned_ref, flipped_ref,
    center_ref, mean_ref, weights, lowered,
):
    col = columns(PIX)
    bias = bias_ref[...]
    for row in range(3):
        for tap in range(3):
            begin = (3 * row + tap) * CH
            weights[row * CH : (row + 1) * CH, tap * CH : (tap + 1) * CH] = kernel_ref[begin : begin + CH, :]
    current = start_ref[...].astype(jnp.float32)
    for section in range(STEPS_DEV):
        buffer = lowered.at[section]
        clear_edges(buffer)
        spread(buffer, current.astype(jnp.bfloat16))
        tanh_out = jnp.tanh(convolve(buffer[...], weights, col) + bias)
        slope = 1.0 - tanh_out * tanh_out
        slope_ref[section] = slope
        if section == 0:
            mean = jnp.sum(slope, axis=0, keepdims=True) * (STEPS_DEV * step / PIX)
            mean_ref[...] = jnp.broadcast_to(mean, (8, CH))
        current = current + step * tanh_out
    for section in range(STEPS_DEV):
        block = lowered[section].astype(jnp.float32)
        turned_ref[:, section * PIX : (section + 1) * PIX] = block.T.astype(jnp.bfloat16)
    for row in range(3):
        for tap in range(3):
            begin = (8 - 3 * row - tap) * CH
            turned = kernel_ref[begin : begin + CH, :].astype(jnp.float32).T.astype(jnp.bfloat16)
            flipped_ref[row * CH : (row + 1) * CH, tap * CH : (tap + 1) * CH] = turned
            if row == 1 and tap == 1:
                center_ref[0:CH, :] = turned
                center_ref[CH : 2 * CH, :] = turned


def adjoint_step(buffer, flipped, lows, values, step, col):
    for k, low in enumerate(lows):
        spread_piece(buffer, low, k * PIECE)
    return [
        value + step * convolve(buffer[k * PIECE : (k + 1) * PIECE, :], flipped, col)
        for k, value in enumerate(values)
    ]


def lowered_grads(slope_ref, section, values):
    return [(slope * value).astype(jnp.bfloat16) for slope, value in zip(pieces(slope_ref, section), values)]


def relax_kernel(
    step, upper_ref, terminal_ref, own_ref, slope_ref, flipped_ref, mean_ref,
    packed_ref, residue_ref, chosen_ref, buffer,
):
    col = columns(PIECE)
    clear_edges(buffer)
    final = lax.axis_index(("y", "z")) == SLICES - 1
    values = [jnp.where(final, last, upper) for last, upper in zip(pieces(terminal_ref), pieces(upper_ref))]
    for k, value in enumerate(values):
        chosen_ref[k * PIECE : (k + 1) * PIECE, :] = value
    for section in range(STEPS_DEV - 1, -1, -1):
        lows = lowered_grads(slope_ref, section, values)
        values = adjoint_step(buffer, flipped_ref, lows, values, step, col)
    mean = mean_ref[0:1, :]
    for k, (value, own) in enumerate(zip(values, pieces(own_ref))):
        residue = value - own
        residue_ref[k * PIECE : (k + 1) * PIECE, :] = residue
        for share in range(PIECE // SHARE):
            begin = (k * (PIECE // SHARE) + share) * SLOT
            packed_ref[begin : begin + SHARE, :] = residue[share * SHARE : (share + 1) * SHARE]
            packed_ref[begin + SHARE : begin + SLOT, :] = mean


def moved_by(value, mean, center):
    return exact_left(value * mean, center)


def stack_parts(parts_ref, value, lanes):
    high, low = split(value)
    parts_ref[0:CH, lanes] = high
    parts_ref[CH : 2 * CH, lanes] = high
    parts_ref[2 * CH : 3 * CH, lanes] = low


def times(value, parts):
    high, low = split(value)
    return jnp.dot(jnp.concatenate([high, low, high], axis=1), parts, preferred_element_type=jnp.float32)


def scan_kernel(packed_ref, center_ref, upper_ref, parts):
    center = center_ref[...]
    row = lax.broadcasted_iota(jnp.int32, (CH, CH), 0)
    lane = lax.broadcasted_iota(jnp.int32, (CH, CH), 1)
    identity = jnp.where(row == lane, 1.0, 0.0)
    groups = SLICES // LENGTH
    pairs = groups // 2
    middle = range(1, groups - 1)

    def residues(place):
        begins = [(group * LENGTH + place) * SLOT for group in range(groups)]
        return jnp.concatenate([packed_ref[begin : begin + SHARE, :] for begin in begins], axis=0)

    def mean(group, place):
        begin = (group * LENGTH + place) * SLOT + SHARE
        return packed_ref[begin : begin + 1, :]

    def scaled(errors, place):
        return [errors[group * SHARE : (group + 1) * SHARE] * mean(group, place) for group in range(groups)]

    def change(group):
        return changes[(group - 1) * CH : group * CH]

    def prepared(place, value):
        stack_parts(parts.at[place], value, slice(0, CH))
        return parts[place]

    split_at = groups * SHARE
    errors = residues(LENGTH - 1)
    starts = [identity * mean(group, LENGTH - 1) for group in middle]
    changes = exact_left(jnp.concatenate(starts, axis=0), center)
    for place in range(LENGTH - 2, -1, -1):
        rows = scaled(errors, place)
        for group in middle:
            rows.append((change(group) + identity) * mean(group, place))
        moved = exact_left(jnp.concatenate(rows, axis=0), center)
        errors = residues(place) + errors + moved[0:split_at]
        changes = changes + moved[split_at:]

    totals = [errors[group * SHARE : (group + 1) * SHARE] for group in range(groups)]
    maps = {group: prepared(group, change(group)) for group in middle}
    pair_totals, pair_maps = {}, {}
    for pair in range(1, pairs):
        low, high = 2 * pair, 2 * pair + 1
        pair_totals[pair] = totals[low] + totals[high] + times(totals[high], maps[low])
        if pair < pairs - 1:
            both = change(low) + change(high) + times(change(high), maps[low])
            pair_maps[pair] = prepared(groups - 1 + pair, both)
    carries = [None] * groups
    carry = jnp.zeros((SHARE, CH), jnp.float32)
    for pair in range(pairs - 1, -1, -1):
        low, high = 2 * pair, 2 * pair + 1
        carries[high] = carry
        carries[low] = totals[high] if pair == pairs - 1 else totals[high] + carry + times(carry, maps[high])
        if pair > 0:
            if pair < pairs - 1:
                carry = carry + times(carry, pair_maps[pair])
            carry = carry + pair_totals[pair]

    errors = jnp.concatenate(carries, axis=0)
    for place in range(LENGTH - 1, -1, -1):
        for group in range(groups):
            begin = (group * LENGTH + place) * SHARE
            upper_ref[begin : begin + SHARE, :] = errors[group * SHARE : (group + 1) * SHARE]
        if place > 0:
            moved = exact_left(jnp.concatenate(scaled(errors, place), axis=0), center)
            errors = residues(place) + errors + moved


def points_kernel(own_ref, residue_ref, error_ref, mean_ref, center_ref, points_ref, mark_ref):
    mark_ref[...] = mean_ref[...]
    error = error_ref[...]
    moved = moved_by(error, mean_ref[0:1, :], center_ref[...])
    points_ref[...] = own_ref[...] + (residue_ref[...] + error + moved)


def half_rows(turned_ref, half, lanes):
    begins = [pl.multiple_of(row * CH + half * (CH // 2), CH // 2) for row in range(3)]
    return jnp.concatenate([turned_ref[pl.ds(begin, CH // 2), lanes] for begin in begins], axis=0)


def store_half(out_ref, taps):
    height = CH // 2
    for row in range(3):
        for tap in range(3):
            begin = (3 * row + tap) * height
            out_ref[begin : begin + height, :] = taps[row * height : (row + 1) * height, tap * CH : (tap + 1) * CH]


def second_kernel(
    step, chosen_ref, error_ref, slope_ref, turned_ref, flipped_ref, sent_ref, grads_ref, buffer, total
):
    col = columns(PIECE)
    clear_edges(buffer)
    values = [chosen + error for chosen, error in zip(pieces(chosen_ref), pieces(error_ref))]
    for section in range(STEPS_DEV - 1, -1, -1):
        lows = lowered_grads(slope_ref, section, values)
        if section > 0:
            values = adjoint_step(buffer, flipped_ref, lows, values, step, col)
        for k, low in enumerate(lows):
            begin = section * PIX + k * PIECE
            grad, span = low.astype(jnp.float32), slice(begin, begin + PIECE)
            grads_ref[span, 0:CH] = from_right(grad, col).astype(jnp.bfloat16)
            grads_ref[span, CH : 2 * CH] = low
            grads_ref[span, 2 * CH : WIDE] = from_left(grad, col).astype(jnp.bfloat16)
        part = slice(section * PIX, (section + 1) * PIX)
        term = jnp.dot(
            half_rows(turned_ref, 1 - lax.axis_index("core"), part), grads_ref[part, :], preferred_element_type=jnp.float32
        )
        if section == STEPS_DEV - 1:
            total[...] = term
        elif section > 0:
            total[...] += term
        else:
            store_half(sent_ref, step * (total[...] + term))


def kept_kernel(step, turned_ref, grads_ref, kept_ref):
    rows = half_rows(turned_ref, lax.axis_index("core"), slice(0, STEPS_DEV * PIX))
    store_half(kept_ref, step * jnp.dot(rows, grads_ref[...], preferred_element_type=jnp.float32))


def add_kernel(left_ref, right_ref, after_ref, out_ref):
    out_ref[...] = left_ref[...] + right_ref[...]


def sum_kernel(parts_ref, out_ref):
    total = parts_ref[0:PART, :]
    for part in range(1, parts_ref.shape[0] // PART):
        total = total + parts_ref[part * PART : (part + 1) * PART, :]
    for copy in range(out_ref.shape[0] // PART):
        out_ref[copy * PART : (copy + 1) * PART, :] = total


def place_kernel(other, half_ref, *refs):
    out_ref, sems = refs[-2:]
    core = lax.axis_index("core")
    place = 1 - core if other else core
    copies = []
    for row in range(3):
        taps = slice(3 * row, 3 * row + 3)
        copies.append(pltpu.make_async_copy(half_ref.at[taps], out_ref.at[taps, place], sems.at[row]))
    for copy in copies:
        copy.start()
    for copy in copies:
        copy.wait()


def placed(other, half, so_far=()):
    anywhere = pl.BlockSpec(memory_space=pl.ANY)

    def kernel_of(*refs):
        place_kernel(other, *refs)

    return pl.pallas_call(
        kernel_of,
        out_shape=f32(9, 2, CH // 2, CH),
        in_specs=[pl.BlockSpec(memory_space=pltpu.VMEM)] + [anywhere] * len(so_far),
        out_specs=anywhere,
        scratch_shapes=[pltpu.SemaphoreType.DMA((3,))],
        input_output_aliases={1: 0} if so_far else {},
        cost_estimate=pl.CostEstimate(flops=0, bytes_accessed=8 * HALF * CH, transcendentals=0),
        compiler_params=pltpu.CompilerParams(vmem_limit_bytes=LIMIT),
    )(half.reshape(9, CH // 2, CH), *so_far)


def ring_down(value, axis, count, distance):
    return lax.ppermute(value, axis, [((i + distance) % count, i) for i in range(count)])


def swapped(rows, axes, count):
    parts = rows.reshape(count, 1, rows.shape[0] // count * CH)
    return lax.all_to_all(parts, axes, 0, 0).reshape(rows.shape)


def local(checkpoints, conv_weight, conv_bias, point_guess, terminal):
    step = 2.0 / (STEPS_DEV * SLICES)
    own = point_guess.reshape(PIX, CH)
    terminal = terminal.reshape(PIX, CH)
    kernel = conv_weight.reshape(TAPS, CH)
    upper = ring_down(own, ("y", "z"), SLICES, 1)

    def bound(function):
        def kernel_of(*refs):
            function(step, *refs)

        return kernel_of

    mark = call(first_kernel, f32(8, CH), 3.0)()
    slopes, turned, flipped, center, mean = call(
        bound(forward_kernel),
        [f32(STEPS_DEV, PIX, CH), bf16(WIDE, STEPS_DEV * PIX), bf16(WIDE, WIDE), bf16(2 * CH, CH), f32(8, CH)],
        1.5,
        "vvvv",
        [pltpu.VMEM((WIDE, WIDE), jnp.bfloat16), pltpu.VMEM((STEPS_DEV, PIX, WIDE), jnp.bfloat16)],
    )(mark, checkpoints.reshape(PIX, CH), kernel, conv_bias.reshape(1, CH))

    wide = pltpu.VMEM((PIX, WIDE), jnp.bfloat16)
    packed, residue, chosen = call(
        bound(relax_kernel),
        [f32(SLICES * SLOT, CH), f32(PIX, CH), f32(PIX, CH)],
        1.2,
        scratch=[wide],
    )(upper, terminal, own, slopes, flipped, mean)

    gathered = swapped(packed, ("y", "z"), SLICES)
    errors = call(
        scan_kernel, f32(PIX, CH), 2.5, scratch=[pltpu.VMEM((SLICES // LENGTH * 3 // 2, 3 * CH, CH), jnp.bfloat16)]
    )(gathered, center)
    upper_error = swapped(errors, ("y", "z"), SLICES)

    sent, grads = call(
        bound(second_kernel),
        [f32(HALF, CH), bf16(STEPS_DEV * PIX, WIDE)],
        1.1,
        scratch=[wide, pltpu.VMEM((WIDE // 2, WIDE), jnp.float32)],
    )(chosen, upper_error, slopes, turned, flipped)

    received = lax.ppermute(sent, "core", [(0, 1), (1, 0)])
    kept = call(bound(kept_kernel), f32(HALF, CH), 0.4)(turned, grads)
    points, points_mark = call(points_kernel, [f32(PIX, CH), f32(8, CH)], 0.8)(own, residue, upper_error, mean, center)
    half = call(add_kernel, f32(HALF, CH), 0.1, "vva")(kept, received, points_mark)
    parts = swapped(half, ("y", "x"), PLANE)
    copies = call(sum_kernel, f32(SIZE_Z * PART, CH), 0.1)(parts)
    parts = swapped(copies, "z", SIZE_Z)
    copies = call(sum_kernel, f32(HALF, CH), 0.1)(parts)
    half = swapped(copies, ("y", "x"), PLANE)
    other = lax.ppermute(half, "core", [(0, 1), (1, 0)])
    grad_w = placed(True, other, [placed(False, half)])
    return points.reshape(1, 1, ROWS, COLS, CH), grad_w.reshape(3, 3, CH, CH)


def solution(mesh):
    fine = Mesh(mesh.devices.reshape(SIZE_Y, SIZE_Z, SIZE_X, 2), ("y", "z", "x", "core"))
    state = P(("y", "z"), ("x", "core"), None, None, None)
    return jax.shard_map(
        local,
        mesh=fine,
        in_specs=(state, P(), P(), state, P(("x", "core"), None, None, None)),
        out_specs=(state, P()),
        check_vma=False,
    )
```

```python
import jax
import jax.numpy as jnp
from jax import lax
from jax.experimental import pallas as pl
from jax.experimental.pallas import tpu as pltpu
from jax.sharding import Mesh, PartitionSpec as P

STEPS_DEV = 4
ROWS = 8
COLS = 32
CH = 128
PIX = ROWS * COLS
WIDE = 3 * CH
PIECE = 64
LENGTH = 4
TAPS = 9 * CH
SIZE_Y = 4
SIZE_Z = 8
SIZE_X = 4
PLANE = SIZE_X * SIZE_Y
PART = 36
HALF = PLANE * PART
SLICES = SIZE_Y * SIZE_Z
SHARE = PIX // SLICES
SLOT = SHARE + 1
LIMIT = 12 << 20


def call(kernel, outs, micros, specs=None, scratch=()):
    space = pl.BlockSpec(memory_space=pltpu.VMEM)
    places = {"s": pl.BlockSpec(memory_space=pltpu.SMEM), "v": space, "a": pl.BlockSpec(memory_space=pl.ANY)}

    def run(*operands):
        kinds = specs or "v" * len(operands)
        return pl.pallas_call(
            kernel,
            out_shape=outs,
            in_specs=[places[kind] for kind in kinds],
            out_specs=[space] * len(outs) if isinstance(outs, list) else space,
            scratch_shapes=scratch,
            cost_estimate=pl.CostEstimate(
                flops=int(micros * 1e9), bytes_accessed=int(micros * 3.6e6), transcendentals=0
            ),
            compiler_params=pltpu.CompilerParams(vmem_limit_bytes=LIMIT),
        )(*operands)

    return run


def f32(*shape):
    return jax.ShapeDtypeStruct(shape, jnp.float32)


def bf16(*shape):
    return jax.ShapeDtypeStruct(shape, jnp.bfloat16)


def columns(count):
    return lax.broadcasted_iota(jnp.int32, (count, CH), 0) % COLS


def clear_edges(buffer):
    zeros = jnp.zeros((COLS, CH), jnp.bfloat16)
    buffer[0:COLS, 0:CH] = zeros
    buffer[PIX - COLS : PIX, 2 * CH : WIDE] = zeros


def spread(buffer, low):
    buffer[COLS:PIX, 0:CH] = low[0 : PIX - COLS]
    buffer[:, CH : 2 * CH] = low
    buffer[0 : PIX - COLS, 2 * CH : WIDE] = low[COLS:PIX]


def from_left(value, col):
    return jnp.where(col > 0, pltpu.roll(value, 1, 0), 0.0)


def from_right(value, col):
    return jnp.where(col < COLS - 1, pltpu.roll(value, value.shape[0] - 1, 0), 0.0)


def convolve(buffer, kernel, col):
    taps = jnp.dot(buffer, kernel[...], preferred_element_type=jnp.float32)
    sides = from_left(taps[:, 0:CH], col) + from_right(taps[:, 2 * CH : WIDE], col)
    return taps[:, CH : 2 * CH] + sides


def spread_piece(buffer, low, begin):
    end = begin + PIECE
    below, above = min(PIX, end + COLS), max(0, begin - COLS)
    buffer[begin + COLS : below, 0:CH] = low[0 : below - begin - COLS]
    buffer[begin:end, CH : 2 * CH] = low
    buffer[above : end - COLS, 2 * CH : WIDE] = low[above + COLS - begin : PIECE]


def pieces(ref, *lead):
    return [ref[(*lead, slice(begin, begin + PIECE))] for begin in range(0, PIX, PIECE)]


def split(value):
    high = value.astype(jnp.bfloat16)
    return high, (value - high.astype(jnp.float32)).astype(jnp.bfloat16)


def exact_left(value, weight_twice):
    return jnp.dot(
        jnp.concatenate(split(value), axis=1), weight_twice, preferred_element_type=jnp.float32
    )


def first_kernel(core_ref, final_ref, mark_ref):
    mark_ref[...] = jnp.zeros_like(mark_ref)


def forward_kernel(
    step, mark_ref, start_ref, kernel_ref, bias_ref, slope_ref, turned_ref, flipped_ref,
    center_ref, mean_ref, weights, lowered,
):
    col = columns(PIX)
    bias = bias_ref[...]
    for row in range(3):
        for tap in range(3):
            begin = (3 * row + tap) * CH
            weights[row * CH : (row + 1) * CH, tap * CH : (tap + 1) * CH] = kernel_ref[begin : begin + CH, :]
    current = start_ref[...].astype(jnp.float32)
    for section in range(STEPS_DEV):
        buffer = lowered.at[section]
        clear_edges(buffer)
        spread(buffer, current.astype(jnp.bfloat16))
        tanh_out = jnp.tanh(convolve(buffer[...], weights, col) + bias)
        slope = 1.0 - tanh_out * tanh_out
        slope_ref[section] = slope
        if section == 0:
            mean = jnp.sum(slope, axis=0, keepdims=True) * (STEPS_DEV * step / PIX)
            mean_ref[...] = jnp.broadcast_to(mean, (8, CH))
        current = current + step * tanh_out
    for section in range(STEPS_DEV):
        lanes = slice(section * PIX, (section + 1) * PIX)
        for row in range(3):
            block = lowered[section, :, row * CH : (row + 1) * CH].astype(jnp.float32)
            for tap, moved in enumerate((from_left(block, col), block, from_right(block, col))):
                begin = (3 * row + tap) * CH
                turned_ref[begin : begin + CH, lanes] = moved.T.astype(jnp.bfloat16)
    for row in range(3):
        for tap in range(3):
            begin = (8 - 3 * row - tap) * CH
            turned = kernel_ref[begin : begin + CH, :].astype(jnp.float32).T.astype(jnp.bfloat16)
            flipped_ref[row * CH : (row + 1) * CH, tap * CH : (tap + 1) * CH] = turned
            if row == 1 and tap == 1:
                center_ref[0:CH, :] = turned
                center_ref[CH : 2 * CH, :] = turned


def adjoint_step(buffer, flipped, lows, values, step, col):
    for k, low in enumerate(lows):
        spread_piece(buffer, low, k * PIECE)
    return [
        value + step * convolve(buffer[k * PIECE : (k + 1) * PIECE, :], flipped, col)
        for k, value in enumerate(values)
    ]


def lowered_grads(slope_ref, section, values):
    return [(slope * value).astype(jnp.bfloat16) for slope, value in zip(pieces(slope_ref, section), values)]


def relax_kernel(
    step, final_ref, upper_ref, terminal_ref, own_ref, slope_ref, flipped_ref, mean_ref,
    packed_ref, residue_ref, chosen_ref, buffer,
):
    col = columns(PIECE)
    clear_edges(buffer)
    final = final_ref[0] == 1
    values = [jnp.where(final, last, upper) for last, upper in zip(pieces(terminal_ref), pieces(upper_ref))]
    for k, value in enumerate(values):
        chosen_ref[k * PIECE : (k + 1) * PIECE, :] = value
    for section in range(STEPS_DEV - 1, -1, -1):
        lows = lowered_grads(slope_ref, section, values)
        values = adjoint_step(buffer, flipped_ref, lows, values, step, col)
    mean = mean_ref[0:1, :]
    for k, (value, own) in enumerate(zip(values, pieces(own_ref))):
        residue = value - own
        residue_ref[k * PIECE : (k + 1) * PIECE, :] = residue
        for share in range(PIECE // SHARE):
            begin = (k * (PIECE // SHARE) + share) * SLOT
            packed_ref[begin : begin + SHARE, :] = residue[share * SHARE : (share + 1) * SHARE]
            packed_ref[begin + SHARE : begin + SLOT, :] = mean


def moved_by(value, mean, center):
    return exact_left(value * mean, center)


def stack_parts(parts_ref, value, lanes):
    high, low = split(value)
    parts_ref[0:CH, lanes] = high
    parts_ref[CH : 2 * CH, lanes] = high
    parts_ref[2 * CH : 3 * CH, lanes] = low


def times(value, parts):
    high, low = split(value)
    return jnp.dot(jnp.concatenate([high, low, high], axis=1), parts, preferred_element_type=jnp.float32)


def scan_kernel(packed_ref, center_ref, upper_ref, parts):
    center = center_ref[...]
    row = lax.broadcasted_iota(jnp.int32, (CH, CH), 0)
    lane = lax.broadcasted_iota(jnp.int32, (CH, CH), 1)
    identity = jnp.where(row == lane, 1.0, 0.0)
    groups = SLICES // LENGTH
    pairs = groups // 2
    middle = range(1, groups - 1)

    def residues(place):
        begins = [(group * LENGTH + place) * SLOT for group in range(groups)]
        return jnp.concatenate([packed_ref[begin : begin + SHARE, :] for begin in begins], axis=0)

    def mean(group, place):
        begin = (group * LENGTH + place) * SLOT + SHARE
        return packed_ref[begin : begin + 1, :]

    def scaled(errors, place):
        return [errors[group * SHARE : (group + 1) * SHARE] * mean(group, place) for group in range(groups)]

    def change(group):
        return changes[(group - 1) * CH : group * CH]

    def prepared(place, value):
        stack_parts(parts.at[place], value, slice(0, CH))
        return parts[place]

    split_at = groups * SHARE
    errors = residues(LENGTH - 1)
    starts = [identity * mean(group, LENGTH - 1) for group in middle]
    changes = exact_left(jnp.concatenate(starts, axis=0), center)
    for place in range(LENGTH - 2, -1, -1):
        rows = scaled(errors, place)
        for group in middle:
            rows.append((change(group) + identity) * mean(group, place))
        moved = exact_left(jnp.concatenate(rows, axis=0), center)
        errors = residues(place) + errors + moved[0:split_at]
        changes = changes + moved[split_at:]

    totals = [errors[group * SHARE : (group + 1) * SHARE] for group in range(groups)]
    maps = {group: prepared(group, change(group)) for group in middle}
    pair_totals, pair_maps = {}, {}
    for pair in range(1, pairs):
        low, high = 2 * pair, 2 * pair + 1
        pair_totals[pair] = totals[low] + totals[high] + times(totals[high], maps[low])
        if pair < pairs - 1:
            both = change(low) + change(high) + times(change(high), maps[low])
            pair_maps[pair] = prepared(groups - 1 + pair, both)
    carries = [None] * groups
    carry = jnp.zeros((SHARE, CH), jnp.float32)
    for pair in range(pairs - 1, -1, -1):
        low, high = 2 * pair, 2 * pair + 1
        carries[high] = carry
        carries[low] = totals[high] if pair == pairs - 1 else totals[high] + carry + times(carry, maps[high])
        if pair > 0:
            if pair < pairs - 1:
                carry = carry + times(carry, pair_maps[pair])
            carry = carry + pair_totals[pair]

    errors = jnp.concatenate(carries, axis=0)
    for place in range(LENGTH - 1, -1, -1):
        for group in range(groups):
            begin = (group * LENGTH + place) * SHARE
            upper_ref[begin : begin + SHARE, :] = errors[group * SHARE : (group + 1) * SHARE]
        if place > 0:
            moved = exact_left(jnp.concatenate(scaled(errors, place), axis=0), center)
            errors = residues(place) + errors + moved


def points_kernel(own_ref, residue_ref, error_ref, mean_ref, center_ref, points_ref, mark_ref):
    mark_ref[...] = mean_ref[...]
    error = error_ref[...]
    moved = moved_by(error, mean_ref[0:1, :], center_ref[...])
    points_ref[...] = own_ref[...] + (residue_ref[...] + error + moved)


def half_rows(turned_ref, half, lanes):
    begins = [pl.multiple_of(tap * CH + half * (CH // 2), CH // 2) for tap in range(9)]
    return jnp.concatenate([turned_ref[pl.ds(begin, CH // 2), lanes] for begin in begins], axis=0)


def second_kernel(
    step, core_ref, chosen_ref, error_ref, slope_ref, turned_ref, flipped_ref, sent_ref, grads_ref, buffer, total
):
    col = columns(PIECE)
    clear_edges(buffer)
    values = [chosen + error for chosen, error in zip(pieces(chosen_ref), pieces(error_ref))]
    for section in range(STEPS_DEV - 1, -1, -1):
        lows = lowered_grads(slope_ref, section, values)
        if section > 0:
            values = adjoint_step(buffer, flipped_ref, lows, values, step, col)
        for k, low in enumerate(lows):
            begin = section * PIX + k * PIECE
            grads_ref[begin : begin + PIECE, :] = low
        part = slice(section * PIX, (section + 1) * PIX)
        term = jnp.dot(
            half_rows(turned_ref, 1 - core_ref[0], part),
            jnp.concatenate(lows, axis=0),
            preferred_element_type=jnp.float32,
        )
        if section == STEPS_DEV - 1:
            total[...] = term
        elif section > 0:
            total[...] += term
        else:
            sent_ref[...] = step * (total[...] + term)


def kept_kernel(step, core_ref, turned_ref, grads_ref, kept_ref):
    rows = half_rows(turned_ref, core_ref[0], slice(0, STEPS_DEV * PIX))
    kept_ref[...] = step * jnp.dot(rows, grads_ref[...], preferred_element_type=jnp.float32)


def add_kernel(left_ref, right_ref, after_ref, out_ref):
    out_ref[...] = left_ref[...] + right_ref[...]


def sum_kernel(parts_ref, out_ref):
    total = parts_ref[0:PART, :]
    for part in range(1, parts_ref.shape[0] // PART):
        total = total + parts_ref[part * PART : (part + 1) * PART, :]
    for copy in range(out_ref.shape[0] // PART):
        out_ref[copy * PART : (copy + 1) * PART, :] = total


def place_kernel(other, core_ref, half_ref, *refs):
    out_ref, sems = refs[-2:]
    place = 1 - core_ref[0] if other else core_ref[0]
    copies = []
    for row in range(3):
        taps = slice(3 * row, 3 * row + 3)
        copies.append(pltpu.make_async_copy(half_ref.at[taps], out_ref.at[taps, place], sems.at[row]))
    for copy in copies:
        copy.start()
    for copy in copies:
        copy.wait()


def placed(other, core, half, so_far=()):
    anywhere = pl.BlockSpec(memory_space=pl.ANY)

    def kernel_of(*refs):
        place_kernel(other, *refs)

    return pl.pallas_call(
        kernel_of,
        out_shape=f32(9, 2, CH // 2, CH),
        in_specs=[pl.BlockSpec(memory_space=pltpu.SMEM), pl.BlockSpec(memory_space=pltpu.VMEM)]
        + [anywhere] * len(so_far),
        out_specs=anywhere,
        scratch_shapes=[pltpu.SemaphoreType.DMA((3,))],
        input_output_aliases={2: 0} if so_far else {},
        cost_estimate=pl.CostEstimate(flops=0, bytes_accessed=8 * HALF * CH, transcendentals=0),
        compiler_params=pltpu.CompilerParams(vmem_limit_bytes=LIMIT),
    )(core, half.reshape(9, CH // 2, CH), *so_far)


def ring_down(value, axis, count, distance):
    return lax.ppermute(value, axis, [((i + distance) % count, i) for i in range(count)])


def swapped(rows, axes, count):
    parts = rows.reshape(count, 1, rows.shape[0] // count * CH)
    return lax.all_to_all(parts, axes, 0, 0).reshape(rows.shape)


def local(checkpoints, conv_weight, conv_bias, point_guess, terminal):
    step = 2.0 / (STEPS_DEV * SLICES)
    own = point_guess.reshape(PIX, CH)
    terminal = terminal.reshape(PIX, CH)
    kernel = conv_weight.reshape(TAPS, CH)
    final = (lax.axis_index(("y", "z")) == SLICES - 1).astype(jnp.int32).reshape(1)
    core = lax.axis_index("core").astype(jnp.int32).reshape(1)
    upper = ring_down(own, ("y", "z"), SLICES, 1)

    def bound(function):
        def kernel_of(*refs):
            function(step, *refs)

        return kernel_of

    mark = call(first_kernel, f32(8, CH), 3.0, "ss")(core, final)
    slopes, turned, flipped, center, mean = call(
        bound(forward_kernel),
        [f32(STEPS_DEV, PIX, CH), bf16(TAPS, STEPS_DEV * PIX), bf16(WIDE, WIDE), bf16(2 * CH, CH), f32(8, CH)],
        1.5,
        "vvvv",
        [pltpu.VMEM((WIDE, WIDE), jnp.bfloat16), pltpu.VMEM((STEPS_DEV, PIX, WIDE), jnp.bfloat16)],
    )(mark, checkpoints.reshape(PIX, CH), kernel, conv_bias.reshape(1, CH))

    wide = pltpu.VMEM((PIX, WIDE), jnp.bfloat16)
    packed, residue, chosen = call(
        bound(relax_kernel),
        [f32(SLICES * SLOT, CH), f32(PIX, CH), f32(PIX, CH)],
        1.2,
        "svvvvvv",
        [wide],
    )(final, upper, terminal, own, slopes, flipped, mean)

    gathered = swapped(packed, ("y", "z"), SLICES)
    errors = call(
        scan_kernel, f32(PIX, CH), 2.5, scratch=[pltpu.VMEM((SLICES // LENGTH * 3 // 2, 3 * CH, CH), jnp.bfloat16)]
    )(gathered, center)
    upper_error = swapped(errors, ("y", "z"), SLICES)

    sent, grads = call(
        bound(second_kernel),
        [f32(HALF, CH), bf16(STEPS_DEV * PIX, CH)],
        1.1,
        "svvvvv",
        [wide, pltpu.VMEM((HALF, CH), jnp.float32)],
    )(core, chosen, upper_error, slopes, turned, flipped)

    received = lax.ppermute(sent, "core", [(0, 1), (1, 0)])
    kept = call(bound(kept_kernel), f32(HALF, CH), 0.4, "svv")(core, turned, grads)
    points, points_mark = call(points_kernel, [f32(PIX, CH), f32(8, CH)], 0.8)(own, residue, upper_error, mean, center)
    half = call(add_kernel, f32(HALF, CH), 0.1, "vva")(kept, received, points_mark)
    parts = swapped(half, ("y", "x"), PLANE)
    copies = call(sum_kernel, f32(SIZE_Z * PART, CH), 0.1)(parts)
    parts = swapped(copies, "z", SIZE_Z)
    copies = call(sum_kernel, f32(HALF, CH), 0.1)(parts)
    half = swapped(copies, ("y", "x"), PLANE)
    other = lax.ppermute(half, "core", [(0, 1), (1, 0)])
    grad_w = placed(True, core, other, [placed(False, core, half)])
    return points.reshape(1, 1, ROWS, COLS, CH), grad_w.reshape(3, 3, CH, CH)


def solution(mesh):
    fine = Mesh(mesh.devices.reshape(SIZE_Y, SIZE_Z, SIZE_X, 2), ("y", "z", "x", "core"))
    state = P(("y", "z"), ("x", "core"), None, None, None)
    return jax.shard_map(
        local,
        mesh=fine,
        in_specs=(state, P(), P(), state, P(("x", "core"), None, None, None)),
        out_specs=(state, P()),
        check_vma=False,
    )
```

```python
import jax
import jax.numpy as jnp
from jax import lax
from jax.experimental import pallas as pl
from jax.experimental.pallas import tpu as pltpu
from jax.sharding import Mesh, PartitionSpec as P

STEPS_DEV = 4
ROWS = 8
COLS = 32
CH = 128
PIX = ROWS * COLS
WIDE = 3 * CH
FIRST_PIECE = 64
SECOND_PIECE = 128
LENGTH = 4
TAPS = 9 * CH
SIZE_Y = 4
SIZE_Z = 8
SIZE_X = 4
PLANE = SIZE_X * SIZE_Y
PART = 36
HALF = PLANE * PART
SLICES = SIZE_Y * SIZE_Z
SHARE = PIX // SLICES
SLOT = SHARE + 1
LIMIT = 12 << 20


def call(kernel, outs, micros, specs=None, scratch=()):
    space = pl.BlockSpec(memory_space=pltpu.VMEM)
    places = {"s": pl.BlockSpec(memory_space=pltpu.SMEM), "v": space, "a": pl.BlockSpec(memory_space=pl.ANY)}

    def run(*operands):
        kinds = specs or "v" * len(operands)
        return pl.pallas_call(
            kernel,
            out_shape=outs,
            in_specs=[places[kind] for kind in kinds],
            out_specs=[space] * len(outs) if isinstance(outs, list) else space,
            scratch_shapes=scratch,
            cost_estimate=pl.CostEstimate(
                flops=int(micros * 1e9), bytes_accessed=int(micros * 3.6e6), transcendentals=0
            ),
            compiler_params=pltpu.CompilerParams(vmem_limit_bytes=LIMIT),
        )(*operands)

    return run


def f32(*shape):
    return jax.ShapeDtypeStruct(shape, jnp.float32)


def bf16(*shape):
    return jax.ShapeDtypeStruct(shape, jnp.bfloat16)


def columns(count):
    return lax.broadcasted_iota(jnp.int32, (count, CH), 0) % COLS


def clear_edges(buffer):
    zeros = jnp.zeros((COLS, CH), jnp.bfloat16)
    buffer[0:COLS, 0:CH] = zeros
    buffer[PIX - COLS : PIX, 2 * CH : WIDE] = zeros


def spread(buffer, low):
    buffer[COLS:PIX, 0:CH] = low[0 : PIX - COLS]
    buffer[:, CH : 2 * CH] = low
    buffer[0 : PIX - COLS, 2 * CH : WIDE] = low[COLS:PIX]


def from_left(value, col):
    return jnp.where(col > 0, pltpu.roll(value, 1, 0), 0.0)


def from_right(value, col):
    return jnp.where(col < COLS - 1, pltpu.roll(value, value.shape[0] - 1, 0), 0.0)


def convolve(buffer, kernel, col):
    taps = jnp.dot(buffer, kernel[...], preferred_element_type=jnp.float32)
    sides = from_left(taps[:, 0:CH], col) + from_right(taps[:, 2 * CH : WIDE], col)
    return taps[:, CH : 2 * CH] + sides


def spread_piece(buffer, low, begin):
    end = begin + low.shape[0]
    below, above = min(PIX, end + COLS), max(0, begin - COLS)
    buffer[begin + COLS : below, 0:CH] = low[0 : below - begin - COLS]
    buffer[begin:end, CH : 2 * CH] = low
    buffer[above : end - COLS, 2 * CH : WIDE] = low[above + COLS - begin : end - begin]


def pieces(ref, size, *lead):
    return [ref[(*lead, slice(begin, begin + size))] for begin in range(0, PIX, size)]


def split(value):
    high = value.astype(jnp.bfloat16)
    return high, (value - high.astype(jnp.float32)).astype(jnp.bfloat16)


def exact_left(value, weight_twice):
    return jnp.dot(
        jnp.concatenate(split(value), axis=1), weight_twice, preferred_element_type=jnp.float32
    )


def first_kernel(core_ref, final_ref, mark_ref):
    mark_ref[...] = jnp.zeros_like(mark_ref)


def forward_kernel(
    step, mark_ref, start_ref, kernel_ref, bias_ref, slope_ref, turned_ref, flipped_ref,
    center_ref, mean_ref, weights, lowered,
):
    col = columns(PIX)
    bias = bias_ref[...]
    for row in range(3):
        for tap in range(3):
            begin = (3 * row + tap) * CH
            weights[row * CH : (row + 1) * CH, tap * CH : (tap + 1) * CH] = kernel_ref[begin : begin + CH, :]
    current = start_ref[...].astype(jnp.float32)
    for section in range(STEPS_DEV):
        buffer = lowered.at[section]
        clear_edges(buffer)
        spread(buffer, current.astype(jnp.bfloat16))
        tanh_out = jnp.tanh(convolve(buffer[...], weights, col) + bias)
        slope = 1.0 - tanh_out * tanh_out
        slope_ref[section] = slope
        if section == 0:
            mean = jnp.sum(slope, axis=0, keepdims=True) * (STEPS_DEV * step / PIX)
            mean_ref[...] = jnp.broadcast_to(mean, (8, CH))
        current = current + step * tanh_out
    for section in range(STEPS_DEV):
        block = lowered[section].astype(jnp.float32)
        turned_ref[:, section * PIX : (section + 1) * PIX] = block.T.astype(jnp.bfloat16)
    for row in range(3):
        for tap in range(3):
            begin = (8 - 3 * row - tap) * CH
            turned = kernel_ref[begin : begin + CH, :].astype(jnp.float32).T.astype(jnp.bfloat16)
            flipped_ref[row * CH : (row + 1) * CH, tap * CH : (tap + 1) * CH] = turned
            if row == 1 and tap == 1:
                center_ref[0:CH, :] = turned
                center_ref[CH : 2 * CH, :] = turned


def adjoint_step(buffer, flipped, lows, values, step, col):
    size = PIX // len(lows)
    for k, low in enumerate(lows):
        spread_piece(buffer, low, k * size)
    return [
        value + step * convolve(buffer[k * size : (k + 1) * size, :], flipped, col)
        for k, value in enumerate(values)
    ]


def lowered_grads(slope_ref, section, values):
    return [(slope * value).astype(jnp.bfloat16) for slope, value in zip(pieces(slope_ref, PIX // len(values), section), values)]


def relax_kernel(
    step, final_ref, upper_ref, terminal_ref, own_ref, slope_ref, flipped_ref, mean_ref,
    packed_ref, residue_ref, chosen_ref, buffer,
):
    col = columns(FIRST_PIECE)
    clear_edges(buffer)
    final = final_ref[0] == 1
    values = [jnp.where(final, last, upper) for last, upper in zip(pieces(terminal_ref, FIRST_PIECE), pieces(upper_ref, FIRST_PIECE))]
    for k, value in enumerate(values):
        chosen_ref[k * FIRST_PIECE : (k + 1) * FIRST_PIECE, :] = value
    for section in range(STEPS_DEV - 1, -1, -1):
        lows = lowered_grads(slope_ref, section, values)
        values = adjoint_step(buffer, flipped_ref, lows, values, step, col)
    mean = mean_ref[0:1, :]
    for k, (value, own) in enumerate(zip(values, pieces(own_ref, FIRST_PIECE))):
        residue = value - own
        residue_ref[k * FIRST_PIECE : (k + 1) * FIRST_PIECE, :] = residue
        for share in range(FIRST_PIECE // SHARE):
            begin = (k * (FIRST_PIECE // SHARE) + share) * SLOT
            packed_ref[begin : begin + SHARE, :] = residue[share * SHARE : (share + 1) * SHARE]
            packed_ref[begin + SHARE : begin + SLOT, :] = mean


def moved_by(value, mean, center):
    return exact_left(value * mean, center)


def stack_parts(parts_ref, value, lanes):
    high, low = split(value)
    parts_ref[0:CH, lanes] = high
    parts_ref[CH : 2 * CH, lanes] = high
    parts_ref[2 * CH : 3 * CH, lanes] = low


def times(value, parts):
    high, low = split(value)
    return jnp.dot(jnp.concatenate([high, low, high], axis=1), parts, preferred_element_type=jnp.float32)


def scan_kernel(packed_ref, center_ref, upper_ref, parts):
    center = center_ref[...]
    row = lax.broadcasted_iota(jnp.int32, (CH, CH), 0)
    lane = lax.broadcasted_iota(jnp.int32, (CH, CH), 1)
    identity = jnp.where(row == lane, 1.0, 0.0)
    groups = SLICES // LENGTH
    pairs = groups // 2
    middle = range(1, groups - 1)

    def residues(place):
        begins = [(group * LENGTH + place) * SLOT for group in range(groups)]
        return jnp.concatenate([packed_ref[begin : begin + SHARE, :] for begin in begins], axis=0)

    def mean(group, place):
        begin = (group * LENGTH + place) * SLOT + SHARE
        return packed_ref[begin : begin + 1, :]

    def scaled(errors, place):
        return [errors[group * SHARE : (group + 1) * SHARE] * mean(group, place) for group in range(groups)]

    def change(group):
        return changes[(group - 1) * CH : group * CH]

    def prepared(place, value):
        stack_parts(parts.at[place], value, slice(0, CH))
        return parts[place]

    split_at = groups * SHARE
    errors = residues(LENGTH - 1)
    starts = [identity * mean(group, LENGTH - 1) for group in middle]
    changes = exact_left(jnp.concatenate(starts, axis=0), center)
    for place in range(LENGTH - 2, -1, -1):
        rows = scaled(errors, place)
        for group in middle:
            rows.append((change(group) + identity) * mean(group, place))
        moved = exact_left(jnp.concatenate(rows, axis=0), center)
        errors = residues(place) + errors + moved[0:split_at]
        changes = changes + moved[split_at:]

    totals = [errors[group * SHARE : (group + 1) * SHARE] for group in range(groups)]
    maps = {group: prepared(group, change(group)) for group in middle}
    pair_totals, pair_maps = {}, {}
    for pair in range(1, pairs):
        low, high = 2 * pair, 2 * pair + 1
        pair_totals[pair] = totals[low] + totals[high] + times(totals[high], maps[low])
        if pair < pairs - 1:
            both = change(low) + change(high) + times(change(high), maps[low])
            pair_maps[pair] = prepared(groups - 1 + pair, both)
    carries = [None] * groups
    carry = jnp.zeros((SHARE, CH), jnp.float32)
    for pair in range(pairs - 1, -1, -1):
        low, high = 2 * pair, 2 * pair + 1
        carries[high] = carry
        carries[low] = totals[high] if pair == pairs - 1 else totals[high] + carry + times(carry, maps[high])
        if pair > 0:
            if pair < pairs - 1:
                carry = carry + times(carry, pair_maps[pair])
            carry = carry + pair_totals[pair]

    errors = jnp.concatenate(carries, axis=0)
    for place in range(LENGTH - 1, -1, -1):
        for group in range(groups):
            begin = (group * LENGTH + place) * SHARE
            upper_ref[begin : begin + SHARE, :] = errors[group * SHARE : (group + 1) * SHARE]
        if place > 0:
            moved = exact_left(jnp.concatenate(scaled(errors, place), axis=0), center)
            errors = residues(place) + errors + moved


def points_kernel(own_ref, residue_ref, error_ref, mean_ref, center_ref, points_ref, mark_ref):
    mark_ref[...] = mean_ref[...]
    error = error_ref[...]
    moved = moved_by(error, mean_ref[0:1, :], center_ref[...])
    points_ref[...] = own_ref[...] + (residue_ref[...] + error + moved)


def half_rows(turned_ref, half, lanes):
    begins = [pl.multiple_of(row * CH + half * (CH // 2), CH // 2) for row in range(3)]
    return jnp.concatenate([turned_ref[pl.ds(begin, CH // 2), lanes] for begin in begins], axis=0)


def store_half(out_ref, taps):
    height = CH // 2
    for row in range(3):
        for tap in range(3):
            begin = (3 * row + tap) * height
            out_ref[begin : begin + height, :] = taps[row * height : (row + 1) * height, tap * CH : (tap + 1) * CH]


def second_kernel(
    step, core_ref, chosen_ref, error_ref, slope_ref, turned_ref, flipped_ref, sent_ref, grads_ref, buffer, total
):
    col = columns(SECOND_PIECE)
    clear_edges(buffer)
    values = [chosen + error for chosen, error in zip(pieces(chosen_ref, SECOND_PIECE), pieces(error_ref, SECOND_PIECE))]
    for section in range(STEPS_DEV - 1, -1, -1):
        lows = lowered_grads(slope_ref, section, values)
        if section > 0:
            values = adjoint_step(buffer, flipped_ref, lows, values, step, col)
        for k, low in enumerate(lows):
            begin = section * PIX + k * SECOND_PIECE
            grad, span = low.astype(jnp.float32), slice(begin, begin + SECOND_PIECE)
            grads_ref[span, 0:CH] = from_right(grad, col).astype(jnp.bfloat16)
            grads_ref[span, CH : 2 * CH] = low
            grads_ref[span, 2 * CH : WIDE] = from_left(grad, col).astype(jnp.bfloat16)
        part = slice(section * PIX, (section + 1) * PIX)
        term = jnp.dot(
            half_rows(turned_ref, 1 - core_ref[0], part), grads_ref[part, :], preferred_element_type=jnp.float32
        )
        if section == STEPS_DEV - 1:
            total[...] = term
        elif section > 0:
            total[...] += term
        else:
            store_half(sent_ref, step * (total[...] + term))


def kept_kernel(step, core_ref, turned_ref, grads_ref, kept_ref):
    rows = half_rows(turned_ref, core_ref[0], slice(0, STEPS_DEV * PIX))
    store_half(kept_ref, step * jnp.dot(rows, grads_ref[...], preferred_element_type=jnp.float32))


def add_kernel(left_ref, right_ref, after_ref, out_ref):
    out_ref[...] = left_ref[...] + right_ref[...]


def sum_kernel(parts_ref, out_ref):
    total = parts_ref[0:PART, :]
    for part in range(1, parts_ref.shape[0] // PART):
        total = total + parts_ref[part * PART : (part + 1) * PART, :]
    for copy in range(out_ref.shape[0] // PART):
        out_ref[copy * PART : (copy + 1) * PART, :] = total


def place_kernel(other, core_ref, half_ref, *refs):
    out_ref, sems = refs[-2:]
    place = 1 - core_ref[0] if other else core_ref[0]
    copies = []
    for row in range(3):
        taps = slice(3 * row, 3 * row + 3)
        copies.append(pltpu.make_async_copy(half_ref.at[taps], out_ref.at[taps, place], sems.at[row]))
    for copy in copies:
        copy.start()
    for copy in copies:
        copy.wait()


def placed(other, core, half, so_far=()):
    anywhere = pl.BlockSpec(memory_space=pl.ANY)

    def kernel_of(*refs):
        place_kernel(other, *refs)

    return pl.pallas_call(
        kernel_of,
        out_shape=f32(9, 2, CH // 2, CH),
        in_specs=[pl.BlockSpec(memory_space=pltpu.SMEM), pl.BlockSpec(memory_space=pltpu.VMEM)]
        + [anywhere] * len(so_far),
        out_specs=anywhere,
        scratch_shapes=[pltpu.SemaphoreType.DMA((3,))],
        input_output_aliases={2: 0} if so_far else {},
        cost_estimate=pl.CostEstimate(flops=0, bytes_accessed=8 * HALF * CH, transcendentals=0),
        compiler_params=pltpu.CompilerParams(vmem_limit_bytes=LIMIT),
    )(core, half.reshape(9, CH // 2, CH), *so_far)


def ring_down(value, axis, count, distance):
    return lax.ppermute(value, axis, [((i + distance) % count, i) for i in range(count)])


def swapped(rows, axes, count):
    parts = rows.reshape(count, 1, rows.shape[0] // count * CH)
    return lax.all_to_all(parts, axes, 0, 0).reshape(rows.shape)


def local(checkpoints, conv_weight, conv_bias, point_guess, terminal):
    step = 2.0 / (STEPS_DEV * SLICES)
    own = point_guess.reshape(PIX, CH)
    terminal = terminal.reshape(PIX, CH)
    kernel = conv_weight.reshape(TAPS, CH)
    final = (lax.axis_index(("y", "z")) == SLICES - 1).astype(jnp.int32).reshape(1)
    core = lax.axis_index("core").astype(jnp.int32).reshape(1)
    upper = ring_down(own, ("y", "z"), SLICES, 1)

    def bound(function):
        def kernel_of(*refs):
            function(step, *refs)

        return kernel_of

    mark = call(first_kernel, f32(8, CH), 3.0, "ss")(core, final)
    slopes, turned, flipped, center, mean = call(
        bound(forward_kernel),
        [f32(STEPS_DEV, PIX, CH), bf16(WIDE, STEPS_DEV * PIX), bf16(WIDE, WIDE), bf16(2 * CH, CH), f32(8, CH)],
        1.5,
        "vvvv",
        [pltpu.VMEM((WIDE, WIDE), jnp.bfloat16), pltpu.VMEM((STEPS_DEV, PIX, WIDE), jnp.bfloat16)],
    )(mark, checkpoints.reshape(PIX, CH), kernel, conv_bias.reshape(1, CH))

    wide = pltpu.VMEM((PIX, WIDE), jnp.bfloat16)
    packed, residue, chosen = call(
        bound(relax_kernel),
        [f32(SLICES * SLOT, CH), f32(PIX, CH), f32(PIX, CH)],
        1.2,
        "svvvvvv",
        [wide],
    )(final, upper, terminal, own, slopes, flipped, mean)

    gathered = swapped(packed, ("y", "z"), SLICES)
    errors = call(
        scan_kernel, f32(PIX, CH), 2.5, scratch=[pltpu.VMEM((SLICES // LENGTH * 3 // 2, 3 * CH, CH), jnp.bfloat16)]
    )(gathered, center)
    upper_error = swapped(errors, ("y", "z"), SLICES)

    sent, grads = call(
        bound(second_kernel),
        [f32(HALF, CH), bf16(STEPS_DEV * PIX, WIDE)],
        1.1,
        "svvvvv",
        [wide, pltpu.VMEM((WIDE // 2, WIDE), jnp.float32)],
    )(core, chosen, upper_error, slopes, turned, flipped)

    received = lax.ppermute(sent, "core", [(0, 1), (1, 0)])
    kept = call(bound(kept_kernel), f32(HALF, CH), 0.4, "svv")(core, turned, grads)
    points, points_mark = call(points_kernel, [f32(PIX, CH), f32(8, CH)], 0.8)(own, residue, upper_error, mean, center)
    half = call(add_kernel, f32(HALF, CH), 0.1, "vva")(kept, received, points_mark)
    parts = swapped(half, ("x", "y"), PLANE)
    copies = call(sum_kernel, f32(SIZE_Z * PART, CH), 0.1)(parts)
    parts = swapped(copies, "z", SIZE_Z)
    copies = call(sum_kernel, f32(HALF, CH), 0.1)(parts)
    half = swapped(copies, ("x", "y"), PLANE)
    other = lax.ppermute(half, "core", [(0, 1), (1, 0)])
    grad_w = placed(True, core, other, [placed(False, core, half)])
    return points.reshape(1, 1, ROWS, COLS, CH), grad_w.reshape(3, 3, CH, CH)


def solution(mesh):
    fine = Mesh(mesh.devices.reshape(SIZE_Y, SIZE_Z, SIZE_X, 2), ("y", "z", "x", "core"))
    state = P(("y", "z"), ("x", "core"), None, None, None)
    return jax.shard_map(
        local,
        mesh=fine,
        in_specs=(state, P(), P(), state, P(("x", "core"), None, None, None)),
        out_specs=(state, P()),
        check_vma=False,
    )
```

```python
import jax
import jax.numpy as jnp
from jax import lax
from jax.experimental import pallas as pl
from jax.experimental.pallas import tpu as pltpu
from jax.sharding import Mesh, PartitionSpec as P

STEPS_DEV = 4
ROWS = 8
COLS = 32
CH = 128
PIX = ROWS * COLS
WIDE = 3 * CH
FIRST_PIECE = 64
SECOND_PIECE = 128
LENGTH = 4
TAPS = 9 * CH
SIZE_Y = 4
SIZE_Z = 8
SIZE_X = 4
PLANE = SIZE_X * SIZE_Y
PART = 36
HALF = PLANE * PART
SLICES = SIZE_Y * SIZE_Z
SHARE = PIX // SLICES
SLOT = SHARE + 1
LIMIT = 12 << 20


def call(kernel, outs, micros, specs=None, scratch=()):
    space = pl.BlockSpec(memory_space=pltpu.VMEM)
    places = {"s": pl.BlockSpec(memory_space=pltpu.SMEM), "v": space, "a": pl.BlockSpec(memory_space=pl.ANY)}

    def run(*operands):
        kinds = specs or "v" * len(operands)
        return pl.pallas_call(
            kernel,
            out_shape=outs,
            in_specs=[places[kind] for kind in kinds],
            out_specs=[space] * len(outs) if isinstance(outs, list) else space,
            scratch_shapes=scratch,
            cost_estimate=pl.CostEstimate(
                flops=int(micros * 1e9), bytes_accessed=int(micros * 3.6e6), transcendentals=0
            ),
            compiler_params=pltpu.CompilerParams(vmem_limit_bytes=LIMIT),
        )(*operands)

    return run


def f32(*shape):
    return jax.ShapeDtypeStruct(shape, jnp.float32)


def bf16(*shape):
    return jax.ShapeDtypeStruct(shape, jnp.bfloat16)


def columns(count):
    return lax.broadcasted_iota(jnp.int32, (count, CH), 0) % COLS


def clear_edges(buffer):
    zeros = jnp.zeros((COLS, CH), jnp.bfloat16)
    buffer[0:COLS, 0:CH] = zeros
    buffer[PIX - COLS : PIX, 2 * CH : WIDE] = zeros


def spread(buffer, low):
    buffer[COLS:PIX, 0:CH] = low[0 : PIX - COLS]
    buffer[:, CH : 2 * CH] = low
    buffer[0 : PIX - COLS, 2 * CH : WIDE] = low[COLS:PIX]


def from_left(value, col):
    return jnp.where(col > 0, pltpu.roll(value, 1, 0), 0.0)


def from_right(value, col):
    return jnp.where(col < COLS - 1, pltpu.roll(value, value.shape[0] - 1, 0), 0.0)


def convolve(buffer, kernel, col):
    taps = jnp.dot(buffer, kernel[...], preferred_element_type=jnp.float32)
    sides = from_left(taps[:, 0:CH], col) + from_right(taps[:, 2 * CH : WIDE], col)
    return taps[:, CH : 2 * CH] + sides


def spread_piece(buffer, low, begin):
    end = begin + low.shape[0]
    below, above = min(PIX, end + COLS), max(0, begin - COLS)
    buffer[begin + COLS : below, 0:CH] = low[0 : below - begin - COLS]
    buffer[begin:end, CH : 2 * CH] = low
    buffer[above : end - COLS, 2 * CH : WIDE] = low[above + COLS - begin : end - begin]


def pieces(ref, size, *lead):
    return [ref[(*lead, slice(begin, begin + size))] for begin in range(0, PIX, size)]


def split(value):
    high = value.astype(jnp.bfloat16)
    return high, (value - high.astype(jnp.float32)).astype(jnp.bfloat16)


def exact_left(value, weight_twice):
    return jnp.dot(
        jnp.concatenate(split(value), axis=1), weight_twice, preferred_element_type=jnp.float32
    )


def first_kernel(mark_ref):
    mark_ref[...] = jnp.zeros_like(mark_ref)


def forward_kernel(
    step, mark_ref, start_ref, kernel_ref, bias_ref, slope_ref, turned_ref, flipped_ref,
    center_ref, mean_ref, weights, lowered,
):
    col = columns(PIX)
    bias = bias_ref[...]
    for row in range(3):
        for tap in range(3):
            begin = (3 * row + tap) * CH
            weights[row * CH : (row + 1) * CH, tap * CH : (tap + 1) * CH] = kernel_ref[begin : begin + CH, :]
    current = start_ref[...].astype(jnp.float32)
    for section in range(STEPS_DEV):
        buffer = lowered.at[section]
        clear_edges(buffer)
        spread(buffer, current.astype(jnp.bfloat16))
        tanh_out = jnp.tanh(convolve(buffer[...], weights, col) + bias)
        slope = 1.0 - tanh_out * tanh_out
        slope_ref[section] = slope
        if section == 0:
            mean = jnp.sum(slope, axis=0, keepdims=True) * (STEPS_DEV * step / PIX)
            mean_ref[...] = jnp.broadcast_to(mean, (8, CH))
        current = current + step * tanh_out
    for section in range(STEPS_DEV):
        block = lowered[section].astype(jnp.float32)
        turned_ref[:, section * PIX : (section + 1) * PIX] = block.T.astype(jnp.bfloat16)
    for row in range(3):
        for tap in range(3):
            begin = (8 - 3 * row - tap) * CH
            turned = kernel_ref[begin : begin + CH, :].astype(jnp.float32).T.astype(jnp.bfloat16)
            flipped_ref[row * CH : (row + 1) * CH, tap * CH : (tap + 1) * CH] = turned
            if row == 1 and tap == 1:
                center_ref[0:CH, :] = turned
                center_ref[CH : 2 * CH, :] = turned


def adjoint_step(buffer, flipped, lows, values, step, col):
    size = PIX // len(lows)
    for k, low in enumerate(lows):
        spread_piece(buffer, low, k * size)
    return [
        value + step * convolve(buffer[k * size : (k + 1) * size, :], flipped, col)
        for k, value in enumerate(values)
    ]


def lowered_grads(slope_ref, section, values):
    return [(slope * value).astype(jnp.bfloat16) for slope, value in zip(pieces(slope_ref, PIX // len(values), section), values)]


def relax_kernel(
    step, upper_ref, terminal_ref, own_ref, slope_ref, flipped_ref, mean_ref,
    packed_ref, residue_ref, chosen_ref, buffer,
):
    col = columns(FIRST_PIECE)
    clear_edges(buffer)
    final = lax.axis_index(("y", "z")) == SLICES - 1
    values = [jnp.where(final, last, upper) for last, upper in zip(pieces(terminal_ref, FIRST_PIECE), pieces(upper_ref, FIRST_PIECE))]
    for k, value in enumerate(values):
        chosen_ref[k * FIRST_PIECE : (k + 1) * FIRST_PIECE, :] = value
    for section in range(STEPS_DEV - 1, -1, -1):
        lows = lowered_grads(slope_ref, section, values)
        values = adjoint_step(buffer, flipped_ref, lows, values, step, col)
    mean = mean_ref[0:1, :]
    for k, (value, own) in enumerate(zip(values, pieces(own_ref, FIRST_PIECE))):
        residue = value - own
        residue_ref[k * FIRST_PIECE : (k + 1) * FIRST_PIECE, :] = residue
        for share in range(FIRST_PIECE // SHARE):
            begin = (k * (FIRST_PIECE // SHARE) + share) * SLOT
            packed_ref[begin : begin + SHARE, :] = residue[share * SHARE : (share + 1) * SHARE]
            packed_ref[begin + SHARE : begin + SLOT, :] = mean


def moved_by(value, mean, center):
    return exact_left(value * mean, center)


def stack_parts(parts_ref, value, lanes):
    high, low = split(value)
    parts_ref[0:CH, lanes] = high
    parts_ref[CH : 2 * CH, lanes] = high
    parts_ref[2 * CH : 3 * CH, lanes] = low


def times(value, parts):
    high, low = split(value)
    return jnp.dot(jnp.concatenate([high, low, high], axis=1), parts, preferred_element_type=jnp.float32)


def scan_kernel(packed_ref, center_ref, upper_ref, parts):
    center = center_ref[...]
    row = lax.broadcasted_iota(jnp.int32, (CH, CH), 0)
    lane = lax.broadcasted_iota(jnp.int32, (CH, CH), 1)
    identity = jnp.where(row == lane, 1.0, 0.0)
    groups = SLICES // LENGTH
    pairs = groups // 2
    middle = range(1, groups - 1)

    def residues(place):
        begins = [(group * LENGTH + place) * SLOT for group in range(groups)]
        return jnp.concatenate([packed_ref[begin : begin + SHARE, :] for begin in begins], axis=0)

    def mean(group, place):
        begin = (group * LENGTH + place) * SLOT + SHARE
        return packed_ref[begin : begin + 1, :]

    def scaled(errors, place):
        return [errors[group * SHARE : (group + 1) * SHARE] * mean(group, place) for group in range(groups)]

    def change(group):
        return changes[(group - 1) * CH : group * CH]

    def prepared(place, value):
        stack_parts(parts.at[place], value, slice(0, CH))
        return parts[place]

    split_at = groups * SHARE
    errors = residues(LENGTH - 1)
    starts = [identity * mean(group, LENGTH - 1) for group in middle]
    changes = exact_left(jnp.concatenate(starts, axis=0), center)
    for place in range(LENGTH - 2, -1, -1):
        rows = scaled(errors, place)
        for group in middle:
            rows.append((change(group) + identity) * mean(group, place))
        moved = exact_left(jnp.concatenate(rows, axis=0), center)
        errors = residues(place) + errors + moved[0:split_at]
        changes = changes + moved[split_at:]

    totals = [errors[group * SHARE : (group + 1) * SHARE] for group in range(groups)]
    maps = {group: prepared(group, change(group)) for group in middle}
    pair_totals, pair_maps = {}, {}
    for pair in range(1, pairs):
        low, high = 2 * pair, 2 * pair + 1
        pair_totals[pair] = totals[low] + totals[high] + times(totals[high], maps[low])
        if pair < pairs - 1:
            both = change(low) + change(high) + times(change(high), maps[low])
            pair_maps[pair] = prepared(groups - 1 + pair, both)
    carries = [None] * groups
    carry = jnp.zeros((SHARE, CH), jnp.float32)
    for pair in range(pairs - 1, -1, -1):
        low, high = 2 * pair, 2 * pair + 1
        carries[high] = carry
        carries[low] = totals[high] if pair == pairs - 1 else totals[high] + carry + times(carry, maps[high])
        if pair > 0:
            if pair < pairs - 1:
                carry = carry + times(carry, pair_maps[pair])
            carry = carry + pair_totals[pair]

    errors = jnp.concatenate(carries, axis=0)
    for place in range(LENGTH - 1, -1, -1):
        for group in range(groups):
            begin = (group * LENGTH + place) * SHARE
            upper_ref[begin : begin + SHARE, :] = errors[group * SHARE : (group + 1) * SHARE]
        if place > 0:
            moved = exact_left(jnp.concatenate(scaled(errors, place), axis=0), center)
            errors = residues(place) + errors + moved


def points_kernel(own_ref, residue_ref, error_ref, mean_ref, center_ref, points_ref, mark_ref):
    mark_ref[...] = mean_ref[...]
    error = error_ref[...]
    moved = moved_by(error, mean_ref[0:1, :], center_ref[...])
    points_ref[...] = own_ref[...] + (residue_ref[...] + error + moved)


def half_rows(turned_ref, half, lanes):
    begins = [pl.multiple_of(row * CH + half * (CH // 2), CH // 2) for row in range(3)]
    return jnp.concatenate([turned_ref[pl.ds(begin, CH // 2), lanes] for begin in begins], axis=0)


def store_half(out_ref, taps):
    height = CH // 2
    for row in range(3):
        for tap in range(3):
            begin = (3 * row + tap) * height
            out_ref[begin : begin + height, :] = taps[row * height : (row + 1) * height, tap * CH : (tap + 1) * CH]


def second_kernel(
    step, chosen_ref, error_ref, slope_ref, turned_ref, flipped_ref, sent_ref, grads_ref, buffer, total
):
    col = columns(SECOND_PIECE)
    clear_edges(buffer)
    values = [chosen + error for chosen, error in zip(pieces(chosen_ref, SECOND_PIECE), pieces(error_ref, SECOND_PIECE))]
    for section in range(STEPS_DEV - 1, -1, -1):
        lows = lowered_grads(slope_ref, section, values)
        if section > 0:
            values = adjoint_step(buffer, flipped_ref, lows, values, step, col)
        for k, low in enumerate(lows):
            begin = section * PIX + k * SECOND_PIECE
            grad, span = low.astype(jnp.float32), slice(begin, begin + SECOND_PIECE)
            grads_ref[span, 0:CH] = from_right(grad, col).astype(jnp.bfloat16)
            grads_ref[span, CH : 2 * CH] = low
            grads_ref[span, 2 * CH : WIDE] = from_left(grad, col).astype(jnp.bfloat16)
        part = slice(section * PIX, (section + 1) * PIX)
        term = jnp.dot(
            half_rows(turned_ref, 1 - lax.axis_index("core"), part), grads_ref[part, :], preferred_element_type=jnp.float32
        )
        if section == STEPS_DEV - 1:
            total[...] = term
        elif section > 0:
            total[...] += term
        else:
            store_half(sent_ref, step * (total[...] + term))


def kept_kernel(step, turned_ref, grads_ref, kept_ref):
    rows = half_rows(turned_ref, lax.axis_index("core"), slice(0, STEPS_DEV * PIX))
    store_half(kept_ref, step * jnp.dot(rows, grads_ref[...], preferred_element_type=jnp.float32))


def add_kernel(left_ref, right_ref, after_ref, out_ref):
    out_ref[...] = left_ref[...] + right_ref[...]


def sum_kernel(parts_ref, out_ref):
    total = parts_ref[0:PART, :]
    for part in range(1, parts_ref.shape[0] // PART):
        total = total + parts_ref[part * PART : (part + 1) * PART, :]
    for copy in range(out_ref.shape[0] // PART):
        out_ref[copy * PART : (copy + 1) * PART, :] = total


def place_kernel(other, half_ref, *refs):
    out_ref, sems = refs[-2:]
    core = lax.axis_index("core")
    place = 1 - core if other else core
    copies = []
    for row in range(3):
        taps = slice(3 * row, 3 * row + 3)
        copies.append(pltpu.make_async_copy(half_ref.at[taps], out_ref.at[taps, place], sems.at[row]))
    for copy in copies:
        copy.start()
    for copy in copies:
        copy.wait()


def placed(other, half, so_far=()):
    anywhere = pl.BlockSpec(memory_space=pl.ANY)

    def kernel_of(*refs):
        place_kernel(other, *refs)

    return pl.pallas_call(
        kernel_of,
        out_shape=f32(9, 2, CH // 2, CH),
        in_specs=[pl.BlockSpec(memory_space=pltpu.VMEM)] + [anywhere] * len(so_far),
        out_specs=anywhere,
        scratch_shapes=[pltpu.SemaphoreType.DMA((3,))],
        input_output_aliases={1: 0} if so_far else {},
        cost_estimate=pl.CostEstimate(flops=0, bytes_accessed=8 * HALF * CH, transcendentals=0),
        compiler_params=pltpu.CompilerParams(vmem_limit_bytes=LIMIT),
    )(half.reshape(9, CH // 2, CH), *so_far)


def ring_down(value, axis, count, distance):
    return lax.ppermute(value, axis, [((i + distance) % count, i) for i in range(count)])


def swapped(rows, axes, count):
    parts = rows.reshape(count, 1, rows.shape[0] // count * CH)
    return lax.all_to_all(parts, axes, 0, 0).reshape(rows.shape)


def local(checkpoints, conv_weight, conv_bias, point_guess, terminal):
    step = 2.0 / (STEPS_DEV * SLICES)
    own = point_guess.reshape(PIX, CH)
    terminal = terminal.reshape(PIX, CH)
    kernel = conv_weight.reshape(TAPS, CH)
    upper = ring_down(own, ("y", "z"), SLICES, 1)

    def bound(function):
        def kernel_of(*refs):
            function(step, *refs)

        return kernel_of

    mark = call(first_kernel, f32(8, CH), 3.0)()
    slopes, turned, flipped, center, mean = call(
        bound(forward_kernel),
        [f32(STEPS_DEV, PIX, CH), bf16(WIDE, STEPS_DEV * PIX), bf16(WIDE, WIDE), bf16(2 * CH, CH), f32(8, CH)],
        1.5,
        "vvvv",
        [pltpu.VMEM((WIDE, WIDE), jnp.bfloat16), pltpu.VMEM((STEPS_DEV, PIX, WIDE), jnp.bfloat16)],
    )(mark, checkpoints.reshape(PIX, CH), kernel, conv_bias.reshape(1, CH))

    wide = pltpu.VMEM((PIX, WIDE), jnp.bfloat16)
    packed, residue, chosen = call(
        bound(relax_kernel),
        [f32(SLICES * SLOT, CH), f32(PIX, CH), f32(PIX, CH)],
        1.2,
        scratch=[wide],
    )(upper, terminal, own, slopes, flipped, mean)

    gathered = swapped(packed, ("y", "z"), SLICES)
    errors = call(
        scan_kernel, f32(PIX, CH), 2.5, scratch=[pltpu.VMEM((SLICES // LENGTH * 3 // 2, 3 * CH, CH), jnp.bfloat16)]
    )(gathered, center)
    upper_error = swapped(errors, ("y", "z"), SLICES)

    sent, grads = call(
        bound(second_kernel),
        [f32(HALF, CH), bf16(STEPS_DEV * PIX, WIDE)],
        1.1,
        scratch=[wide, pltpu.VMEM((WIDE // 2, WIDE), jnp.float32)],
    )(chosen, upper_error, slopes, turned, flipped)

    received = lax.ppermute(sent, "core", [(0, 1), (1, 0)])
    kept = call(bound(kept_kernel), f32(HALF, CH), 0.4)(turned, grads)
    points, points_mark = call(points_kernel, [f32(PIX, CH), f32(8, CH)], 0.8)(own, residue, upper_error, mean, center)
    half = call(add_kernel, f32(HALF, CH), 0.1, "vva")(kept, received, points_mark)
    parts = swapped(half, ("x", "y"), PLANE)
    copies = call(sum_kernel, f32(SIZE_Z * PART, CH), 0.1)(parts)
    parts = swapped(copies, "z", SIZE_Z)
    copies = call(sum_kernel, f32(HALF, CH), 0.1)(parts)
    half = swapped(copies, ("x", "y"), PLANE)
    other = lax.ppermute(half, "core", [(0, 1), (1, 0)])
    grad_w = placed(True, other, [placed(False, half)])
    return points.reshape(1, 1, ROWS, COLS, CH), grad_w.reshape(3, 3, CH, CH)


def solution(mesh):
    fine = Mesh(mesh.devices.reshape(SIZE_Y, SIZE_Z, SIZE_X, 2), ("y", "z", "x", "core"))
    state = P(("y", "z"), ("x", "core"), None, None, None)
    return jax.shard_map(
        local,
        mesh=fine,
        in_specs=(state, P(), P(), state, P(("x", "core"), None, None, None)),
        out_specs=(state, P()),
        check_vma=False,
    )
```
